256 devices in a mesh: rows: 8 (over z_hi, core), cols: 16 (over x, y), batch: 2 (over z_lo).
Axes of the slice: x: 4, y: 4, z: 8 (z_hi: 4, z_lo: 2; z = z_hi * 2 + z_lo), core: 2. Of those that a mesh axis runs over, the one named last changes fastest.
Arguments:
- fine_input: bfloat16 [2, 256, 2048, 128], P('batch', 'rows', 'cols'), may hold values from -60 to 60
- coarse: bfloat16 [2, 64, 512, 512], P('batch', 'rows', 'cols'), may hold values from -6 to 6
- rain_bins: int32 [2, 256, 2048], P('batch', 'rows', 'cols'), may hold values from 0 to 63
- w_qkv: bfloat16 [512, 1536], replicated, may hold values from -0.25 to 0.25
- w_out: bfloat16 [512, 512], replicated, may hold values from -0.25 to 0.25
- w_up: bfloat16 [512, 128], replicated, may hold values from -0.25 to 0.25
- w_conv: bfloat16 [3, 3, 128, 128], replicated, may hold values from -0.4375 to 0.4375
- w_head: bfloat16 [128, 9], replicated, may hold values from -0.5 to 0.5
Outputs:
- quantiles: float32 [2, 9, 256, 2048], P('batch', None, 'rows', 'cols')
- loss_value: float32 [], replicated
- grad_qkv: float32 [512, 1536], replicated
- grad_out: float32 [512, 512], replicated
- grad_up: float32 [512, 128], replicated
- grad_conv: float32 [3, 3, 128, 128], replicated
- grad_head: float32 [128, 9], replicated
- grad_fine: float32 [2, 256, 2048, 128], P('batch', 'rows', 'cols')
The draws below stay inside these ranges and needn't reach their ends.
All inputs are finite; a program needn't handle non-finite values.
Results may differ from the reference program's by a relative error of at most 0.015.
Values may be sent and summed in bfloat16 or wider, within the bound.
A program may use at most 64 MiB of HBM per device.

```python
import jax
import jax.numpy as jnp
from jax import lax

W = 512
C = 128
HEAD_DIM = 32
QUANT = 9
CR = 8
CC = 32
B = 2
HC = 64
WC = 512
HF = 256
WF = 2048
N_ROWS = 8
N_COLS = 16


def draw_fine_input(key, part):
    key = jax.random.fold_in(key, 11)
    shape = (B, HF, WF, C)
    row_place = jnp.arange(HF, dtype=jnp.float32)[:, None] / (HF - 1.0)
    col_place = jnp.arange(WF, dtype=jnp.float32)[None, :] / (WF - 1.0)
    noise = jnp.clip(jax.random.normal(key, shape, jnp.float32), -6.0, 6.0)
    ratio = 10.0
    scale = jnp.exp(jnp.log(ratio) * (0.5 * row_place + 0.5 * col_place))
    return (noise * scale[None, :, :, None]).astype(jnp.bfloat16)


def set_ends(array, stream_key, least, largest):
    place = [jax.random.randint(jax.random.fold_in(stream_key, axis), (), 0, length) for axis, length in enumerate(array.shape)]
    widest = array.shape.index(max(array.shape))
    next_to = place[:widest] + [(place[widest] + 1) % array.shape[widest]] + place[widest + 1:]
    return array.at[tuple(place)].set(least).at[tuple(next_to)].set(largest)


def shard_levels(rng, shape, cuts, low, high):
    loudness, own = 1.0, jax.random.fold_in(rng, 6)
    for position, parts in cuts:
        steps = jnp.exp(jax.random.uniform(jax.random.fold_in(own, position), (parts,), jnp.float32, low / len(cuts), high / len(cuts)))
        loudness = loudness * jnp.repeat(steps, shape[position] // parts).reshape([-1 if axis == position else 1 for axis in range(len(shape))])
    return loudness


def gaussian(key, dims, deviation, most, shards=(), kind=jnp.bfloat16):
    level = shard_levels(key, dims, shards, -0.22, 0.18) if shards else 1.0
    values = jax.random.normal(key, dims, jnp.float32) * deviation * level
    return jnp.minimum(jnp.maximum(values, -most), most).astype(kind)


def setup_inputs(seed: int = 0) -> dict:
    splits = jax.random.split(jax.random.key(seed), 9)
    fine_input = draw_fine_input(jax.random.fold_in(splits[8], 71), 0)
    coarse = gaussian(splits[1], (B, HC, WC, W), 1.0, 6.0, ((0, 2), (1, 8), (2, 16)))
    rain_bins = set_ends(jax.random.randint(splits[2], (B, HF, WF), 0, 64), jax.random.fold_in(splits[2], 1), 0, 63).astype(jnp.int32)
    w_qkv = gaussian(splits[3], (W, 3 * W), W ** -0.5, 0.25)
    w_out = gaussian(splits[4], (W, W), W ** -0.5, 0.25)
    w_up = gaussian(splits[5], (W, C), W ** -0.5, 0.25)
    w_conv = gaussian(splits[6], (3, 3, C, C), (3 * C // 2) ** -0.5, 0.4375)
    w_head = gaussian(splits[7], (C, QUANT), C ** -0.5, 0.5)
    return {"fine_input": fine_input, "coarse": coarse, "rain_bins": rain_bins, "w_qkv": w_qkv, "w_out": w_out, "w_up": w_up, "w_conv": w_conv, "w_head": w_head}


def attend(tokens, w_qkv, w_out):
    members, groups, width = tokens.shape
    heads = width // HEAD_DIM
    projected = jnp.einsum('sgw,wk->sgk', tokens.astype(jnp.float32), w_qkv.astype(jnp.float32)).astype(jnp.bfloat16)
    query = projected[:, :, :width].reshape(members, groups, heads, HEAD_DIM)
    keyed = projected[:, :, width:2 * width].reshape(members, groups, heads, HEAD_DIM)
    valued = projected[:, :, 2 * width:].reshape(members, groups, heads, HEAD_DIM)
    scores = jnp.einsum('sghd,tghd->ghst', query.astype(jnp.float32), keyed.astype(jnp.float32)) * HEAD_DIM ** (-0.5)
    peak = lax.optimization_barrier(jnp.max(scores, axis=-1, keepdims=True))
    powers = jnp.exp(scores - peak)
    probability = powers / lax.optimization_barrier(jnp.sum(powers, axis=-1, keepdims=True))
    prob_b = probability.astype(jnp.bfloat16)
    mixed = jnp.einsum('ghst,tghd->sghd', prob_b.astype(jnp.float32), valued.astype(jnp.float32)).astype(jnp.bfloat16)
    mixed = mixed.reshape(members, groups, width)
    result = jnp.einsum('sgw,wk->sgk', mixed.astype(jnp.float32), w_out.astype(jnp.float32))
    return (result, (query, keyed, valued, probability, prob_b, mixed))

def attend_back(tokens, w_out, saved, cotangent):
    query, keyed, valued, probability, prob_b, mixed = saved
    members, groups, heads, _ = query.shape
    width = heads * HEAD_DIM
    grad_out = jnp.einsum('sgw,sgk->wk', mixed.astype(jnp.float32), cotangent.astype(jnp.float32))
    mix_grad = jnp.einsum('sgk,wk->sgw', cotangent.astype(jnp.float32), w_out.astype(jnp.float32)).astype(jnp.bfloat16)
    mix_grad = mix_grad.reshape(members, groups, heads, HEAD_DIM)
    dprob = jnp.einsum('sghd,tghd->ghst', mix_grad.astype(jnp.float32), valued.astype(jnp.float32))
    dvalue = jnp.einsum('ghst,sghd->tghd', prob_b.astype(jnp.float32), mix_grad.astype(jnp.float32))
    inner = lax.optimization_barrier(jnp.sum(probability * dprob, axis=-1, keepdims=True))
    dscore = (probability * (dprob - inner) * HEAD_DIM ** (-0.5)).astype(jnp.bfloat16)
    dquery = jnp.einsum('ghst,tghd->sghd', dscore.astype(jnp.float32), keyed.astype(jnp.float32))
    dkey = jnp.einsum('ghst,sghd->tghd', dscore.astype(jnp.float32), query.astype(jnp.float32))
    dproj = jnp.concatenate([dquery.reshape(members, groups, width), dkey.reshape(members, groups, width), dvalue.reshape(members, groups, width)], axis=-1).astype(jnp.bfloat16)
    grad_qkv = jnp.einsum('sgw,sgk->wk', tokens.astype(jnp.float32), dproj.astype(jnp.float32))
    return (grad_qkv, grad_out)

def to_groups(image, samples, width):
    shaped = image.reshape(samples, N_ROWS, CR, N_COLS, CC, width).transpose(0, 1, 3, 2, 4, 5)
    return shaped.reshape(samples, N_ROWS * N_COLS, CR * CC, width)

def from_groups(grouped, samples, width):
    shaped = grouped.reshape(samples, N_ROWS, N_COLS, CR, CC, width).transpose(0, 1, 3, 2, 4, 5)
    return shaped.reshape(samples, N_ROWS * CR, N_COLS * CC, width)

def reference(fine_input, coarse, rain_bins, w_qkv, w_out, w_up, w_conv, w_head):
    samples, coarse_rows, coarse_cols, width = coarse.shape
    fine_rows, fine_cols, channels = fine_input.shape[1:]
    grid_tokens = to_groups(coarse, samples, width)

    def forward_sample(sample):
        return attend(sample, w_qkv, w_out)[0].astype(jnp.bfloat16)
    attended = from_groups(lax.map(forward_sample, grid_tokens), samples, width)
    context = (coarse.astype(jnp.float32) + attended.astype(jnp.float32)).astype(jnp.bfloat16)
    lifted = jnp.einsum('bijw,wc->bijc', context.astype(jnp.float32), w_up.astype(jnp.float32))
    spread = jnp.repeat(jnp.repeat(lifted, 4, axis=1), 4, axis=2)
    hidden = fine_input.astype(jnp.float32) + spread
    active = jax.nn.gelu(hidden).astype(jnp.bfloat16)
    padded = jnp.pad(active, ((0, 0), (1, 1), (1, 1), (0, 0)))
    conv_out = jnp.zeros(hidden.shape, jnp.float32)
    for row_tap in range(3):
        for col_tap in range(3):
            window = padded[:, row_tap:row_tap + fine_rows, col_tap:col_tap + fine_cols]
            conv_out = conv_out + jnp.einsum('bhwc,ck->bhwk', window.astype(jnp.float32), w_conv[row_tap, col_tap].astype(jnp.float32))
    outer = (hidden + conv_out).astype(jnp.bfloat16)
    quantiles = jnp.einsum('bhwc,cq->bqhw', outer.astype(jnp.float32), w_head.astype(jnp.float32))
    target = rain_bins.astype(jnp.float32)[:, None] / 16.0 - 1.0
    levels = ((jnp.arange(QUANT) + 1).astype(jnp.float32) / (QUANT + 1.0))[None, :, None, None]
    error_term = target - quantiles
    weight_term = jnp.where(error_term < 0.0, 1.0 - levels, levels)
    magnitude = jnp.abs(error_term)
    huber_term = jnp.where(magnitude <= 1.0, 0.5 * error_term * error_term, magnitude - 0.5)
    loss_value = jnp.mean(weight_term * huber_term)
    pixel_count = samples * fine_rows * fine_cols
    root_count = jnp.sqrt(jnp.asarray(pixel_count, jnp.float32))
    dpred = (-weight_term * jnp.clip(error_term, -1.0, 1.0) / root_count).astype(jnp.bfloat16)
    grad_head = jnp.einsum('bhwc,bqhw->cq', outer.astype(jnp.float32), dpred.astype(jnp.float32))
    douter = jnp.einsum('bqhw,cq->bhwc', dpred.astype(jnp.float32), w_head.astype(jnp.float32))
    douter_b = douter.astype(jnp.bfloat16)
    grad_pad = jnp.pad(douter_b, ((0, 0), (1, 1), (1, 1), (0, 0)))
    dactive = jnp.zeros(hidden.shape, jnp.float32)
    kernel_rows = []
    for row_tap in range(3):
        kernel_row = []
        for col_tap in range(3):
            window = padded[:, row_tap:row_tap + fine_rows, col_tap:col_tap + fine_cols]
            kernel_row.append(jnp.einsum('bhwc,bhwk->ck', window.astype(jnp.float32), douter_b.astype(jnp.float32)))
            back_window = grad_pad[:, 2 - row_tap:2 - row_tap + fine_rows, 2 - col_tap:2 - col_tap + fine_cols]
            dactive = dactive + jnp.einsum('bhwk,ck->bhwc', back_window.astype(jnp.float32), w_conv[row_tap, col_tap].astype(jnp.float32))
        kernel_rows.append(jnp.stack(kernel_row))
    grad_conv = jnp.stack(kernel_rows)
    slope = jax.vjp(jax.nn.gelu, hidden)[1](dactive)[0]
    dhidden = douter + slope
    grad_fine = dhidden * root_count
    dlift = dhidden.reshape(samples, coarse_rows, 4, coarse_cols, 4, channels).sum(axis=(2, 4)).astype(jnp.bfloat16)
    grad_up = jnp.einsum('bijw,bijc->wc', context.astype(jnp.float32), dlift.astype(jnp.float32))
    dcontext = jnp.einsum('bijc,wc->bijw', dlift.astype(jnp.float32), w_up.astype(jnp.float32)).astype(jnp.bfloat16)
    grid_grads = to_groups(dcontext, samples, width)

    def backward_sample(pair):
        sample, cotangent = pair
        saved = attend(sample, w_qkv, w_out)[1]
        return attend_back(sample, w_out, saved, cotangent)
    qkv_terms, out_terms = lax.map(backward_sample, (grid_tokens, grid_grads))
    grad_qkv = lax.optimization_barrier(jnp.sum(qkv_terms, axis=0))
    grad_out = lax.optimization_barrier(jnp.sum(out_terms, axis=0))
    return (quantiles, loss_value, grad_qkv, grad_out, grad_up, grad_conv, grad_head, grad_fine)
```

```python
import jax
import jax.numpy as jnp
from jax import lax
from jax.experimental import pallas as pl
from jax.experimental.pallas import tpu as pltpu
from jax.sharding import PartitionSpec as P

HEAD_DIM = 32
QUANT = 9
UNITS = 1280
MESH = pl.DeviceIdType.MESH


def meet(targets):
    barrier = pltpu.get_barrier_semaphore()
    for target in targets:
        pl.semaphore_signal(barrier, inc=1, device_id=target, device_id_type=MESH)
    pl.semaphore_wait(barrier, len(targets))


def add_blocks(dst, dst_at, terms, count, step):
    def one(i, carry):
        at = i * step
        total = None
        for ref, start in terms:
            value = ref[pl.ds(start + at, step)].astype(jnp.float32)
            total = value if total is None else total + value
        dst[pl.ds(dst_at + at, step)] = total.astype(dst.dtype)
        return carry

    lax.fori_loop(0, count // step, one, 0)


def reduce_kernel(g, out, got0, sum0, got1, sum1, got2, sum2, got3, ss0, rs0, ss1, rs1, ss2, rs2, ss3, rs3,
                  sa3, ra3, sa2, ra2, sa1, ra1, sa0, ra0):
    row, col, batch = lax.axis_index("rows"), lax.axis_index("cols"), lax.axis_index("batch")
    core, deep = row % 2, (row // 2) * 2 + batch
    x, y = col // 4, col % 4
    first = x * (1 - core) + y * core
    second = y * (1 - core) + x * core
    other = {"rows": row + 1 - 2 * core}
    u0, u1, u2, u3 = UNITS // 2, UNITS // 8, UNITS // 32, UNITS // 256

    def in_first(k):
        p = (first + k) % 4
        return p, {"cols": (p * 4 + y) * (1 - core) + (x * 4 + p) * core}

    def in_second(k):
        p = (second + k) % 4
        return p, {"cols": (x * 4 + p) * (1 - core) + (p * 4 + y) * core}

    def in_deep(k):
        p = (deep + k) % 8
        return p, {"rows": (p // 2) * 2 + core, "batch": p % 2}

    def copy(src, dst, send, recv, to):
        return pltpu.make_async_remote_copy(src_ref=src, dst_ref=dst, send_sem=send, recv_sem=recv,
                                            device_id=to, device_id_type=MESH)

    meet([other] + [in_first(k)[1] for k in (1, 2, 3)] + [in_second(k)[1] for k in (1, 2, 3)]
         + [in_deep(k)[1] for k in range(1, 8)])

    near = []
    for q in range(4):
        c = copy(g.at[pl.ds((1 - core) * u0 + q * u1, u1)], got0.at[pl.ds(q * u1, u1)], ss0.at[q], rs0.at[q], other)
        c.start()
        near.append(c)
    for c in near:
        c.wait()
    add_blocks(sum0, 0, [(g, core * u0), (got0, 0)], u0, 8)

    def scatter(src, size, got, total, send, recv, where, mine, n, step):
        copies = []
        for k in range(1, n):
            p, to = where(k)
            c = copy(src.at[pl.ds(p * size, size)], got.at[k - 1], send.at[k - 1], recv.at[k - 1], to)
            c.start()
            copies.append(c)
        for c in copies:
            c.wait()
        def one(i, carry):
            at = i * step
            value = src[pl.ds(mine * size + at, step)].astype(jnp.float32)
            for k in range(n - 1):
                value = value + got[k, pl.ds(at, step)].astype(jnp.float32)
            total(at, step, value)
            return carry
        lax.fori_loop(0, size // step, one, 0)

    def keep(ref, base):
        def store(at, step, value):
            ref[pl.ds(base + at, step)] = value.astype(ref.dtype)
        return store

    scatter(sum0, u1, got1, keep(sum1, 0), ss1, rs1, in_first, first, 4, 8)
    scatter(sum1, u2, got2, keep(sum2, 0), ss2, rs2, in_second, second, 4, 8)
    place = core * u0 + first * u1 + second * u2
    scatter(sum2, u3, got3, keep(out, place + deep * u3), ss3, rs3, in_deep, deep, 8, 5)

    def gather(start, size, send, recv, where, n):
        copies = []
        block = out.at[pl.ds(start, size)]
        for k in range(1, n):
            c = copy(block, block, send.at[k - 1], recv.at[k - 1], where(k)[1])
            c.start()
            copies.append(c)
        for c in copies:
            c.wait()

    gather(place + deep * u3, u3, sa3, ra3, in_deep, 8)
    gather(place, u2, sa2, ra2, in_second, 4)
    gather(core * u0 + first * u1, u1, sa1, ra1, in_first, 4)
    gather(core * u0, u0, sa0, ra0, lambda k: (0, other), 2)


def reduce_units(g):
    unit = (8, 128)
    b16 = jnp.bfloat16
    dma = pltpu.SemaphoreType.DMA
    return pl.pallas_call(
        reduce_kernel,
        out_shape=jax.ShapeDtypeStruct((UNITS,) + unit, b16),
        in_specs=[pl.BlockSpec(memory_space=pltpu.VMEM)],
        out_specs=pl.BlockSpec(memory_space=pltpu.VMEM),
        scratch_shapes=[
            pltpu.VMEM((UNITS // 2,) + unit, b16),
            pltpu.VMEM((UNITS // 2,) + unit, b16),
            pltpu.VMEM((3, UNITS // 8) + unit, b16),
            pltpu.VMEM((UNITS // 8,) + unit, b16),
            pltpu.VMEM((3, UNITS // 32) + unit, b16),
            pltpu.VMEM((UNITS // 32,) + unit, b16),
            pltpu.VMEM((7, UNITS // 256) + unit, b16),
            dma((4,)), dma((4,)), dma((3,)), dma((3,)), dma((3,)), dma((3,)), dma((7,)), dma((7,)),
            dma((7,)), dma((7,)), dma((3,)), dma((3,)), dma((3,)), dma((3,)), dma((1,)), dma((1,)),
        ],
        compiler_params=pltpu.CompilerParams(collective_id=7, has_side_effects=True,
                                             vmem_limit_bytes=40 * 1024 * 1024),
    )(g)


def tiles(array):
    rows, columns = array.shape
    return array.reshape(rows // 8, 8, columns // 128, 128).transpose(0, 2, 1, 3).reshape(-1, 8, 128)


def untile(units, rows, columns):
    return units.reshape(rows // 8, columns // 128, 8, 128).transpose(0, 2, 1, 3).reshape(rows, columns)


def reduce_all(grad_qkv, grad_out, grad_up, grad_conv, grad_head, loss_row):
    tail = jnp.concatenate([grad_head.T, loss_row, jnp.zeros((6, 128), jnp.float32)], axis=0)
    parts = [tiles(grad_qkv), tiles(grad_out), tiles(grad_up), tiles(grad_conv.reshape(1152, 128)), tail.reshape(2, 8, 128)]
    used = sum(part.shape[0] for part in parts)
    parts.append(jnp.zeros((UNITS - used, 8, 128), jnp.float32))
    g = jnp.concatenate([part.astype(jnp.bfloat16) for part in parts], axis=0)
    total = reduce_units(g).astype(jnp.float32)
    tail = total[1232:1234].reshape(16, 128)
    return (
        untile(total[:768], 512, 1536),
        untile(total[768:1024], 512, 512),
        untile(total[1024:1088], 512, 128),
        total[1088:1232].reshape(3, 3, 128, 128),
        tail[:9].T,
        jnp.sum(tail[9]),
    )


def with_halo(block, sides, width):
    for axis, dim in sides:
        count = lax.axis_size(axis)
        forward = [(i, i + 1) for i in range(count - 1)]
        backward = [(target, source) for source, target in forward]
        low = lax.ppermute(
            lax.slice_in_dim(block, block.shape[dim] - width, None, axis=dim), axis, forward
        )
        high = lax.ppermute(lax.slice_in_dim(block, 0, width, axis=dim), axis, backward)
        block = jnp.concatenate([low, block, high], axis=dim)
    return block


def regroup(block):
    return lax.all_to_all(block, ("rows", "cols"), split_axis=0, concat_axis=0, tiled=True)


def attend(tokens, w_qkv, w_out):
    members, groups, width = tokens.shape
    heads = width // HEAD_DIM
    projected = jnp.einsum("sgw,wk->sgk", tokens, w_qkv, preferred_element_type=jnp.float32).astype(
        jnp.bfloat16
    )
    query = projected[:, :, :width].reshape(members, groups, heads, HEAD_DIM)
    keyed = projected[:, :, width : 2 * width].reshape(members, groups, heads, HEAD_DIM)
    valued = projected[:, :, 2 * width :].reshape(members, groups, heads, HEAD_DIM)
    scores = jnp.einsum(
        "sghd,tghd->ghst", query, keyed, preferred_element_type=jnp.float32
    ) * HEAD_DIM ** (-0.5)
    peak = jnp.max(scores, axis=-1, keepdims=True)
    powers = jnp.exp(scores - peak)
    probability = powers / jnp.sum(powers, axis=-1, keepdims=True)
    prob_b = probability.astype(jnp.bfloat16)
    mixed = jnp.einsum(
        "ghst,tghd->sghd", prob_b, valued, preferred_element_type=jnp.float32
    ).astype(jnp.bfloat16)
    mixed = mixed.reshape(members, groups, width)
    result = jnp.einsum("sgw,wk->sgk", mixed, w_out, preferred_element_type=jnp.float32)
    return (result, (query, keyed, valued, probability, prob_b, mixed))


def attend_back(tokens, w_out, saved, cotangent):
    query, keyed, valued, probability, prob_b, mixed = saved
    members, groups, heads, _ = query.shape
    width = heads * HEAD_DIM
    grad_out = jnp.einsum("sgw,sgk->wk", mixed, cotangent, preferred_element_type=jnp.float32)
    mix_grad = jnp.einsum(
        "sgk,wk->sgw", cotangent, w_out, preferred_element_type=jnp.float32
    ).astype(jnp.bfloat16)
    mix_grad = mix_grad.reshape(members, groups, heads, HEAD_DIM)
    dprob = jnp.einsum("sghd,tghd->ghst", mix_grad, valued, preferred_element_type=jnp.float32)
    dvalue = jnp.einsum("ghst,sghd->tghd", prob_b, mix_grad, preferred_element_type=jnp.float32)
    inner = jnp.sum(probability * dprob, axis=-1, keepdims=True)
    dscore = (probability * (dprob - inner) * HEAD_DIM ** (-0.5)).astype(jnp.bfloat16)
    dquery = jnp.einsum("ghst,tghd->sghd", dscore, keyed, preferred_element_type=jnp.float32)
    dkey = jnp.einsum("ghst,sghd->tghd", dscore, query, preferred_element_type=jnp.float32)
    dproj = jnp.concatenate(
        [
            dquery.reshape(members, groups, width),
            dkey.reshape(members, groups, width),
            dvalue.reshape(members, groups, width),
        ],
        axis=-1,
    ).astype(jnp.bfloat16)
    grad_qkv = jnp.einsum("sgw,sgk->wk", tokens, dproj, preferred_element_type=jnp.float32)
    return (grad_qkv, grad_out)


def body(fine_input, coarse, rain_bins, w_qkv, w_out, w_up, w_conv, w_head):
    samples, coarse_rows, coarse_cols, width = coarse.shape
    fine_rows, fine_cols, channels = fine_input.shape[1:]
    peers = lax.axis_size("rows") * lax.axis_size("cols")
    groups = coarse_rows * coarse_cols // peers
    grid_tokens = regroup(coarse.reshape(peers, groups, width))
    result, saved = attend(grid_tokens, w_qkv, w_out)
    attended = result.astype(jnp.bfloat16)
    context = (grid_tokens.astype(jnp.float32) + attended.astype(jnp.float32)).astype(jnp.bfloat16)
    raised = jnp.einsum("sgw,wc->sgc", context, w_up, preferred_element_type=jnp.float32).astype(jnp.bfloat16)
    lifted = regroup(raised).reshape(samples, coarse_rows, coarse_cols, channels).astype(jnp.float32)
    spread = jnp.repeat(jnp.repeat(lifted, 4, axis=1), 4, axis=2)
    hidden = fine_input.astype(jnp.float32) + spread
    active = jax.nn.gelu(hidden).astype(jnp.bfloat16)
    padded = with_halo(active, (("rows", 1), ("cols", 2)), 1)
    conv_out = jnp.zeros(hidden.shape, jnp.float32)
    for row_tap in range(3):
        for col_tap in range(3):
            window = padded[:, row_tap : row_tap + fine_rows, col_tap : col_tap + fine_cols]
            conv_out = conv_out + jnp.einsum(
                "bhwc,ck->bhwk",
                window,
                w_conv[row_tap, col_tap],
                preferred_element_type=jnp.float32,
            )
    outer = (hidden + conv_out).astype(jnp.bfloat16)
    quantiles = jnp.einsum("bhwc,cq->bqhw", outer, w_head, preferred_element_type=jnp.float32)
    target = rain_bins.astype(jnp.float32)[:, None] / 16.0 - 1.0
    levels = ((jnp.arange(QUANT) + 1).astype(jnp.float32) / (QUANT + 1.0))[None, :, None, None]
    error_term = target - quantiles
    weight_term = jnp.where(error_term < 0.0, 1.0 - levels, levels)
    magnitude = jnp.abs(error_term)
    huber_term = jnp.where(magnitude <= 1.0, 0.5 * error_term * error_term, magnitude - 0.5)
    loss_part = jnp.sum(weight_term * huber_term, axis=(0, 1, 2)).reshape(1, 128)
    pixel_count = (
        samples
        * lax.axis_size("batch")
        * fine_rows
        * lax.axis_size("rows")
        * fine_cols
        * lax.axis_size("cols")
    )
    root_count = jnp.sqrt(jnp.asarray(pixel_count, jnp.float32))
    dpred = (-weight_term * jnp.clip(error_term, -1.0, 1.0) / root_count).astype(jnp.bfloat16)
    grad_head = jnp.einsum("bhwc,bqhw->cq", outer, dpred, preferred_element_type=jnp.float32)
    douter = jnp.einsum("bqhw,cq->bhwc", dpred, w_head, preferred_element_type=jnp.float32)
    douter_b = douter.astype(jnp.bfloat16)
    grad_pad = with_halo(douter_b, (("rows", 1), ("cols", 2)), 1)
    dactive = jnp.zeros(hidden.shape, jnp.float32)
    kernel_rows = []
    for row_tap in range(3):
        kernel_row = []
        for col_tap in range(3):
            window = padded[:, row_tap : row_tap + fine_rows, col_tap : col_tap + fine_cols]
            kernel_row.append(
                jnp.einsum("bhwc,bhwk->ck", window, douter_b, preferred_element_type=jnp.float32)
            )
            back_window = grad_pad[
                :, 2 - row_tap : 2 - row_tap + fine_rows, 2 - col_tap : 2 - col_tap + fine_cols
            ]
            dactive = dactive + jnp.einsum(
                "bhwk,ck->bhwc",
                back_window,
                w_conv[row_tap, col_tap],
                preferred_element_type=jnp.float32,
            )
        kernel_rows.append(jnp.stack(kernel_row))
    grad_conv = jnp.stack(kernel_rows)
    slope = jax.vjp(jax.nn.gelu, hidden)[1](dactive)[0]
    dhidden = douter + slope
    grad_fine = dhidden * root_count
    dlift = (
        dhidden.reshape(samples, coarse_rows, 4, coarse_cols, 4, channels)
        .sum(axis=(2, 4))
        .astype(jnp.bfloat16)
    )
    grid_lift = regroup(dlift.reshape(peers, groups, channels))
    grad_up = jnp.einsum("sgw,sgc->wc", context, grid_lift, preferred_element_type=jnp.float32)
    grid_grads = jnp.einsum("sgc,wc->sgw", grid_lift, w_up, preferred_element_type=jnp.float32).astype(
        jnp.bfloat16
    )
    grad_qkv, grad_out = attend_back(grid_tokens, w_out, saved, grid_grads)
    grad_qkv, grad_out, grad_up, grad_conv, grad_head, loss_total = reduce_all(
        grad_qkv, grad_out, grad_up, grad_conv, grad_head, loss_part
    )
    loss_value = loss_total / (pixel_count * QUANT)
    return (quantiles, loss_value, grad_qkv, grad_out, grad_up, grad_conv, grad_head, grad_fine)


def solution(mesh):
    placed = (
        P("batch", "rows", "cols", None),
        P("batch", "rows", "cols", None),
        P("batch", "rows", "cols"),
        P(),
        P(),
        P(),
        P(),
        P(),
    )
    return jax.shard_map(
        body,
        mesh=mesh,
        in_specs=placed,
        out_specs=(
            P("batch", None, "rows", "cols"),
            P(),
            P(),
            P(),
            P(),
            P(),
            P(),
            P("batch", "rows", "cols", None),
        ),
        check_vma=False,
    )
```

```python
import jax
import jax.numpy as jnp
import numpy as np
from jax import lax
from jax.experimental import pallas as pl
from jax.experimental.pallas import tpu as pltpu
from jax.sharding import PartitionSpec as P

HEAD_DIM = 32
QUANT = 9
UNITS = 1280
MESH = pl.DeviceIdType.MESH


def meet(targets):
    barrier = pltpu.get_barrier_semaphore()
    for target in targets:
        pl.semaphore_signal(barrier, inc=1, device_id=target, device_id_type=MESH)
    pl.semaphore_wait(barrier, len(targets))


def add_blocks(dst, dst_at, terms, count, step):
    def one(i, carry):
        at = i * step
        total = None
        for ref, start in terms:
            value = ref[pl.ds(start + at, step)].astype(jnp.float32)
            total = value if total is None else total + value
        dst[pl.ds(dst_at + at, step)] = total.astype(dst.dtype)
        return carry

    lax.fori_loop(0, count // step, one, 0)


def reduce_kernel(g, out, got0, sum0, got1, sum1, got2, sum2, got3, ss0, rs0, ss1, rs1, ss2, rs2, ss3, rs3,
                  sa3, ra3, sa2, ra2, sa1, ra1, sa0, ra0):
    row, col, batch = lax.axis_index("rows"), lax.axis_index("cols"), lax.axis_index("batch")
    core, deep = row % 2, (row // 2) * 2 + batch
    x, y = col // 4, col % 4
    first = x * (1 - core) + y * core
    second = y * (1 - core) + x * core
    other = {"rows": row + 1 - 2 * core}
    u0, u1, u2, u3 = UNITS // 2, UNITS // 8, UNITS // 32, UNITS // 256

    def in_first(k):
        p = (first + k) % 4
        return p, {"cols": (p * 4 + y) * (1 - core) + (x * 4 + p) * core}

    def in_second(k):
        p = (second + k) % 4
        return p, {"cols": (x * 4 + p) * (1 - core) + (p * 4 + y) * core}

    def in_deep(k):
        p = (deep + k) % 8
        return p, {"rows": (p // 2) * 2 + core, "batch": p % 2}

    def copy(src, dst, send, recv, to):
        return pltpu.make_async_remote_copy(src_ref=src, dst_ref=dst, send_sem=send, recv_sem=recv,
                                            device_id=to, device_id_type=MESH)

    meet([other] + [in_first(k)[1] for k in (1, 2, 3)] + [in_second(k)[1] for k in (1, 2, 3)]
         + [in_deep(k)[1] for k in range(1, 8)])

    near = []
    for q in range(4):
        c = copy(g.at[pl.ds((1 - core) * u0 + q * u1, u1)], got0.at[pl.ds(q * u1, u1)], ss0.at[q], rs0.at[q], other)
        c.start()
        near.append(c)
    for c in near:
        c.wait()
    add_blocks(sum0, 0, [(g, core * u0), (got0, 0)], u0, 8)

    def scatter(src, size, got, total, send, recv, where, mine, n, step):
        copies = []
        for k in range(1, n):
            p, to = where(k)
            c = copy(src.at[pl.ds(p * size, size)], got.at[k - 1], send.at[k - 1], recv.at[k - 1], to)
            c.start()
            copies.append(c)
        for c in copies:
            c.wait()
        def one(i, carry):
            at = i * step
            value = src[pl.ds(mine * size + at, step)].astype(jnp.float32)
            for k in range(n - 1):
                value = value + got[k, pl.ds(at, step)].astype(jnp.float32)
            total(at, step, value)
            return carry
        lax.fori_loop(0, size // step, one, 0)

    def keep(ref, base):
        def store(at, step, value):
            ref[pl.ds(base + at, step)] = value.astype(ref.dtype)
        return store

    scatter(sum0, u1, got1, keep(sum1, 0), ss1, rs1, in_first, first, 4, 8)
    scatter(sum1, u2, got2, keep(sum2, 0), ss2, rs2, in_second, second, 4, 8)
    place = core * u0 + first * u1 + second * u2
    scatter(sum2, u3, got3, keep(out, place + deep * u3), ss3, rs3, in_deep, deep, 8, 5)

    def gather(start, size, send, recv, where, n):
        copies = []
        block = out.at[pl.ds(start, size)]
        for k in range(1, n):
            c = copy(block, block, send.at[k - 1], recv.at[k - 1], where(k)[1])
            c.start()
            copies.append(c)
        for c in copies:
            c.wait()

    gather(place + deep * u3, u3, sa3, ra3, in_deep, 8)
    gather(place, u2, sa2, ra2, in_second, 4)
    gather(core * u0 + first * u1, u1, sa1, ra1, in_first, 4)
    gather(core * u0, u0, sa0, ra0, lambda k: (0, other), 2)


def reduce_units(g):
    unit = (8, 128)
    b16 = jnp.bfloat16
    dma = pltpu.SemaphoreType.DMA
    return pl.pallas_call(
        reduce_kernel,
        out_shape=jax.ShapeDtypeStruct((UNITS,) + unit, b16),
        in_specs=[pl.BlockSpec(memory_space=pltpu.VMEM)],
        out_specs=pl.BlockSpec(memory_space=pltpu.VMEM),
        scratch_shapes=[
            pltpu.VMEM((UNITS // 2,) + unit, b16),
            pltpu.VMEM((UNITS // 2,) + unit, b16),
            pltpu.VMEM((3, UNITS // 8) + unit, b16),
            pltpu.VMEM((UNITS // 8,) + unit, b16),
            pltpu.VMEM((3, UNITS // 32) + unit, b16),
            pltpu.VMEM((UNITS // 32,) + unit, b16),
            pltpu.VMEM((7, UNITS // 256) + unit, b16),
            dma((4,)), dma((4,)), dma((3,)), dma((3,)), dma((3,)), dma((3,)), dma((7,)), dma((7,)),
            dma((7,)), dma((7,)), dma((3,)), dma((3,)), dma((3,)), dma((3,)), dma((1,)), dma((1,)),
        ],
        compiler_params=pltpu.CompilerParams(collective_id=7, has_side_effects=True,
                                             vmem_limit_bytes=40 * 1024 * 1024),
    )(g)


F32, B16 = jnp.float32, jnp.bfloat16
DMA = pltpu.SemaphoreType.DMA
SCALE = HEAD_DIM ** (-0.5)
LIMIT = 56 * 1024 * 1024


def onehot(rows, cols, pairs):
    table = np.zeros((rows, cols), np.float32)
    for row, col in pairs:
        table[row, col] = 1.0
    return jnp.asarray(table, B16)


def mid_table():
    return onehot(256, 256, [(p * 16 + r * 2 + m, r * 32 + p * 2 + m)
                             for p in range(16) for r in range(8) for m in range(2)])


def group_table():
    return onehot(256, 256, [(m * 128 + c * 8 + r, c * 16 + r * 2 + m)
                             for m in range(2) for c in range(16) for r in range(8)])


def back_table():
    pairs = []
    for r in range(8):
        for j in range(32):
            pairs.append((r * 48 + j, (1 + j // 2) * 16 + r * 2 + j % 2))
        pairs.append((r * 48 + 32, 17 * 16 + r * 2))
        pairs.append((r * 48 + 35, r * 2 + 1))
    return onehot(384, 288, pairs)


def pick_table(first):
    return onehot(16, 128, [(2 * i + s, 16 * i + first + s) for i in range(8) for s in range(2)])


def spread_table(first):
    return onehot(128, 16, [(16 * i + first + s, 2 * i + s) for i in range(8) for s in range(2)])


def bins_table():
    return onehot(48, 64, [(0, 15)] + [(1 + y, 16 + y) for y in range(32)] + [(33, 48)])


def up_table():
    return onehot(144, 48, [(p, p // 4) for p in range(144)])


def sum_table():
    return onehot(32, 128, [(p // 4, p) for p in range(128)])


def dot(a, b):
    return jnp.dot(a, b, preferred_element_type=F32)


def dot_nt(a, b):
    return lax.dot_general(a, b, (((1,), (1,)), ((), ())), preferred_element_type=F32)


def rcopy(src, dst, send, recv, to):
    return pltpu.make_async_remote_copy(src_ref=src, dst_ref=dst, send_sem=send, recv_sem=recv,
                                        device_id=to, device_id_type=MESH)


def row_peers(row):
    return [{"rows": (row + k) % 8} for k in range(1, 8)]


def col_peers(col):
    return [{"cols": (col + k) % 16} for k in range(1, 16)]


def rows_out(src, got, send, recv, row):
    copies = []
    for k in range(1, 8):
        p = (row + k) % 8
        c = rcopy(src.at[p], got.at[row], send.at[k - 1], recv.at[k - 1], {"rows": p})
        c.start()
        copies.append(c)
    got[row] = src[row]
    return copies


def cols_out(src, got, send, recv, col):
    copies = []
    for k in range(1, 16):
        p = (col + k) % 16
        c = rcopy(src.at[p], got.at[col], send.at[k - 1], recv.at[k - 1], {"cols": p})
        c.start()
        copies.append(c)
    got[col] = src[col]
    return copies


def wait_all(copies):
    for c in copies:
        c.wait()


def tokens_kernel(coarse, fine, bins, mid, pick_lo, pick_hi, spread_lo, spread_hi, place, tokens, field, rain, rain_lo, rain_hi,
                  got, turned, bin_got, edge_out, edge_in, bin_out, s_r, r_r, s_c, r_c, s_h, r_h, s_e, r_e, s_l):
    row, col = lax.axis_index("rows"), lax.axis_index("cols")
    meet(row_peers(row) + col_peers(col))
    own = pltpu.make_async_copy(fine, field.at[pl.ds(4, 32), pl.ds(0, 128)], s_l.at[0])
    own.start()
    first = rows_out(coarse, got, s_r, r_r, row)

    def halo(start):
        lower, upper = row > 0, row < 7

        def down():
            for n, (src, dst) in enumerate([
                (fine.at[pl.ds(30, 2)], field.at[pl.ds(2, 2), pl.ds(0, 128)]),
                (bins.at[pl.ds(16, 16)], bin_got.at[pl.ds(0, 16)]),
            ]):
                c = rcopy(src, dst, s_h.at[n], r_h.at[n], {"rows": row + 1})
                c.start() if start else c.wait_send()

        def up():
            for n, (src, dst) in enumerate([
                (fine.at[pl.ds(0, 2)], field.at[pl.ds(36, 2), pl.ds(0, 128)]),
                (bins.at[pl.ds(0, 16)], bin_got.at[pl.ds(48, 16)]),
            ]):
                c = rcopy(src, dst, s_h.at[2 + n], r_h.at[2 + n], {"rows": row - 1})
                c.start() if start else c.wait_send()

        def from_low():
            for n, (src, dst) in enumerate([
                (fine.at[pl.ds(30, 2)], field.at[pl.ds(2, 2), pl.ds(0, 128)]),
                (bins.at[pl.ds(16, 16)], bin_got.at[pl.ds(0, 16)]),
            ]):
                rcopy(src, dst, s_h.at[n], r_h.at[n], {"rows": row - 1}).wait_recv()

        def from_high():
            for n, (src, dst) in enumerate([
                (fine.at[pl.ds(0, 2)], field.at[pl.ds(36, 2), pl.ds(0, 128)]),
                (bins.at[pl.ds(0, 16)], bin_got.at[pl.ds(48, 16)]),
            ]):
                rcopy(src, dst, s_h.at[2 + n], r_h.at[2 + n], {"rows": row + 1}).wait_recv()

        pl.when(upper)(down)
        pl.when(lower)(up)
        if not start:
            pl.when(lower)(from_low)
            pl.when(upper)(from_high)

    halo(True)

    @pl.when(row == 0)
    def _():
        field[pl.ds(0, 4), :128] = jnp.zeros((4, 128, 128), B16)
        bin_got[pl.ds(0, 16)] = jnp.zeros((16, 128), B16)

    @pl.when(row > 0)
    def _():
        field[pl.ds(0, 2), :128] = jnp.zeros((2, 128, 128), B16)

    @pl.when(row == 7)
    def _():
        field[pl.ds(36, 4), :128] = jnp.zeros((4, 128, 128), B16)
        bin_got[pl.ds(48, 16)] = jnp.zeros((16, 128), B16)

    @pl.when(row < 7)
    def _():
        field[pl.ds(38, 2), :128] = jnp.zeros((2, 128, 128), B16)

    bin_got[pl.ds(16, 32)] = bins[...]

    wait_all(first)
    turned[...] = dot(mid[...], got[...].reshape(256, 512)).astype(B16).reshape(16, 16, 512)
    second = cols_out(turned, tokens, s_c, r_c, col)

    own.wait()
    halo(False)
    rows = dot(place[...], bin_got[...])
    rain[...] = rows
    bin_out[0] = jnp.broadcast_to(rows[:, 127:128], (48, 128)).astype(B16)
    bin_out[1] = jnp.broadcast_to(rows[:, 0:1], (48, 128)).astype(B16)
    for q in range(5):
        edge_out[0, q] = dot(pick_hi[...], field[8 * q:8 * q + 8, 112:128].reshape(128, 128)).astype(B16)
        edge_out[1, q] = dot(pick_lo[...], field[8 * q:8 * q + 8, 0:16].reshape(128, 128)).astype(B16)

    @pl.when(col == 0)
    def _():
        edge_in[0] = jnp.zeros((5, 16, 128), B16)
        rain_lo[...] = jnp.zeros((48, 128), B16)

    @pl.when(col == 15)
    def _():
        edge_in[1] = jnp.zeros((5, 16, 128), B16)
        rain_hi[...] = jnp.zeros((48, 128), B16)

    def sides(side, to):
        into = (rain_lo, rain_hi)[side]
        return [rcopy(edge_out.at[side], edge_in.at[side], s_e.at[2 * side], r_e.at[2 * side], {"cols": to}),
                rcopy(bin_out.at[side], into, s_e.at[2 * side + 1], r_e.at[2 * side + 1], {"cols": to})]

    @pl.when(col < 15)
    def _():
        for c in sides(0, col + 1):
            c.start()

    @pl.when(col > 0)
    def _():
        for c in sides(1, col - 1):
            c.start()

    @pl.when(col < 15)
    def _():
        for c in sides(0, col + 1):
            c.wait_send()
        for c in sides(1, col + 1):
            c.wait_recv()

    @pl.when(col > 0)
    def _():
        for c in sides(1, col - 1):
            c.wait_send()
        for c in sides(0, col - 1):
            c.wait_recv()

    for q in range(5):
        edge = dot(spread_hi[...], edge_in[0, q]) + dot(spread_lo[...], edge_in[1, q])
        field[8 * q:8 * q + 8, 128:144] = edge.astype(B16).reshape(8, 16, 128)
    wait_all(second)


def vmem(shape, dtype):
    return pltpu.VMEM(shape, dtype)


def call(kernel, out, scratch, args, collective=None, hbm=()):
    extra = {} if collective is None else {"collective_id": collective, "has_side_effects": True}
    return pl.pallas_call(
        kernel,
        out_shape=[jax.ShapeDtypeStruct(shape, dtype) for shape, dtype in out],
        in_specs=[pl.BlockSpec(memory_space=pl.ANY if n in hbm else pltpu.VMEM) for n in range(len(args))],
        out_specs=[pl.BlockSpec(memory_space=pltpu.VMEM) for _ in out],
        scratch_shapes=scratch,
        compiler_params=pltpu.CompilerParams(vmem_limit_bytes=LIMIT, **extra),
    )(*args)


def lift_kernel(raised, back, lifted, slots, turned, s_c, r_c, s_x, r_x, s_r, r_r, s_y, r_y):
    row, col = lax.axis_index("rows"), lax.axis_index("cols")
    meet(row_peers(row) + col_peers(col))

    def spread(count, axis, me, src, low, main, copies_sems, extra_sems):
        send, recv = copies_sems
        send_x, recv_x = extra_sems
        copies = []
        for k in range(1, count):
            p = (me + k) % count
            c = rcopy(src.at[p], main.at[1 + me], send.at[k - 1], recv.at[k - 1], {axis: p})
            c.start()
            copies.append(c)
        main[1 + me] = src[me]

        def after(t):
            return rcopy(src.at[t - 1], main.at[0], send_x.at[t], recv_x.at[0], {axis: t})

        def before(t):
            return rcopy(src.at[t + 1], main.at[count + 1], send_x.at[t], recv_x.at[1], {axis: t})

        @pl.when(me == count - 1)
        def _():
            for t in range(1, count - 1):
                after(t).start()
            main[0] = src[count - 2]
            main[count + 1] = jnp.zeros(main.shape[1:], B16)

        @pl.when(me == 0)
        def _():
            for t in range(1, count - 1):
                before(t).start()
            main[count + 1] = src[1]
            main[0] = jnp.zeros(main.shape[1:], B16)

        @pl.when(me == count - 1)
        def _():
            for t in range(1, count - 1):
                after(t).wait_send()

        @pl.when(me == 0)
        def _():
            for t in range(1, count - 1):
                before(t).wait_send()

        @pl.when((me > 0) & (me < count - 1))
        def _():
            after(1).wait_recv()
            before(1).wait_recv()

        wait_all(copies)

    spread(16, "cols", col, raised, None, slots, (s_c, r_c), (s_x, r_x))
    turned[...] = dot(back[...], slots[...].reshape(288, 128)).astype(B16).reshape(8, 48, 128)
    spread(8, "rows", row, turned, None, lifted, (s_r, r_r), (s_y, r_y))


def fold_kernel(dlift, mid, out, got, turned, s_r, r_r, s_c, r_c):
    row, col = lax.axis_index("rows"), lax.axis_index("cols")
    meet(row_peers(row) + col_peers(col))
    wait_all(rows_out(dlift, got, s_r, r_r, row))
    turned[...] = dot(mid[...], got[...].reshape(256, 128)).astype(B16).reshape(16, 16, 128)
    wait_all(cols_out(turned, out, s_c, r_c, col))


def head_mask(h):
    lane = lax.broadcasted_iota(jnp.int32, (1, 128), 1)
    return jnp.where((lane >> 5) == h, 1.0, 0.0).astype(B16)


def heads_down(tile):
    return jnp.concatenate([tile * head_mask(h) for h in range(4)], axis=0)


def heads_across(tile):
    turned = tile.astype(F32).T
    line = lax.broadcasted_iota(jnp.int32, (128, 1), 0) >> 5
    return jnp.concatenate([jnp.where(line == h, turned, 0.0) for h in range(4)], axis=1).astype(B16)


def side_by_side(stack):
    return jnp.concatenate([stack[h * 128:(h + 1) * 128] for h in range(4)], axis=1)


def attend_kernel(tokens, w_qkv, w_out, w_up, group, ungroup, raised, tok, qkv, prob, mixed, context):
    tok[...] = dot(group[...], tokens[...]).astype(B16)
    for n in range(3):
        qkv[:, n * 512:(n + 1) * 512] = dot(tok[...], w_qkv[:, n * 512:(n + 1) * 512]).astype(B16)
    for g in range(2):
        for t in range(4):
            rows, at = slice(g * 128, g * 128 + 128), t * 128
            query = qkv[rows, at:at + 128]
            keyed = qkv[rows, 512 + at:512 + at + 128]
            valued = qkv[rows, 1024 + at:1024 + at + 128]
            scores = dot_nt(heads_down(query), keyed) * SCALE
            peak = jnp.max(scores, axis=-1, keepdims=True)
            powers = jnp.exp(scores - peak)
            share = powers / jnp.sum(powers, axis=-1, keepdims=True)
            prob[g * 4 + t] = share
            mixed[rows, at:at + 128] = dot(side_by_side(share.astype(B16)), heads_down(valued)).astype(B16)
    attended = dot(mixed[...], w_out[...]).astype(B16)
    context[...] = (tok[...].astype(F32) + attended.astype(F32)).astype(B16)
    lifted = dot(context[...], w_up[...]).astype(B16)
    raised[...] = dot(ungroup[...], lifted).astype(B16)


def put(g, at, value):
    rows, cols = value.shape
    size = rows // 8
    for n in range(cols // 128):
        g[at + n * size:at + (n + 1) * size] = value[:, n * 128:(n + 1) * 128].reshape(size, 8, 128).astype(B16)


def attend_back_kernel(folded, group, w_out, w_up, tok, qkv, prob, mixed, context, local, g, dquery, dkey, dvalue):
    lift = dot(group[...], folded[...]).astype(B16)
    dcontext = dot_nt(lift, w_up[...]).astype(B16)
    mix_grad = dot_nt(dcontext, w_out[...]).astype(B16)
    g[1088:1234] = local[...]
    g[1234:UNITS] = jnp.zeros((UNITS - 1234, 8, 128), B16)
    for s in range(2):
        for t in range(4):
            rows, at = slice(s * 128, s * 128 + 128), t * 128
            query = qkv[rows, at:at + 128]
            keyed = qkv[rows, 512 + at:512 + at + 128]
            valued = qkv[rows, 1024 + at:1024 + at + 128]
            mine = mix_grad[rows, at:at + 128]
            dprob = dot_nt(heads_down(mine), valued)
            share = prob[s * 4 + t]
            inner = jnp.sum(share * dprob, axis=-1, keepdims=True)
            dscore = (share * (dprob - inner) * SCALE).astype(B16)
            dquery[rows, at:at + 128] = dot(side_by_side(dscore), heads_down(keyed)).astype(B16)
            dkey[at:at + 128, rows] = dot(heads_across(query), dscore).astype(B16)
            dvalue[at:at + 128, rows] = dot(heads_across(mine), share.astype(B16)).astype(B16)
    turned = tok[...].astype(F32).T.astype(B16)
    put(g, 0, dot(turned, dquery[...]))
    put(g, 256, dot_nt(turned, dkey[...]))
    put(g, 512, dot_nt(turned, dvalue[...]))
    put(g, 768, dot(mixed[...].astype(F32).T.astype(B16), dcontext))
    put(g, 1024, dot(context[...].astype(F32).T.astype(B16), lift))


ROOT_2_PI = 0.7978845608028654


def shifted(line):
    return jnp.concatenate([pltpu.roll(line, 1, 0), line, pltpu.roll(line, 143, 0)], axis=1)


def conv_kernel(field, lifted, rain, rain_lo, rain_hi, up, fold, w_conv, w_head, w_head_t,
                quantiles, grad_fine, dlift, local,
                hidden, slope, active, outer, out_grad, out_wide, out_turned, halo_grad, kernel_sum, loss_sum, head_sum):
    row, col = lax.axis_index("rows"), lax.axis_index("cols")
    place = lax.broadcasted_iota(jnp.int32, (144, 1), 0)
    right = jnp.where(col < 15, 130, 128)
    left = jnp.where(col > 0, 142, 144)
    inside = (place < right) | (place >= left)

    def start(i, carry):
        raised = dot(up[...], lifted[i])
        for s in range(4):
            y = 4 * i + s - 4
            x = field[4 * i + s].astype(F32) + raised
            square = x * x
            bend = jnp.tanh(ROOT_2_PI * x * (1.0 + 0.044715 * square))
            half = 0.5 * (1.0 + bend)
            seen = (row * 32 + y >= 0) & (row * 32 + y < 256)
            act = jnp.where(inside & seen, x * half, 0.0)
            hidden[4 * i + s] = x
            active[4 * i + s] = shifted(act).astype(B16)
            slope[4 * i + s] = half[:128] + (0.5 * ROOT_2_PI) * x[:128] * (1.0 - bend[:128] * bend[:128]) * (
                1.0 + (3 * 0.044715) * square[:128])
        return carry

    lax.fori_loop(0, 10, start, 0)

    def forward(i, carry):
        total = hidden[pl.ds(4 * i + 3, 4)].reshape(576, 128)
        for a in range(3):
            window = active[pl.ds(4 * i + 2 + a, 4)].reshape(576, 384)
            total = total + dot(window, w_conv[a].reshape(384, 128))
        outer[pl.ds(4 * i, 4)] = total.astype(B16).reshape(4, 144, 128)
        return carry

    lax.fori_loop(0, 9, forward, 0)

    def quantile_terms(predicted, target, keep):
        level = (lax.broadcasted_iota(jnp.int32, (16, 1), 0) + 1).astype(F32) / 10.0
        error = target - predicted
        weight = jnp.where(error < 0.0, 1.0 - level, level)
        down = jnp.where(keep, -weight * jnp.clip(error, -1.0, 1.0) * (1.0 / 1024.0), 0.0)
        return error, weight, down

    quant = lax.broadcasted_iota(jnp.int32, (16, 1), 0) < QUANT

    lane = lax.broadcasted_iota(jnp.int32, (48, 640), 1)
    line = lax.broadcasted_iota(jnp.int32, (48, 640), 0)
    wide_lo = jnp.concatenate([rain_lo[...].astype(F32)] * 5, axis=1)
    wide_hi = jnp.concatenate([rain_hi[...].astype(F32)] * 5, axis=1)
    here = (lane >> 4) == line
    edge_bins = jnp.sum(jnp.where(here & ((lane & 15) == 0), wide_hi, 0.0)
                        + jnp.where(here & ((lane & 15) == 15), wide_lo, 0.0), axis=0, keepdims=True)
    edge = jnp.concatenate([outer[:, 128:144, :].reshape(576, 128), jnp.zeros((64, 128), B16)], axis=0)
    predicted = dot_nt(w_head_t[...], edge)
    at = lax.broadcasted_iota(jnp.int32, (1, 640), 1)
    glob = row * 32 + (at >> 4) - 1
    keep = ((((at & 15) == 0) & (col < 15)) | (((at & 15) == 15) & (col > 0))) & (at < 544) & (glob >= 0) & (glob < 256)
    down = quantile_terms(predicted, edge_bins * (1.0 / 16.0) - 1.0, keep & quant)[2].astype(B16)
    halo_grad[...] = dot(down.astype(F32).T.astype(B16), w_head_t[...]).reshape(40, 16, 128)

    loss_sum[...] = jnp.zeros((16, 128), F32)
    head_sum[...] = jnp.zeros((16, 128), F32)
    kernel_sum[...] = jnp.zeros((3, 128, 384), F32)

    def turn(i, carry):
        lines = [rain[pl.ds(4 * i + s, 1), :] for s in range(4)]
        target = jnp.concatenate(lines, axis=1) * (1.0 / 16.0) - 1.0
        pixels = outer[pl.ds(4 * i, 4), :128].reshape(512, 128)
        predicted = dot_nt(w_head_t[...], pixels)
        glob = row * 32 + 4 * i - 1
        at = lax.broadcasted_iota(jnp.int32, (1, 512), 1) >> 7
        mine = (4 * i - 1 + at >= 0) & (4 * i - 1 + at < 32)
        seen = (glob + at >= 0) & (glob + at < 256) & (4 * i - 1 + at < 33)
        error, weight, down = quantile_terms(predicted, target, seen & quant)
        size = jnp.abs(error)
        loss = weight * jnp.where(size <= 1.0, 0.5 * error * error, size - 0.5)
        loss = jnp.where(mine & quant, loss, 0.0)
        loss_sum[...] += loss[:, :128] + loss[:, 128:256] + loss[:, 256:384] + loss[:, 384:]
        down_b = down.astype(B16)
        head_sum[...] += dot(jnp.where(mine, down, 0.0).astype(B16), pixels)
        across = dot(w_head[...], down_b).astype(B16)
        along = dot(down_b.astype(F32).T.astype(B16), w_head_t[...])
        for s in range(4):
            y = 4 * i + s - 1
            value = predicted[:, s * 128:(s + 1) * 128]

            @pl.when((y >= 0) & (y < 32))
            def _():
                for q in range(QUANT):
                    quantiles[q, pl.ds(y, 1), :] = value[q:q + 1]

            out_turned[4 * i + s] = across[:, s * 128:(s + 1) * 128]
            mid_part = along[s * 128:(s + 1) * 128]
            out_grad[4 * i + s] = mid_part
            full = jnp.concatenate([mid_part, halo_grad[4 * i + s]], axis=0)
            out_wide[4 * i + s] = shifted(full).astype(B16)
        return carry

    lax.fori_loop(0, 9, turn, 0)

    def back(i, carry):
        total = None
        for a in range(3):
            window = out_wide[pl.ds(4 * i + a, 4), :128].reshape(512, 384)
            turned = jnp.concatenate([w_conv[2 - a, 2 - b] for b in range(3)], axis=1)
            part = dot_nt(window, turned)
            total = part if total is None else total + part
        across = jnp.concatenate([out_turned[4 * i + 1 + s] for s in range(4)], axis=1)
        for a in range(3):
            window = active[pl.ds(4 * i + 3 + a, 4), :128].reshape(512, 384)
            kernel_sum[a] += dot(across, window)
        dhidden = out_grad[pl.ds(4 * i + 1, 4)] + slope[pl.ds(4 * i + 4, 4)] * total.reshape(4, 128, 128)
        grad_fine[pl.ds(4 * i, 4)] = dhidden * 1024.0
        summed = dhidden[0] + dhidden[1] + dhidden[2] + dhidden[3]
        high = summed.astype(B16)
        low = (summed - high.astype(F32)).astype(B16)
        dlift[i] = (dot(fold[...], high) + dot(fold[...], low)).astype(B16)
        return carry

    lax.fori_loop(0, 8, back, 0)
    for a in range(3):
        for b in range(3):
            local[a * 48 + b * 16:a * 48 + b * 16 + 16] = kernel_sum[a, :, b * 128:(b + 1) * 128].T.reshape(16, 8, 128).astype(B16)
    spot = lax.broadcasted_iota(jnp.int32, (16, 1), 0)
    total = jnp.sum(loss_sum[...], axis=0, keepdims=True)
    tail = jnp.where(spot < QUANT, head_sum[...], jnp.where(spot == QUANT, total, 0.0))
    local[144:146] = tail.reshape(2, 8, 128).astype(B16)


def unpack_kernel(g, grad_qkv, grad_out, grad_up, grad_conv, tail):
    for n in range(12):
        grad_qkv[:, n * 128:(n + 1) * 128] = g[n * 64:(n + 1) * 64].astype(F32).reshape(512, 128)
    for n in range(4):
        grad_out[:, n * 128:(n + 1) * 128] = g[768 + n * 64:768 + (n + 1) * 64].astype(F32).reshape(512, 128)
    grad_up[...] = g[1024:1088].astype(F32).reshape(512, 128)
    grad_conv[...] = g[1088:1232].astype(F32).reshape(1152, 128)
    tail[...] = g[1232:1234].astype(F32).reshape(16, 128)


def body(fine_input, coarse, rain_bins, w_qkv, w_out, w_up, w_conv, w_head):
    fine, bins = fine_input[0], rain_bins[0].astype(B16)
    mid, group = mid_table(), group_table()
    head = jnp.pad(w_head, ((0, 0), (0, 16 - QUANT)))
    head_t = head.T
    tokens, field, rain, rain_lo, rain_hi = call(
        tokens_kernel,
        [((16, 16, 512), B16), ((40, 144, 128), B16), ((48, 128), F32), ((48, 128), B16), ((48, 128), B16)],
        [vmem((8, 32, 512), B16), vmem((16, 16, 512), B16), vmem((64, 128), B16),
         vmem((2, 5, 16, 128), B16), vmem((2, 5, 16, 128), B16), vmem((2, 48, 128), B16),
         DMA((7,)), DMA((7,)), DMA((15,)), DMA((15,)), DMA((4,)), DMA((4,)), DMA((4,)), DMA((4,)), DMA((1,))],
        [coarse[0], fine, bins, mid, pick_table(0), pick_table(14), spread_table(0), spread_table(14), bins_table()],
        collective=1, hbm=(1,),
    )
    raised, tok, qkv, prob, mixed, context = call(
        attend_kernel,
        [((256, 128), B16), ((256, 512), B16), ((256, 1536), B16), ((8, 512, 128), F32), ((256, 512), B16),
         ((256, 512), B16)],
        [],
        [tokens.reshape(256, 512), w_qkv, w_out, w_up, group, group.T],
    )
    lifted, = call(
        lift_kernel,
        [((10, 48, 128), B16)],
        [vmem((18, 16, 128), B16), vmem((8, 48, 128), B16),
         DMA((15,)), DMA((15,)), DMA((16,)), DMA((2,)), DMA((7,)), DMA((7,)), DMA((8,)), DMA((2,))],
        [raised.reshape(16, 16, 128), back_table()],
        collective=2,
    )
    quantiles, grad_fine, dlift, local = call(
        conv_kernel,
        [((9, 32, 128), F32), ((32, 128, 128), F32), ((8, 32, 128), B16), ((146, 8, 128), B16)],
        [vmem((40, 144, 128), F32), vmem((40, 128, 128), F32), vmem((40, 144, 384), B16), vmem((36, 144, 128), B16),
         vmem((36, 128, 128), F32), vmem((36, 144, 384), B16), vmem((36, 128, 128), B16), vmem((40, 16, 128), F32),
         vmem((3, 128, 384), F32), vmem((16, 128), F32), vmem((16, 128), F32)],
        [field, lifted, rain, rain_lo, rain_hi, up_table(), sum_table(), w_conv, head, head_t],
    )
    folded, = call(
        fold_kernel,
        [((16, 16, 128), B16)],
        [vmem((8, 32, 128), B16), vmem((16, 16, 128), B16), DMA((7,)), DMA((7,)), DMA((15,)), DMA((15,))],
        [dlift, mid],
        collective=3,
    )
    g, = call(
        attend_back_kernel,
        [((UNITS, 8, 128), B16)],
        [vmem((256, 512), B16), vmem((512, 256), B16), vmem((512, 256), B16)],
        [folded.reshape(256, 128), group, w_out, w_up, tok, qkv, prob, mixed, context, local],
    )
    grad_qkv, grad_out, grad_up, grad_conv, tail = call(
        unpack_kernel,
        [((512, 1536), F32), ((512, 512), F32), ((512, 128), F32), ((1152, 128), F32), ((16, 128), F32)],
        [],
        [reduce_units(g)],
    )
    loss_value = jnp.sum(tail[QUANT]) / (1048576.0 * QUANT)
    return (quantiles[None], loss_value, grad_qkv, grad_out, grad_up, grad_conv.reshape(3, 3, 128, 128),
            tail[:QUANT].T, grad_fine[None])


def solution(mesh):
    placed = (
        P("batch", "rows", "cols", None),
        P("batch", "rows", "cols", None),
        P("batch", "rows", "cols"),
        P(),
        P(),
        P(),
        P(),
        P(),
    )
    return jax.shard_map(
        body,
        mesh=mesh,
        in_specs=placed,
        out_specs=(
            P("batch", None, "rows", "cols"),
            P(),
            P(),
            P(),
            P(),
            P(),
            P(),
            P("batch", "rows", "cols", None),
        ),
        check_vma=False,
    )
```

```python
import jax
import jax.numpy as jnp
import numpy as np
from types import SimpleNamespace
from jax import lax
from jax.experimental import pallas as pl
from jax.experimental.pallas import tpu as pltpu
from jax.sharding import PartitionSpec as P

HEAD_DIM = 32
QUANT = 9
MESH = pl.DeviceIdType.MESH
F32, B16 = jnp.float32, jnp.bfloat16
DMA = pltpu.SemaphoreType.DMA
SCALE = HEAD_DIM ** (-0.5)
ROOT_2_PI = 0.7978845608028654
LIMIT = 58 * 1024 * 1024
EARLY, LATE = 512, 768


def onehot(rows, cols, pairs):
    table = np.zeros((rows, cols), np.float32)
    for row, col in pairs:
        table[row, col] = 1.0
    return jnp.asarray(table, B16)


def mid_table():
    return onehot(256, 256, [(p * 16 + r * 2 + m, r * 32 + p * 2 + m)
                             for p in range(16) for r in range(8) for m in range(2)])


def group_table():
    return onehot(256, 256, [(m * 128 + c * 8 + r, c * 16 + r * 2 + m)
                             for m in range(2) for c in range(16) for r in range(8)])


def back_table():
    pairs = []
    for r in range(8):
        for j in range(32):
            pairs.append((r * 48 + j, (1 + j // 2) * 16 + r * 2 + j % 2))
        pairs.append((r * 48 + 32, 17 * 16 + r * 2))
        pairs.append((r * 48 + 35, r * 2 + 1))
    return onehot(384, 288, pairs)


def pick_table(first):
    return onehot(16, 128, [(2 * i + s, 16 * i + first + s) for i in range(8) for s in range(2)])


def spread_table(first):
    return onehot(128, 16, [(16 * i + first + s, 2 * i + s) for i in range(8) for s in range(2)])


def bins_table():
    return onehot(48, 64, [(0, 15)] + [(1 + y, 16 + y) for y in range(32)] + [(33, 48)])


def up_table():
    return onehot(144, 48, [(p, p // 4) for p in range(144)])


def sum_table():
    return onehot(32, 128, [(p // 4, p) for p in range(128)])


def dot(a, b):
    return jnp.dot(a, b, preferred_element_type=F32)


def dot_nt(a, b):
    return lax.dot_general(a, b, (((1,), (1,)), ((), ())), preferred_element_type=F32)


def rcopy(src, dst, send, recv, to):
    return pltpu.make_async_remote_copy(src_ref=src, dst_ref=dst, send_sem=send, recv_sem=recv,
                                        device_id=to, device_id_type=MESH)


def wait_all(copies):
    for c in copies:
        c.wait()


def scatter_out(axis, count, src, got, send, recv, me):
    copies = []
    for k in range(1, count):
        p = (me + k) % count
        c = rcopy(src.at[p], got.at[me], send.at[k - 1], recv.at[k - 1], {axis: p})
        c.start()
        copies.append(c)
    return copies


def spread_out(axis, count, me, src, main, send, recv, send_x, recv_x):
    copies = []
    for k in range(1, count):
        p = (me + k) % count
        c = rcopy(src.at[p], main.at[1 + me], send.at[k - 1], recv.at[k - 1], {axis: p})
        c.start()
        copies.append(c)
    main[1 + me] = src[me]

    def after(t):
        return rcopy(src.at[t - 1], main.at[0], send_x.at[t], recv_x.at[0], {axis: t})

    def before(t):
        return rcopy(src.at[t + 1], main.at[count + 1], send_x.at[t], recv_x.at[1], {axis: t})

    @pl.when(me == count - 1)
    def _():
        for t in range(1, count - 1):
            after(t).start()
        main[0] = src[count - 2]
        main[count + 1] = jnp.zeros(main.shape[1:], B16)

    @pl.when(me == 0)
    def _():
        for t in range(1, count - 1):
            before(t).start()
        main[count + 1] = src[1]
        main[0] = jnp.zeros(main.shape[1:], B16)

    def finish():
        @pl.when(me == count - 1)
        def _():
            for t in range(1, count - 1):
                after(t).wait_send()

        @pl.when(me == 0)
        def _():
            for t in range(1, count - 1):
                before(t).wait_send()

        @pl.when((me > 0) & (me < count - 1))
        def _():
            after(1).wait_recv()
            before(1).wait_recv()

        wait_all(copies)

    return finish


def head_mask(h):
    lane = lax.broadcasted_iota(jnp.int32, (1, 128), 1)
    return jnp.where((lane >> 5) == h, 1.0, 0.0).astype(B16)


def heads_down(tile):
    return jnp.concatenate([tile * head_mask(h) for h in range(4)], axis=0)


def heads_across(tile):
    turned = tile.astype(F32).T
    line = lax.broadcasted_iota(jnp.int32, (128, 1), 0) >> 5
    return jnp.concatenate([jnp.where(line == h, turned, 0.0) for h in range(4)], axis=1).astype(B16)


def side_by_side(stack):
    return jnp.concatenate([stack[h * 128:(h + 1) * 128] for h in range(4)], axis=1)


def put(g, at, value):
    rows, cols = value.shape
    size = rows // 8
    for n in range(cols // 128):
        g[at + n * size:at + (n + 1) * size] = value[:, n * 128:(n + 1) * 128].reshape(size, 8, 128).astype(B16)


def shifted(line):
    return jnp.concatenate([pltpu.roll(line, 1, 0), line, pltpu.roll(line, 143, 0)], axis=1)


def reducer(me, units, g, out, got0, sum0, got1, sum1, got2, sum2, got3, sems):
    core, first, second, deep = me.core, me.first, me.second, me.deep
    u0, u1, u2, u3 = units // 2, units // 8, units // 32, units // 256
    s0, r0, s1, r1, s2, r2, s3, r3, as3, ar3, as2, ar2, as1, ar1, as0, ar0 = sems
    place = core * u0 + first * u1 + second * u2
    held = {}

    def sum_up(terms):
        total = terms[0].astype(F32)
        for term in terms[1:]:
            total = total + term.astype(F32)
        return total

    def near_start():
        held["near"] = []
        for n, k in enumerate((1, 2, 3, 0)):
            p = (second + k) % 4
            c = rcopy(g.at[pl.ds((1 - core) * u0 + p * u1, u1)], got0.at[p], s0.at[n], r0.at[n], me.other)
            c.start()
            held["near"].append(c)

    def first_start():
        held["first"] = []
        for n, k in enumerate((1, 2, 3)):
            p = (first + k) % 4
            held["near"][n].wait_recv()
            sum0[p] = sum_up([g[pl.ds(core * u0 + p * u1, u1)], got0[p]]).astype(B16)
            c = rcopy(sum0.at[p], got1.at[k - 1], s1.at[k - 1], r1.at[k - 1], me.in_first(k))
            c.start()
            held["first"].append(c)
        held["near"][3].wait_recv()

    def second_start():
        wait_all(held["first"])
        sum1[...] = sum_up([g[pl.ds(core * u0 + first * u1, u1)], got0[first], got1[0], got1[1], got1[2]]).astype(B16)
        held["second"] = []
        for k in (1, 2, 3):
            p = (second + k) % 4
            c = rcopy(sum1.at[pl.ds(p * u2, u2)], got2.at[k - 1], s2.at[k - 1], r2.at[k - 1], me.in_second(k))
            c.start()
            held["second"].append(c)
        for c in held["near"]:
            c.wait_send()

    def deep_start():
        wait_all(held["second"])
        sum2[...] = sum_up([sum1[pl.ds(second * u2, u2)], got2[0], got2[1], got2[2]]).astype(B16)
        held["deep"] = []
        for k in range(1, 8):
            p = (deep + k) % 8
            c = rcopy(sum2.at[pl.ds(p * u3, u3)], got3.at[k - 1], s3.at[k - 1], r3.at[k - 1], me.in_deep(k))
            c.start()
            held["deep"].append(c)

    def deep_gather():
        wait_all(held["deep"])
        mine = sum_up([sum2[pl.ds(deep * u3, u3)]] + [got3[k] for k in range(7)])
        out[pl.ds(place + deep * u3, u3)] = mine.astype(B16)
        block = out.at[pl.ds(place + deep * u3, u3)]
        held["deep"] = []
        for k in range(1, 8):
            c = rcopy(block, block, as3.at[k - 1], ar3.at[k - 1], me.in_deep(k))
            c.start()
            held["deep"].append(c)

    def second_gather():
        wait_all(held["deep"])
        block = out.at[pl.ds(place, u2)]
        held["second"] = []
        for k in (1, 2, 3):
            c = rcopy(block, block, as2.at[k - 1], ar2.at[k - 1], me.in_second(k))
            c.start()
            held["second"].append(c)

    def forward(n, p):
        block = out.at[pl.ds(core * u0 + p * u1, u1)]
        c = rcopy(block, block, as0.at[n], ar0.at[n], me.other)
        c.start()
        held["near"].append(c)

    def first_gather():
        wait_all(held["second"])
        block = out.at[pl.ds(core * u0 + first * u1, u1)]
        held["first"], held["near"] = [], []
        for k in (1, 2, 3):
            c = rcopy(block, block, as1.at[k - 1], ar1.at[k - 1], me.in_first(k))
            c.start()
            held["first"].append(c)
        forward(0, first)

    def near_gather():
        for k in (1, 2, 3):
            held["first"][k - 1].wait_recv()
            forward(k, (first + 4 - k) % 4)

    def finish():
        for c in held["first"]:
            c.wait_send()
        wait_all(held["near"])

    return [near_start, first_start, second_start, deep_start, deep_gather, second_gather, first_gather,
            near_gather, finish]


def reducer_scratch(tag, units):
    unit = (8, 128)
    u1, u2, u3 = units // 8, units // 32, units // 256
    shapes = [("g", (units,) + unit), ("got0", (4, u1) + unit), ("sum0", (4, u1) + unit), ("got1", (3, u1) + unit),
              ("sum1", (u1,) + unit), ("got2", (3, u2) + unit), ("sum2", (u2,) + unit), ("got3", (7, u3) + unit)]
    result = [(tag + name, pltpu.VMEM(shape, B16)) for name, shape in shapes]
    for n, count in enumerate((4, 4, 3, 3, 3, 3, 7, 7, 7, 7, 3, 3, 3, 3, 4, 4)):
        result.append((tag + "sem" + str(n), DMA((count,))))
    return result


INPUTS = ("coarse", "fine", "bins", "w_qkv_in", "w_out_in", "w_up", "w_conv_in", "w_head",
          "mid", "group", "ungroup", "back", "pick_lo", "pick_hi", "spread_lo", "spread_hi", "place", "up", "fold", "eye")
IN_HBM = ("coarse", "fine", "w_qkv_in", "w_out_in", "w_conv_in")
OUTPUTS = (("quantiles", (9, 32, 128), F32), ("grad_fine", (32, 128, 128), F32),
           ("early", (EARLY, 8, 128), B16), ("late", (LATE, 8, 128), B16))


def scratch():
    buffers = [
        ("w_qkv", (512, 1536), B16), ("w_out", (512, 512), B16), ("w_conv", (3, 3, 128, 128), B16),
        ("got", (8, 32, 512), B16), ("turned", (16, 16, 512), B16), ("tokens", (16, 16, 512), B16),
        ("field", (40, 144, 128), B16), ("bins16", (32, 128), B16), ("bin_got", (64, 128), B16),
        ("edge_out", (2, 5, 16, 128), B16), ("edge_in", (2, 5, 16, 128), B16), ("bin_out", (2, 48, 128), B16),
        ("bin_in", (2, 48, 128), B16), ("rain", (48, 128), F32), ("edge_bins", (16, 128), F32),
        ("tok", (256, 512), B16), ("qkv", (256, 1536), B16), ("prob", (8, 512, 128), F32), ("mixed", (256, 512), B16),
        ("context", (256, 512), B16), ("raised", (16, 16, 128), B16),
        ("slots", (18, 16, 128), B16), ("lift_turned", (8, 48, 128), B16), ("lifted", (10, 48, 128), B16),
        ("query_turned", (8, 128, 512), B16), ("tok_turned", (512, 256), B16), ("mixed_turned", (512, 256), B16),
        ("context_turned", (512, 256), B16),
        ("hidden", (40, 144, 128), F32), ("slope", (40, 128, 128), F32), ("active", (40, 144, 384), B16),
        ("outer", (36, 144, 128), B16), ("out_grad", (36, 128, 128), F32), ("out_wide", (36, 144, 384), B16),
        ("out_turned", (36, 128, 128), B16), ("kernel_sum", (3, 128, 384), F32), ("loss_sum", (16, 128), F32),
        ("head_sum", (16, 128), F32), ("dlift", (8, 32, 128), B16),
        ("fold_got", (8, 32, 128), B16), ("fold_turned", (16, 16, 128), B16), ("folded", (16, 16, 128), B16),
        ("dquery", (256, 512), B16), ("dkey", (512, 256), B16), ("dvalue", (512, 256), B16),
    ]
    sems = [("s_l", 6), ("s_tr", 7), ("r_tr", 7), ("s_tc", 15), ("r_tc", 15), ("s_h", 4), ("r_h", 4), ("s_e", 4), ("r_e", 4),
            ("s_lc", 15), ("r_lc", 15), ("s_lx", 16), ("r_lx", 2), ("s_lr", 7), ("r_lr", 7), ("s_ly", 8), ("r_ly", 2),
            ("s_fr", 7), ("r_fr", 7), ("s_fc", 15), ("r_fc", 15)]
    return ([(name, pltpu.VMEM(shape, dtype)) for name, shape, dtype in buffers]
            + [(name, DMA((count,))) for name, count in sems]
            + reducer_scratch("a_", EARLY) + reducer_scratch("b_", LATE))


def halo_rows(v, row):
    sends = [
        ((v.fine.at[pl.ds(30, 2)], v.field.at[pl.ds(2, 2), pl.ds(0, 128)], v.s_h.at[0], v.r_h.at[0]),
         (v.bins16.at[pl.ds(16, 16)], v.bin_got.at[pl.ds(0, 16)], v.s_h.at[1], v.r_h.at[1])),
        ((v.fine.at[pl.ds(0, 2)], v.field.at[pl.ds(36, 2), pl.ds(0, 128)], v.s_h.at[2], v.r_h.at[2]),
         (v.bins16.at[pl.ds(0, 16)], v.bin_got.at[pl.ds(48, 16)], v.s_h.at[3], v.r_h.at[3])),
    ]

    def start():
        @pl.when(row < 7)
        def _():
            for args in sends[0]:
                rcopy(*args, {"rows": row + 1}).start()

        @pl.when(row > 0)
        def _():
            for args in sends[1]:
                rcopy(*args, {"rows": row - 1}).start()

    def finish():
        @pl.when(row < 7)
        def _():
            for args in sends[0]:
                rcopy(*args, {"rows": row + 1}).wait_send()
            for args in sends[1]:
                rcopy(*args, {"rows": row + 1}).wait_recv()

        @pl.when(row > 0)
        def _():
            for args in sends[1]:
                rcopy(*args, {"rows": row - 1}).wait_send()
            for args in sends[0]:
                rcopy(*args, {"rows": row - 1}).wait_recv()

    return start, finish


def halo_cols(v, col):
    sends = [((v.edge_out.at[n], v.edge_in.at[n], v.s_e.at[2 * n], v.r_e.at[2 * n]),
              (v.bin_out.at[n], v.bin_in.at[n], v.s_e.at[2 * n + 1], v.r_e.at[2 * n + 1])) for n in range(2)]

    def start():
        @pl.when(col < 15)
        def _():
            for args in sends[0]:
                rcopy(*args, {"cols": col + 1}).start()

        @pl.when(col > 0)
        def _():
            for args in sends[1]:
                rcopy(*args, {"cols": col - 1}).start()

    def finish():
        @pl.when(col < 15)
        def _():
            for args in sends[0]:
                rcopy(*args, {"cols": col + 1}).wait_send()
            for args in sends[1]:
                rcopy(*args, {"cols": col + 1}).wait_recv()

        @pl.when(col > 0)
        def _():
            for args in sends[1]:
                rcopy(*args, {"cols": col - 1}).wait_send()
            for args in sends[0]:
                rcopy(*args, {"cols": col - 1}).wait_recv()

    return start, finish


def exchange_tokens(v, row, col, loads):
    sends = scatter_out("rows", 8, v.coarse, v.got, v.s_tr, v.r_tr, row)
    own = pltpu.make_async_copy(v.coarse.at[row], v.got.at[row], v.s_l.at[0])
    own.start()
    v.bins16[...] = v.bins[...].astype(F32).astype(B16)
    rows_start, rows_finish = halo_rows(v, row)
    rows_start()
    for c in loads:
        c.start()

    @pl.when(row == 0)
    def _():
        v.field[pl.ds(2, 2), :128] = jnp.zeros((2, 128, 128), B16)
        v.bin_got[pl.ds(0, 16)] = jnp.zeros((16, 128), B16)

    @pl.when(row == 7)
    def _():
        v.field[pl.ds(36, 2), :128] = jnp.zeros((2, 128, 128), B16)
        v.bin_got[pl.ds(48, 16)] = jnp.zeros((16, 128), B16)

    v.field[pl.ds(0, 2), :128] = jnp.zeros((2, 128, 128), B16)
    v.field[pl.ds(38, 2), :128] = jnp.zeros((2, 128, 128), B16)
    v.bin_got[pl.ds(16, 32)] = v.bins16[...]

    own.wait()
    wait_all(sends)
    v.turned[...] = dot(v.mid[...], v.got[...].reshape(256, 512)).astype(B16).reshape(16, 16, 512)
    sends = scatter_out("cols", 16, v.turned, v.tokens, v.s_tc, v.r_tc, col)
    v.tokens[col] = v.turned[col]

    loads[0].wait()
    rows_finish()
    rows = dot(v.place[...], v.bin_got[...])
    v.rain[...] = rows
    v.bin_out[0] = jnp.broadcast_to(rows[:, 127:128], (48, 128)).astype(B16)
    v.bin_out[1] = jnp.broadcast_to(rows[:, 0:1], (48, 128)).astype(B16)
    for q in range(5):
        v.edge_out[0, q] = dot(v.pick_hi[...], v.field[8 * q:8 * q + 8, 112:128].reshape(128, 128)).astype(B16)
        v.edge_out[1, q] = dot(v.pick_lo[...], v.field[8 * q:8 * q + 8, 0:16].reshape(128, 128)).astype(B16)
    cols_start, cols_finish = halo_cols(v, col)
    cols_start()

    @pl.when(col == 0)
    def _():
        v.edge_in[0] = jnp.zeros((5, 16, 128), B16)
        v.bin_in[0] = jnp.zeros((48, 128), B16)

    @pl.when(col == 15)
    def _():
        v.edge_in[1] = jnp.zeros((5, 16, 128), B16)
        v.bin_in[1] = jnp.zeros((48, 128), B16)

    wait_all(sends)
    return cols_finish


def attend(v):
    v.tok[...] = dot(v.group[...], v.tokens[...].reshape(256, 512)).astype(B16)
    for n in range(3):
        v.qkv[:, n * 512:(n + 1) * 512] = dot(v.tok[...], v.w_qkv[:, n * 512:(n + 1) * 512]).astype(B16)
    for g in range(2):
        for t in range(4):
            rows, at = slice(g * 128, g * 128 + 128), t * 128
            query = v.qkv[rows, at:at + 128]
            keyed = v.qkv[rows, 512 + at:512 + at + 128]
            valued = v.qkv[rows, 1024 + at:1024 + at + 128]
            scores = dot_nt(heads_down(query), keyed) * SCALE
            peak = jnp.max(scores, axis=-1, keepdims=True)
            powers = jnp.exp(scores - peak)
            share = powers / jnp.sum(powers, axis=-1, keepdims=True)
            v.prob[g * 4 + t] = share
            v.mixed[rows, at:at + 128] = dot(side_by_side(share.astype(B16)), heads_down(valued)).astype(B16)
    attended = dot(v.mixed[...], v.w_out[...]).astype(B16)
    v.context[...] = (v.tok[...].astype(F32) + attended.astype(F32)).astype(B16)
    lifted = dot(v.context[...], v.w_up[...]).astype(B16)
    v.raised[...] = dot(v.ungroup[...], lifted).astype(B16).reshape(16, 16, 128)


def edge_targets(v):
    lane = lax.broadcasted_iota(jnp.int32, (48, 128), 1)
    line = lax.broadcasted_iota(jnp.int32, (48, 128), 0)
    low, high = v.bin_in[0].astype(F32), v.bin_in[1].astype(F32)
    picked = jnp.where((lane & 15) == 0, high, jnp.where((lane & 15) == 15, low, 0.0))
    for b in range(9):
        here = line == 4 * b + (lane >> 4)
        v.edge_bins[b:b + 1] = jnp.sum(jnp.where(here, picked, 0.0), axis=0, keepdims=True)


def convolve(v, row, col):
    head_t = dot_nt(v.eye[...], v.w_head[...]).astype(B16)
    head = dot_nt(v.w_head[...], v.eye[...]).astype(B16)
    place = lax.broadcasted_iota(jnp.int32, (144, 1), 0)
    right = jnp.where(col < 15, 130, 128)
    left = jnp.where(col > 0, 142, 144)
    inside = (place < right) | (place >= left)
    level = (lax.broadcasted_iota(jnp.int32, (16, 1), 0) + 1).astype(F32) / 10.0
    quant = lax.broadcasted_iota(jnp.int32, (16, 1), 0) < QUANT
    v.loss_sum[...] = jnp.zeros((16, 128), F32)
    v.head_sum[...] = jnp.zeros((16, 128), F32)

    def start(i):
        raised = dot(v.up[...], v.lifted[i])
        for s in range(4):
            y = 4 * i + s - 4
            x = v.field[4 * i + s].astype(F32) + raised
            square = x * x
            bend = jnp.tanh(ROOT_2_PI * x * (1.0 + 0.044715 * square))
            half = 0.5 * (1.0 + bend)
            seen = (row * 32 + y >= 0) & (row * 32 + y < 256)
            act = jnp.where(inside & seen, x * half, 0.0)
            v.hidden[4 * i + s] = x
            v.active[4 * i + s] = shifted(act).astype(B16)
            v.slope[4 * i + s] = half[:128] + (0.5 * ROOT_2_PI) * x[:128] * (1.0 - bend[:128] * bend[:128]) * (
                1.0 + (3 * 0.044715) * square[:128])

    def forward(i):
        total = v.hidden[pl.ds(4 * i + 3, 4)].reshape(576, 128)
        for a in range(3):
            window = v.active[pl.ds(4 * i + 2 + a, 4)].reshape(576, 384)
            total = total + dot(window, v.w_conv[a].reshape(384, 128))
        v.outer[pl.ds(4 * i, 4)] = total.astype(B16).reshape(4, 144, 128)

    def turn(i):
        own = v.outer[pl.ds(4 * i, 4), :128].reshape(512, 128)
        edge = v.outer[pl.ds(4 * i, 4), 128:144].reshape(64, 128)
        pixels = jnp.concatenate([own, edge, jnp.zeros((64, 128), B16)], axis=0)
        predicted = dot_nt(head_t, pixels)
        lines = [v.rain[pl.ds(4 * i + s, 1), :] for s in range(4)] + [v.edge_bins[pl.ds(i, 1), :]]
        target = jnp.concatenate(lines, axis=1) * (1.0 / 16.0) - 1.0
        lane = lax.broadcasted_iota(jnp.int32, (1, 640), 1)
        spot = lane - 512
        inner = lane < 512
        y = 4 * i - 1 + jnp.where(inner, lane >> 7, spot >> 4)
        side = (((spot & 15) == 0) & (col < 15)) | (((spot & 15) == 15) & (col > 0))
        seen = (row * 32 + y >= 0) & (row * 32 + y < 256) & (y < 33) & (inner | (side & (spot < 64)))
        mine = inner & (y >= 0) & (y < 32)
        error = target - predicted
        weight = jnp.where(error < 0.0, 1.0 - level, level)
        down = jnp.where(seen & quant, -weight * jnp.clip(error, -1.0, 1.0) * (1.0 / 1024.0), 0.0)
        size = jnp.abs(error)
        loss = weight * jnp.where(size <= 1.0, 0.5 * error * error, size - 0.5)
        loss = jnp.where(mine & quant, loss, 0.0)
        v.loss_sum[...] += loss[:, :128] + loss[:, 128:256] + loss[:, 256:384] + loss[:, 384:512]
        down_b = down.astype(B16)
        v.head_sum[...] += dot(jnp.where(mine, down, 0.0).astype(B16)[:, :512], own)
        across = dot(head, down_b[:, :512]).astype(B16)
        along = dot(down.T.astype(B16), head_t)
        for s in range(4):
            row_y = 4 * i + s - 1
            value = predicted[:, s * 128:(s + 1) * 128]

            def keep():
                for q in range(QUANT):
                    v.quantiles[q, pl.ds(row_y, 1), :] = value[q:q + 1]

            if isinstance(i, int):
                if 0 <= row_y < 32:
                    keep()
            else:
                keep()
            v.out_turned[4 * i + s] = across[:, s * 128:(s + 1) * 128]
            mid_part = along[s * 128:(s + 1) * 128]
            v.out_grad[4 * i + s] = mid_part
            full = jnp.concatenate([mid_part, along[512 + s * 16:528 + s * 16]], axis=0)
            v.out_wide[4 * i + s] = shifted(full).astype(B16)

    def back(i):
        total = None
        for a in range(3):
            window = v.out_wide[pl.ds(4 * i + a, 4), :128].reshape(512, 384)
            turned = jnp.concatenate([v.w_conv[2 - a, 2 - b] for b in range(3)], axis=1)
            part = dot_nt(window, turned)
            total = part if total is None else total + part
        dhidden = v.out_grad[pl.ds(4 * i + 1, 4)] + v.slope[pl.ds(4 * i + 4, 4)] * total.reshape(4, 128, 128)
        v.grad_fine[pl.ds(4 * i, 4)] = dhidden * 1024.0
        summed = dhidden[0] + dhidden[1] + dhidden[2] + dhidden[3]
        high = summed.astype(B16)
        low = (summed - high.astype(F32)).astype(B16)
        v.dlift[i] = (dot(v.fold[...], high) + dot(v.fold[...], low)).astype(B16)

    def step(t):
        known = isinstance(t, int)
        if not known or 0 <= t - 5 <= 7:
            back(t - 5)
        if not known or 0 <= t - 3 <= 8:
            turn(t - 3)
        if not known or 0 <= t - 2 <= 8:
            forward(t - 2)
        if not known or t <= 9:
            start(t)

    for t in range(5):
        step(t)

    def loop(t, carry):
        step(t)
        return carry

    lax.fori_loop(5, 10, loop, 0)
    for t in range(10, 13):
        step(t)


def kernel_terms(v, low, high):
    def one(i, carry):
        across = jnp.concatenate([v.out_turned[4 * i + 1 + s] for s in range(4)], axis=1)
        for a in range(3):
            window = v.active[pl.ds(4 * i + 3 + a, 4), :128].reshape(512, 384)
            v.kernel_sum[a] += dot(across, window)
        return carry

    lax.fori_loop(low, high, one, 0)


def local_units(v):
    for a in range(3):
        for b in range(3):
            at = 320 + a * 48 + b * 16
            v.a_g[at:at + 16] = v.kernel_sum[a, :, b * 128:(b + 1) * 128].T.reshape(16, 8, 128).astype(B16)
    spot = lax.broadcasted_iota(jnp.int32, (16, 1), 0)
    total = jnp.sum(v.loss_sum[...], axis=0, keepdims=True)
    tail = jnp.where(spot < QUANT, v.head_sum[...], jnp.where(spot == QUANT, total, 0.0))
    v.a_g[464:466] = tail.reshape(2, 8, 128).astype(B16)
    v.a_g[466:EARLY] = jnp.zeros((EARLY - 466, 8, 128), B16)


def attend_back(v, mix_grad, s):
    for t in range(4):
        rows, at = slice(s * 128, s * 128 + 128), t * 128
        keyed = v.qkv[rows, 512 + at:512 + at + 128]
        valued = v.qkv[rows, 1024 + at:1024 + at + 128]
        mine = mix_grad[rows, at:at + 128]
        dprob = dot_nt(heads_down(mine), valued)
        share = v.prob[s * 4 + t]
        inner = jnp.sum(share * dprob, axis=-1, keepdims=True)
        dscore = (share * (dprob - inner) * SCALE).astype(B16)
        v.dquery[rows, at:at + 128] = dot(side_by_side(dscore), heads_down(keyed)).astype(B16)
        v.dkey[at:at + 128, rows] = dot(v.query_turned[s * 4 + t], dscore).astype(B16)
        v.dvalue[at:at + 128, rows] = dot(heads_across(mine), share.astype(B16)).astype(B16)


def whole_kernel(names, *refs):
    v = SimpleNamespace(**dict(zip(names, refs)))
    row, col, batch = lax.axis_index("rows"), lax.axis_index("cols"), lax.axis_index("batch")
    core, deep = row % 2, (row // 2) * 2 + batch
    x, y = col // 4, col % 4
    me = SimpleNamespace(
        core=core, deep=deep, other={"rows": row + 1 - 2 * core},
        first=x * (1 - core) + y * core, second=y * (1 - core) + x * core,
    )

    def in_first(k):
        p = (me.first + k) % 4
        return {"cols": (p * 4 + y) * (1 - core) + (x * 4 + p) * core}

    def in_second(k):
        p = (me.second + k) % 4
        return {"cols": (x * 4 + p) * (1 - core) + (p * 4 + y) * core}

    def in_deep(k):
        p = (deep + k) % 8
        return {"rows": (p // 2) * 2 + core, "batch": p % 2}

    me.in_first, me.in_second, me.in_deep = in_first, in_second, in_deep

    peers = [{"rows": (row + k) % 8} for k in range(1, 8)] + [{"cols": (col + k) % 16} for k in range(1, 16)]
    peers += [{"rows": (row + 2 * k) % 8, "batch": 1 - batch} for k in range(4)]
    barrier = pltpu.get_barrier_semaphore()
    for peer in peers:
        pl.semaphore_signal(barrier, inc=1, device_id=peer, device_id_type=MESH)
    pl.semaphore_wait(barrier, len(peers))

    loads = [pltpu.make_async_copy(v.fine, v.field.at[pl.ds(4, 32), pl.ds(0, 128)], v.s_l.at[1]),
             pltpu.make_async_copy(v.w_qkv_in, v.w_qkv, v.s_l.at[2]),
             pltpu.make_async_copy(v.w_out_in, v.w_out, v.s_l.at[3]),
             pltpu.make_async_copy(v.w_conv_in, v.w_conv, v.s_l.at[4])]
    cols_finish = exchange_tokens(v, row, col, loads)
    loads[1].wait()
    loads[2].wait()
    attend(v)

    finish = spread_out("cols", 16, col, v.raised, v.slots, v.s_lc, v.r_lc, v.s_lx, v.r_lx)
    cols_finish()
    for q in range(5):
        edge = dot(v.spread_hi[...], v.edge_in[0, q]) + dot(v.spread_lo[...], v.edge_in[1, q])
        v.field[8 * q:8 * q + 8, 128:144] = edge.astype(B16).reshape(8, 16, 128)
    edge_targets(v)
    for s in range(2):
        for t in range(4):
            v.query_turned[s * 4 + t] = heads_across(v.qkv[s * 128:s * 128 + 128, t * 128:t * 128 + 128])
    finish()
    v.lift_turned[...] = dot(v.back[...], v.slots[...].reshape(288, 128)).astype(B16).reshape(8, 48, 128)
    finish = spread_out("rows", 8, row, v.lift_turned, v.lifted, v.s_lr, v.r_lr, v.s_ly, v.r_ly)
    v.tok_turned[...] = v.tok[...].astype(F32).T.astype(B16)
    v.mixed_turned[...] = v.mixed[...].astype(F32).T.astype(B16)
    v.context_turned[...] = v.context[...].astype(F32).T.astype(B16)
    v.kernel_sum[...] = jnp.zeros((3, 128, 384), F32)
    loads[3].wait()
    finish()

    convolve(v, row, col)

    sends = scatter_out("rows", 8, v.dlift, v.fold_got, v.s_fr, v.r_fr, row)
    v.fold_got[row] = v.dlift[row]
    kernel_terms(v, 0, 4)
    wait_all(sends)
    v.fold_turned[...] = dot(v.mid[...], v.fold_got[...].reshape(256, 128)).astype(B16).reshape(16, 16, 128)
    sends = scatter_out("cols", 16, v.fold_turned, v.folded, v.s_fc, v.r_fc, col)
    v.folded[col] = v.fold_turned[col]
    kernel_terms(v, 4, 8)
    local_units(v)
    wait_all(sends)

    early = reducer(me, EARLY, v.a_g, v.early, v.a_got0, v.a_sum0, v.a_got1, v.a_sum1, v.a_got2, v.a_sum2, v.a_got3,
                    [getattr(v, "a_sem" + str(n)) for n in range(16)])
    late = reducer(me, LATE, v.b_g, v.late, v.b_got0, v.b_sum0, v.b_got1, v.b_sum1, v.b_got2, v.b_sum2, v.b_got3,
                   [getattr(v, "b_sem" + str(n)) for n in range(16)])
    lift = dot(v.group[...], v.folded[...].reshape(256, 128)).astype(B16)
    dcontext = dot_nt(lift, v.w_up[...]).astype(B16)
    put(v.a_g, 0, dot(v.mixed_turned[...], dcontext))
    put(v.a_g, 256, dot(v.context_turned[...], lift))
    early[0]()
    mix_grad = dot_nt(dcontext, v.w_out[...]).astype(B16)
    attend_back(v, mix_grad, 0)
    early[1]()
    attend_back(v, mix_grad, 1)
    early[2]()
    put(v.b_g, 0, dot(v.tok_turned[...], v.dquery[...]))
    put(v.b_g, 256, dot_nt(v.tok_turned[...], v.dkey[...]))
    put(v.b_g, 512, dot_nt(v.tok_turned[...], v.dvalue[...]))
    late[0]()
    early[3]()
    late[1]()
    early[4]()
    late[2]()
    early[5]()
    late[3]()
    early[6]()
    late[4]()
    early[7]()
    late[5]()
    early[8]()
    for step in late[6:]:
        step()


def unpack_kernel(early, late, grad_qkv, grad_out, grad_up, grad_conv, grad_head, loss):
    for n in range(12):
        grad_qkv[:, n * 128:(n + 1) * 128] = late[n * 64:(n + 1) * 64].astype(F32).reshape(512, 128)
    for n in range(4):
        grad_out[:, n * 128:(n + 1) * 128] = early[n * 64:(n + 1) * 64].astype(F32).reshape(512, 128)
    grad_up[...] = early[256:320].astype(F32).reshape(512, 128)
    grad_conv[...] = early[320:464].astype(F32).reshape(1152, 128)
    tail = early[464:466].astype(F32).reshape(16, 128)
    grad_head[...] = tail.T[:, :QUANT]
    loss[...] = jnp.sum(tail[QUANT:QUANT + 1], axis=1, keepdims=True) * (1.0 / (1048576.0 * QUANT))


def body(fine_input, coarse, rain_bins, w_qkv, w_out, w_up, w_conv, w_head):
    group = group_table()
    eye = onehot(16, QUANT, [(q, q) for q in range(QUANT)])
    args = [coarse[0], fine_input[0], rain_bins[0], w_qkv, w_out, w_up, w_conv, w_head,
            mid_table(), group, group.T, back_table(), pick_table(0), pick_table(14), spread_table(0), spread_table(14),
            bins_table(), up_table(), sum_table(), eye]
    spaces = scratch()
    names = INPUTS + tuple(name for name, _, _ in OUTPUTS) + tuple(name for name, _ in spaces)
    vmem = pl.BlockSpec(memory_space=pltpu.VMEM)

    def kernel(*refs):
        whole_kernel(names, *refs)

    quantiles, grad_fine, early, late = pl.pallas_call(
        kernel,
        out_shape=[jax.ShapeDtypeStruct(shape, dtype) for _, shape, dtype in OUTPUTS],
        in_specs=[pl.BlockSpec(memory_space=pl.ANY) if name in IN_HBM else vmem for name in INPUTS],
        out_specs=[vmem] * len(OUTPUTS),
        scratch_shapes=[space for _, space in spaces],
        compiler_params=pltpu.CompilerParams(vmem_limit_bytes=LIMIT, collective_id=1, has_side_effects=True),
    )(*args)
    grad_qkv, grad_out, grad_up, grad_conv, grad_head, loss = pl.pallas_call(
        unpack_kernel,
        out_shape=[jax.ShapeDtypeStruct(shape, F32)
                   for shape in ((512, 1536), (512, 512), (512, 128), (1152, 128), (128, QUANT), (1, 1))],
        in_specs=[vmem] * 2,
        out_specs=[vmem] * 6,
        compiler_params=pltpu.CompilerParams(vmem_limit_bytes=LIMIT),
    )(early, late)
    return (quantiles[None], loss.reshape(()), grad_qkv, grad_out, grad_up, grad_conv.reshape(3, 3, 128, 128),
            grad_head, grad_fine[None])


def solution(mesh):
    placed = (
        P("batch", "rows", "cols", None),
        P("batch", "rows", "cols", None),
        P("batch", "rows", "cols"),
        P(),
        P(),
        P(),
        P(),
        P(),
    )
    return jax.shard_map(
        body,
        mesh=mesh,
        in_specs=placed,
        out_specs=(
            P("batch", None, "rows", "cols"),
            P(),
            P(),
            P(),
            P(),
            P(),
            P(),
            P("batch", "rows", "cols", None),
        ),
        check_vma=False,
    )
```

```python
import jax
import jax.numpy as jnp
import numpy as np
from types import SimpleNamespace
from jax import lax
from jax.experimental import pallas as pl
from jax.experimental.pallas import tpu as pltpu
from jax.sharding import PartitionSpec as P

HEAD_DIM = 32
QUANT = 9
MESH = pl.DeviceIdType.MESH
F32, B16 = jnp.float32, jnp.bfloat16
DMA = pltpu.SemaphoreType.DMA
SCALE = HEAD_DIM ** (-0.5)
ROOT_2_PI = 0.7978845608028654
LIMIT = 58 * 1024 * 1024
EARLY, LATE = 256, 768


def onehot(rows, cols, pairs):
    table = np.zeros((rows, cols), np.float32)
    for row, col in pairs:
        table[row, col] = 1.0
    return jnp.asarray(table, B16)


def mid_table():
    return onehot(256, 256, [(p * 16 + r * 2 + m, r * 32 + p * 2 + m)
                             for p in range(16) for r in range(8) for m in range(2)])


def group_table():
    return onehot(256, 256, [(m * 128 + c * 8 + r, c * 16 + r * 2 + m)
                             for m in range(2) for c in range(16) for r in range(8)])


def back_table():
    pairs = []
    for r in range(8):
        for j in range(32):
            pairs.append((r * 48 + j, (1 + j // 2) * 16 + r * 2 + j % 2))
        pairs.append((r * 48 + 32, 17 * 16 + r * 2))
        pairs.append((r * 48 + 35, r * 2 + 1))
    return onehot(384, 288, pairs)


def pick_table(first):
    return onehot(16, 128, [(2 * i + s, 16 * i + first + s) for i in range(8) for s in range(2)])


def spread_table(first):
    return onehot(128, 16, [(16 * i + first + s, 2 * i + s) for i in range(8) for s in range(2)])


def bins_table():
    return onehot(48, 64, [(0, 15)] + [(1 + y, 16 + y) for y in range(32)] + [(33, 48)])


def up_table():
    return onehot(144, 48, [(p, p // 4) for p in range(144)])


def sum_table():
    return onehot(32, 128, [(p // 4, p) for p in range(128)])


def dot(a, b):
    return jnp.dot(a, b, preferred_element_type=F32)


def dot_nt(a, b):
    return lax.dot_general(a, b, (((1,), (1,)), ((), ())), preferred_element_type=F32)


def rcopy(src, dst, send, recv, to):
    return pltpu.make_async_remote_copy(src_ref=src, dst_ref=dst, send_sem=send, recv_sem=recv,
                                        device_id=to, device_id_type=MESH)


def wait_all(copies):
    for c in copies:
        c.wait()


def scatter_out(axis, count, src, got, send, recv, me):
    copies = []
    for k in range(1, count):
        p = (me + k) % count
        c = rcopy(src.at[p], got.at[me], send.at[k - 1], recv.at[k - 1], {axis: p})
        c.start()
        copies.append(c)
    return copies


def spread_out(axis, count, me, src, main, send, recv, send_x, recv_x):
    copies = []
    for k in range(1, count):
        p = (me + k) % count
        c = rcopy(src.at[p], main.at[1 + me], send.at[k - 1], recv.at[k - 1], {axis: p})
        c.start()
        copies.append(c)
    main[1 + me] = src[me]

    def after(t):
        return rcopy(src.at[t - 1], main.at[0], send_x.at[t], recv_x.at[0], {axis: t})

    def before(t):
        return rcopy(src.at[t + 1], main.at[count + 1], send_x.at[t], recv_x.at[1], {axis: t})

    @pl.when(me == count - 1)
    def _():
        for t in range(1, count - 1):
            after(t).start()
        main[0] = src[count - 2]
        main[count + 1] = jnp.zeros(main.shape[1:], B16)

    @pl.when(me == 0)
    def _():
        for t in range(1, count - 1):
            before(t).start()
        main[count + 1] = src[1]
        main[0] = jnp.zeros(main.shape[1:], B16)

    def finish():
        @pl.when(me == count - 1)
        def _():
            for t in range(1, count - 1):
                after(t).wait_send()

        @pl.when(me == 0)
        def _():
            for t in range(1, count - 1):
                before(t).wait_send()

        @pl.when((me > 0) & (me < count - 1))
        def _():
            after(1).wait_recv()
            before(1).wait_recv()

        wait_all(copies)

    return finish


def head_mask(h):
    lane = lax.broadcasted_iota(jnp.int32, (1, 128), 1)
    return jnp.where((lane >> 5) == h, 1.0, 0.0).astype(B16)


def heads_down(tile):
    return jnp.concatenate([tile * head_mask(h) for h in range(4)], axis=0)


def heads_across(tile):
    turned = tile.astype(F32).T
    line = lax.broadcasted_iota(jnp.int32, (128, 1), 0) >> 5
    return jnp.concatenate([jnp.where(line == h, turned, 0.0) for h in range(4)], axis=1).astype(B16)


def side_by_side(stack):
    return jnp.concatenate([stack[h * 128:(h + 1) * 128] for h in range(4)], axis=1)


def put(g, at, value):
    rows, cols = value.shape
    size = rows // 8
    for n in range(cols // 128):
        g[at + n * size:at + (n + 1) * size] = value[:, n * 128:(n + 1) * 128].reshape(size, 8, 128).astype(B16)


def shifted(line):
    return jnp.concatenate([pltpu.roll(line, 1, 0), line, pltpu.roll(line, 143, 0)], axis=1)


def reducer(me, units, g, out, got0, sum0, got1, sum1, got2, sum2, got3, sems):
    core, first, second, deep = me.core, me.first, me.second, me.deep
    u0, u1, u2, u3 = units // 2, units // 8, units // 32, units // 256
    s0, r0, s1, r1, s2, r2, s3, r3, as3, ar3, as2, ar2, as1, ar1, as0, ar0 = sems
    place = core * u0 + first * u1 + second * u2
    held = {}

    def sum_up(terms):
        total = terms[0].astype(F32)
        for term in terms[1:]:
            total = total + term.astype(F32)
        return total

    def near_start():
        held["near"] = []
        for n, k in enumerate((1, 2, 3, 0)):
            p = (second + k) % 4
            c = rcopy(g.at[pl.ds((1 - core) * u0 + p * u1, u1)], got0.at[p], s0.at[n], r0.at[n], me.other)
            c.start()
            held["near"].append(c)

    def first_start():
        held["first"] = []
        for n, k in enumerate((1, 2, 3)):
            p = (first + k) % 4
            held["near"][n].wait_recv()
            sum0[p] = sum_up([g[pl.ds(core * u0 + p * u1, u1)], got0[p]]).astype(B16)
            c = rcopy(sum0.at[p], got1.at[k - 1], s1.at[k - 1], r1.at[k - 1], me.in_first(k))
            c.start()
            held["first"].append(c)
        held["near"][3].wait_recv()

    def second_start():
        wait_all(held["first"])
        sum1[...] = sum_up([g[pl.ds(core * u0 + first * u1, u1)], got0[first], got1[0], got1[1], got1[2]]).astype(B16)
        held["second"] = []
        for k in (1, 2, 3):
            p = (second + k) % 4
            c = rcopy(sum1.at[pl.ds(p * u2, u2)], got2.at[k - 1], s2.at[k - 1], r2.at[k - 1], me.in_second(k))
            c.start()
            held["second"].append(c)
        for c in held["near"]:
            c.wait_send()

    def deep_start():
        wait_all(held["second"])
        sum2[...] = sum_up([sum1[pl.ds(second * u2, u2)], got2[0], got2[1], got2[2]]).astype(B16)
        held["deep"] = []
        for k in range(1, 8):
            p = (deep + k) % 8
            c = rcopy(sum2.at[pl.ds(p * u3, u3)], got3.at[k - 1], s3.at[k - 1], r3.at[k - 1], me.in_deep(k))
            c.start()
            held["deep"].append(c)

    def deep_gather():
        wait_all(held["deep"])
        mine = sum_up([sum2[pl.ds(deep * u3, u3)]] + [got3[k] for k in range(7)])
        out[pl.ds(place + deep * u3, u3)] = mine.astype(B16)
        block = out.at[pl.ds(place + deep * u3, u3)]
        held["deep"] = []
        for k in range(1, 8):
            c = rcopy(block, block, as3.at[k - 1], ar3.at[k - 1], me.in_deep(k))
            c.start()
            held["deep"].append(c)

    def second_gather():
        wait_all(held["deep"])
        block = out.at[pl.ds(place, u2)]
        held["second"] = []
        for k in (1, 2, 3):
            c = rcopy(block, block, as2.at[k - 1], ar2.at[k - 1], me.in_second(k))
            c.start()
            held["second"].append(c)

    def forward(n, p):
        block = out.at[pl.ds(core * u0 + p * u1, u1)]
        c = rcopy(block, block, as0.at[n], ar0.at[n], me.other)
        c.start()
        held["near"].append(c)

    def first_gather():
        wait_all(held["second"])
        block = out.at[pl.ds(core * u0 + first * u1, u1)]
        held["first"], held["near"] = [], []
        for k in (1, 2, 3):
            c = rcopy(block, block, as1.at[k - 1], ar1.at[k - 1], me.in_first(k))
            c.start()
            held["first"].append(c)
        forward(0, first)

    def near_gather():
        for k in (1, 2, 3):
            held["first"][k - 1].wait_recv()
            forward(k, (first + 4 - k) % 4)

    def finish():
        for c in held["first"]:
            c.wait_send()
        wait_all(held["near"])

    return [near_start, first_start, second_start, deep_start, deep_gather, second_gather, first_gather,
            near_gather, finish]


def reducer_scratch(tag, units):
    unit = (8, 128)
    u1, u2, u3 = units // 8, units // 32, units // 256
    shapes = [("g", (units,) + unit), ("got0", (4, u1) + unit), ("sum0", (4, u1) + unit), ("got1", (3, u1) + unit),
              ("sum1", (u1,) + unit), ("got2", (3, u2) + unit), ("sum2", (u2,) + unit), ("got3", (7, u3) + unit)]
    result = [(tag + name, pltpu.VMEM(shape, B16)) for name, shape in shapes]
    for n, count in enumerate((4, 4, 3, 3, 3, 3, 7, 7, 7, 7, 3, 3, 3, 3, 4, 4)):
        result.append((tag + "sem" + str(n), DMA((count,))))
    return result


INPUTS = ("coarse", "fine", "bins", "w_qkv_in", "w_out_in", "w_up", "w_conv_in", "w_head_t",
          "mid", "group", "ungroup", "back", "pick_lo", "pick_hi", "spread_lo", "spread_hi", "place", "up", "fold", "eye")
IN_HBM = ("coarse", "fine", "w_qkv_in", "w_out_in", "w_conv_in")
OUTPUTS = (("quantiles_out", (9, 32, 128), F32), ("grad_fine_out", (32, 128, 128), F32),
           ("early", (EARLY, 8, 128), B16), ("late", (LATE, 8, 128), B16))


def scratch():
    buffers = [
        ("w_qkv", (512, 1536), B16), ("w_out", (512, 512), B16), ("w_conv", (3, 3, 128, 128), B16),
        ("got", (8, 32, 512), B16), ("turned", (16, 16, 512), B16), ("tokens", (16, 16, 512), B16),
        ("field", (40, 144, 128), B16), ("bins16", (32, 128), B16), ("bin_got", (64, 128), B16),
        ("edge_out", (2, 5, 16, 128), B16), ("edge_in", (2, 5, 16, 128), B16), ("bin_out", (2, 48, 128), B16),
        ("bin_in", (2, 48, 128), B16), ("rain", (48, 128), F32), ("edge_bins", (16, 128), F32),
        ("tok", (256, 512), B16), ("qkv", (256, 1536), B16), ("prob", (8, 512, 128), F32), ("mixed", (256, 512), B16),
        ("context", (256, 512), B16), ("raised", (16, 16, 128), B16),
        ("slots", (18, 16, 128), B16), ("lift_turned", (8, 48, 128), B16), ("lifted", (10, 48, 128), B16),
        ("query_turned", (8, 128, 512), B16), ("tok_turned", (512, 256), B16),
        ("hidden", (40, 144, 128), F32), ("slope", (40, 128, 128), F32), ("active", (40, 144, 384), B16),
        ("outer", (36, 144, 128), B16), ("taps", (36, 48, 128), B16), ("taps_turned", (36, 128, 48), B16),
        ("back_low", (48, 128), B16), ("back_mid", (48, 256), B16), ("back_high", (48, 128), B16),
        ("tap_sum", (144, 128), F32), ("loss_sum", (16, 128), F32), ("head_sum", (16, 128), F32),
        ("dlift", (8, 32, 128), B16), ("grad_fine", (32, 128, 128), F32), ("quantiles", (9, 32, 128), F32),
        ("fold_got", (8, 32, 128), B16), ("fold_turned", (16, 16, 128), B16), ("folded", (16, 16, 128), B16),
        ("dquery", (256, 512), B16), ("dkey", (512, 256), B16), ("dvalue", (512, 256), B16),
    ]
    sems = [("s_l", 7), ("s_tr", 7), ("r_tr", 7), ("s_tc", 15), ("r_tc", 15), ("s_h", 4), ("r_h", 4), ("s_e", 4), ("r_e", 4),
            ("s_lc", 15), ("r_lc", 15), ("s_lx", 16), ("r_lx", 2), ("s_lr", 7), ("r_lr", 7), ("s_ly", 8), ("r_ly", 2),
            ("s_fr", 7), ("r_fr", 7), ("s_fc", 15), ("r_fc", 15)]
    return ([(name, pltpu.VMEM(shape, dtype)) for name, shape, dtype in buffers]
            + [(name, DMA((count,))) for name, count in sems]
            + reducer_scratch("a_", EARLY) + reducer_scratch("b_", LATE))


def halo_rows(v, row):
    sends = [
        ((v.fine.at[pl.ds(30, 2)], v.field.at[pl.ds(2, 2), pl.ds(0, 128)], v.s_h.at[0], v.r_h.at[0]),
         (v.bins16.at[pl.ds(16, 16)], v.bin_got.at[pl.ds(0, 16)], v.s_h.at[1], v.r_h.at[1])),
        ((v.fine.at[pl.ds(0, 2)], v.field.at[pl.ds(36, 2), pl.ds(0, 128)], v.s_h.at[2], v.r_h.at[2]),
         (v.bins16.at[pl.ds(0, 16)], v.bin_got.at[pl.ds(48, 16)], v.s_h.at[3], v.r_h.at[3])),
    ]

    def start():
        @pl.when(row < 7)
        def _():
            for args in sends[0]:
                rcopy(*args, {"rows": row + 1}).start()

        @pl.when(row > 0)
        def _():
            for args in sends[1]:
                rcopy(*args, {"rows": row - 1}).start()

    def finish():
        @pl.when(row < 7)
        def _():
            for args in sends[0]:
                rcopy(*args, {"rows": row + 1}).wait_send()
            for args in sends[1]:
                rcopy(*args, {"rows": row + 1}).wait_recv()

        @pl.when(row > 0)
        def _():
            for args in sends[1]:
                rcopy(*args, {"rows": row - 1}).wait_send()
            for args in sends[0]:
                rcopy(*args, {"rows": row - 1}).wait_recv()

    return start, finish


def halo_cols(v, col):
    sends = [((v.edge_out.at[n], v.edge_in.at[n], v.s_e.at[2 * n], v.r_e.at[2 * n]),
              (v.bin_out.at[n], v.bin_in.at[n], v.s_e.at[2 * n + 1], v.r_e.at[2 * n + 1])) for n in range(2)]

    def start():
        @pl.when(col < 15)
        def _():
            for args in sends[0]:
                rcopy(*args, {"cols": col + 1}).start()

        @pl.when(col > 0)
        def _():
            for args in sends[1]:
                rcopy(*args, {"cols": col - 1}).start()

    def finish():
        @pl.when(col < 15)
        def _():
            for args in sends[0]:
                rcopy(*args, {"cols": col + 1}).wait_send()
            for args in sends[1]:
                rcopy(*args, {"cols": col + 1}).wait_recv()

        @pl.when(col > 0)
        def _():
            for args in sends[1]:
                rcopy(*args, {"cols": col - 1}).wait_send()
            for args in sends[0]:
                rcopy(*args, {"cols": col - 1}).wait_recv()

    return start, finish


def exchange_tokens(v, row, col, loads):
    sends = scatter_out("rows", 8, v.coarse, v.got, v.s_tr, v.r_tr, row)
    own = pltpu.make_async_copy(v.coarse.at[row], v.got.at[row], v.s_l.at[0])
    own.start()
    rows_start, rows_finish = halo_rows(v, row)
    rows_start()

    @pl.when(row == 0)
    def _():
        v.field[pl.ds(2, 2), :128] = jnp.zeros((2, 128, 128), B16)
        v.bin_got[pl.ds(0, 16)] = jnp.zeros((16, 128), B16)

    @pl.when(row == 7)
    def _():
        v.field[pl.ds(36, 2), :128] = jnp.zeros((2, 128, 128), B16)
        v.bin_got[pl.ds(48, 16)] = jnp.zeros((16, 128), B16)

    v.field[pl.ds(0, 2), :128] = jnp.zeros((2, 128, 128), B16)
    v.field[pl.ds(38, 2), :128] = jnp.zeros((2, 128, 128), B16)
    v.bin_got[pl.ds(16, 32)] = v.bins16[...]

    own.wait()
    wait_all(sends)
    v.turned[...] = dot(v.mid[...], v.got[...].reshape(256, 512)).astype(B16).reshape(16, 16, 512)
    sends = scatter_out("cols", 16, v.turned, v.tokens, v.s_tc, v.r_tc, col)
    v.tokens[col] = v.turned[col]

    loads[0].wait()
    rows_finish()
    rows = dot(v.place[...], v.bin_got[...])
    v.rain[...] = rows
    v.bin_out[0] = jnp.broadcast_to(rows[:, 127:128], (48, 128)).astype(B16)
    v.bin_out[1] = jnp.broadcast_to(rows[:, 0:1], (48, 128)).astype(B16)
    for q in range(5):
        v.edge_out[0, q] = dot(v.pick_hi[...], v.field[8 * q:8 * q + 8, 112:128].reshape(128, 128)).astype(B16)
        v.edge_out[1, q] = dot(v.pick_lo[...], v.field[8 * q:8 * q + 8, 0:16].reshape(128, 128)).astype(B16)
    cols_start, cols_finish = halo_cols(v, col)
    cols_start()

    @pl.when(col == 0)
    def _():
        v.edge_in[0] = jnp.zeros((5, 16, 128), B16)
        v.bin_in[0] = jnp.zeros((48, 128), B16)

    @pl.when(col == 15)
    def _():
        v.edge_in[1] = jnp.zeros((5, 16, 128), B16)
        v.bin_in[1] = jnp.zeros((48, 128), B16)

    wait_all(sends)
    return cols_finish


def attend(v):
    v.tok[...] = dot(v.group[...], v.tokens[...].reshape(256, 512)).astype(B16)
    for n in range(3):
        v.qkv[:, n * 512:(n + 1) * 512] = dot(v.tok[...], v.w_qkv[:, n * 512:(n + 1) * 512]).astype(B16)
    for g in range(2):
        for t in range(4):
            rows, at = slice(g * 128, g * 128 + 128), t * 128
            query = v.qkv[rows, at:at + 128]
            keyed = v.qkv[rows, 512 + at:512 + at + 128]
            valued = v.qkv[rows, 1024 + at:1024 + at + 128]
            scores = dot_nt(heads_down(query), keyed) * SCALE
            peak = jnp.max(scores, axis=-1, keepdims=True)
            powers = jnp.exp(scores - peak)
            share = powers / jnp.sum(powers, axis=-1, keepdims=True)
            v.prob[g * 4 + t] = share
            v.mixed[rows, at:at + 128] = dot(side_by_side(share.astype(B16)), heads_down(valued)).astype(B16)
    attended = dot(v.mixed[...], v.w_out[...]).astype(B16)
    v.context[...] = (v.tok[...].astype(F32) + attended.astype(F32)).astype(B16)
    lifted = dot(v.context[...], v.w_up[...]).astype(B16)
    v.raised[...] = dot(v.ungroup[...], lifted).astype(B16).reshape(16, 16, 128)


def edge_targets(v):
    lane = lax.broadcasted_iota(jnp.int32, (48, 128), 1)
    line = lax.broadcasted_iota(jnp.int32, (48, 128), 0)
    low, high = v.bin_in[0].astype(F32), v.bin_in[1].astype(F32)
    picked = jnp.where((lane & 15) == 0, high, jnp.where((lane & 15) == 15, low, 0.0))
    for b in range(9):
        here = line == 4 * b + (lane >> 4)
        v.edge_bins[b:b + 1] = jnp.sum(jnp.where(here, picked, 0.0), axis=0, keepdims=True)


def convolve(v, row, col):
    head_t = dot(v.eye[...], v.w_head_t[...]).astype(B16)
    place = lax.broadcasted_iota(jnp.int32, (144, 1), 0)
    right = jnp.where(col < 15, 130, 128)
    left = jnp.where(col > 0, 142, 144)
    inside = (place < right) | (place >= left)
    level = (lax.broadcasted_iota(jnp.int32, (16, 1), 0) + 1).astype(F32) / 10.0
    quant = lax.broadcasted_iota(jnp.int32, (16, 1), 0) < QUANT
    v.loss_sum[...] = jnp.zeros((16, 128), F32)
    v.head_sum[...] = jnp.zeros((16, 128), F32)
    v.tap_sum[...] = jnp.zeros((144, 128), F32)

    def start(i):
        raised = dot(v.up[...], v.lifted[i])
        for s in range(4):
            y = 4 * i + s - 4
            x = v.field[4 * i + s].astype(F32) + raised
            square = x * x
            bend = jnp.tanh(ROOT_2_PI * x * (1.0 + 0.044715 * square))
            half = 0.5 * (1.0 + bend)
            seen = (row * 32 + y >= 0) & (row * 32 + y < 256)
            act = jnp.where(inside & seen, x * half, 0.0)
            v.hidden[4 * i + s] = x
            v.active[4 * i + s] = shifted(act).astype(B16)
            v.slope[4 * i + s] = half[:128] + (0.5 * ROOT_2_PI) * x[:128] * (1.0 - bend[:128] * bend[:128]) * (
                1.0 + (3 * 0.044715) * square[:128])

    def forward(i):
        total = v.hidden[pl.ds(4 * i + 3, 4)].reshape(576, 128)
        windows = [v.active[pl.ds(4 * i + 2 + a, 4)].reshape(576, 384) for a in range(3)]
        total = total + dot(jnp.concatenate(windows, axis=1), v.w_conv[...].reshape(1152, 128))
        v.outer[pl.ds(4 * i, 4)] = total.astype(B16).reshape(4, 144, 128)

    def turn(i):
        own = v.outer[pl.ds(4 * i, 4), :128].reshape(512, 128)
        edge = v.outer[pl.ds(4 * i, 4), 128:144].reshape(64, 128)
        pixels = jnp.concatenate([own, edge, jnp.zeros((64, 128), B16)], axis=0)
        predicted = dot_nt(head_t, pixels)
        lines = [v.rain[pl.ds(4 * i + s, 1), :] for s in range(4)] + [v.edge_bins[pl.ds(i, 1), :]]
        target = jnp.concatenate(lines, axis=1) * (1.0 / 16.0) - 1.0
        lane = lax.broadcasted_iota(jnp.int32, (1, 640), 1)
        spot = lane - 512
        inner = lane < 512
        y = 4 * i - 1 + jnp.where(inner, lane >> 7, spot >> 4)
        side = (((spot & 15) == 0) & (col < 15)) | (((spot & 15) == 15) & (col > 0))
        seen = (row * 32 + y >= 0) & (row * 32 + y < 256) & (y < 33) & (inner | (side & (spot < 64)))
        mine = inner & (y >= 0) & (y < 32)
        error = target - predicted
        weight = jnp.where(error < 0.0, 1.0 - level, level)
        down = jnp.where(seen & quant, -weight * jnp.clip(error, -1.0, 1.0) * (1.0 / 1024.0), 0.0)
        size = jnp.abs(error)
        loss = weight * jnp.where(size <= 1.0, 0.5 * error * error, size - 0.5)
        loss = jnp.where(mine & quant, loss, 0.0)
        v.loss_sum[...] += loss[:, :128] + loss[:, 128:256] + loss[:, 256:384] + loss[:, 384:512]
        v.head_sum[...] += dot(jnp.where(mine, down, 0.0).astype(B16)[:, :512], own)
        edge = down[:, 512:]
        at = lax.broadcasted_iota(jnp.int32, (1, 128), 1)
        sets = []
        for s in range(4):
            line = down[:, s * 128:(s + 1) * 128]
            before = jnp.where(at == 0, pltpu.roll(edge, 113 - 16 * s, 1), pltpu.roll(line, 1, 1))
            after = jnp.where(at == 127, pltpu.roll(edge, 127 - 16 * s, 1), pltpu.roll(line, 127, 1))
            sets.append(jnp.concatenate([before, line, after], axis=0))
            v.taps[4 * i + s] = sets[s].astype(B16)
            row_y = 4 * i + s - 1
            value = predicted[:, s * 128:(s + 1) * 128]
            if not isinstance(i, int) or 0 <= row_y < 32:
                for q in range(QUANT):
                    v.quantiles[q, pl.ds(row_y, 1), :] = value[q:q + 1]
        v.taps_turned[pl.ds(4 * i, 4)] = jnp.concatenate(sets, axis=1).T.astype(B16).reshape(4, 128, 48)

    def back(i):
        windows = [v.taps_turned[pl.ds(4 * i + a, 4)].reshape(512, 48) for a in range(3)]
        both = dot(windows[1], v.back_mid[...])
        dactive = both[:, :128] + dot(windows[0], v.back_low[...]) + dot(windows[2], v.back_high[...])
        dhidden = (both[:, 128:] + v.slope[pl.ds(4 * i + 4, 4)].reshape(512, 128) * dactive).reshape(4, 128, 128)
        v.grad_fine[pl.ds(4 * i, 4)] = dhidden * 1024.0
        summed = dhidden[0] + dhidden[1] + dhidden[2] + dhidden[3]
        high = summed.astype(B16)
        low = (summed - high.astype(F32)).astype(B16)
        v.dlift[i] = (dot(v.fold[...], high) + dot(v.fold[...], low)).astype(B16)
        lines = [jnp.concatenate([v.taps[4 * i + a + s] for s in range(4)], axis=1) for a in range(3)]
        seen = v.active[pl.ds(4 * i + 4, 4), :128, 128:256].reshape(512, 128)
        v.tap_sum[...] += dot(jnp.concatenate(lines, axis=0), seen)

    def step(t):
        known = isinstance(t, int)
        if not known or 0 <= t - 5 <= 7:
            back(t - 5)
        if not known or 0 <= t - 3 <= 8:
            turn(t - 3)
        if not known or 0 <= t - 2 <= 8:
            forward(t - 2)
        if not known or t <= 9:
            start(t)

    for t in range(5):
        step(t)

    def loop(t, carry):
        step(t)
        return carry

    lax.fori_loop(5, 10, loop, 0)
    for t in range(10, 13):
        step(t)


def back_weights(v):
    head_t = dot(v.eye[...], v.w_head_t[...]).astype(B16)
    for a, name in enumerate(("back_low", "back_mid", "back_high")):
        parts = [dot_nt(head_t, v.w_conv[2 - a, 2 - b]).astype(B16) for b in range(3)]
        getattr(v, name)[:, :128] = jnp.concatenate(parts, axis=0)
    blank = jnp.zeros((16, 128), B16)
    v.back_mid[:, 128:] = jnp.concatenate([blank, head_t, blank], axis=0)


def local_units(v):
    v.a_g[128:146] = v.tap_sum[...].reshape(18, 8, 128).astype(B16)
    spot = lax.broadcasted_iota(jnp.int32, (16, 1), 0)
    total = jnp.sum(v.loss_sum[...], axis=0, keepdims=True)
    tail = jnp.where(spot < QUANT, v.head_sum[...], jnp.where(spot == QUANT, total, 0.0))
    v.a_g[146:148] = tail.reshape(2, 8, 128).astype(B16)
    v.a_g[148:EARLY] = jnp.zeros((EARLY - 148, 8, 128), B16)


def attend_back(v, mix_grad, s):
    for t in range(4):
        rows, at = slice(s * 128, s * 128 + 128), t * 128
        keyed = v.qkv[rows, 512 + at:512 + at + 128]
        valued = v.qkv[rows, 1024 + at:1024 + at + 128]
        mine = mix_grad[rows, at:at + 128]
        dprob = dot_nt(heads_down(mine), valued)
        share = v.prob[s * 4 + t]
        inner = jnp.sum(share * dprob, axis=-1, keepdims=True)
        dscore = (share * (dprob - inner) * SCALE).astype(B16)
        v.dquery[rows, at:at + 128] = dot(side_by_side(dscore), heads_down(keyed)).astype(B16)
        v.dkey[at:at + 128, rows] = dot(v.query_turned[s * 4 + t], dscore).astype(B16)
        v.dvalue[at:at + 128, rows] = dot(heads_across(mine), share.astype(B16)).astype(B16)


def whole_kernel(names, *refs):
    v = SimpleNamespace(**dict(zip(names, refs)))
    row, col, batch = lax.axis_index("rows"), lax.axis_index("cols"), lax.axis_index("batch")
    core, deep = row % 2, (row // 2) * 2 + batch
    x, y = col // 4, col % 4
    me = SimpleNamespace(
        core=core, deep=deep, other={"rows": row + 1 - 2 * core},
        first=x * (1 - core) + y * core, second=y * (1 - core) + x * core,
    )

    def in_first(k):
        p = (me.first + k) % 4
        return {"cols": (p * 4 + y) * (1 - core) + (x * 4 + p) * core}

    def in_second(k):
        p = (me.second + k) % 4
        return {"cols": (x * 4 + p) * (1 - core) + (p * 4 + y) * core}

    def in_deep(k):
        p = (deep + k) % 8
        return {"rows": (p // 2) * 2 + core, "batch": p % 2}

    me.in_first, me.in_second, me.in_deep = in_first, in_second, in_deep

    peers = [{"rows": (row + k) % 8} for k in range(1, 8)] + [{"cols": (col + k) % 16} for k in range(1, 16)]
    peers += [{"rows": (row + 2 * k) % 8, "batch": 1 - batch} for k in range(4)]
    barrier = pltpu.get_barrier_semaphore()
    for peer in peers:
        pl.semaphore_signal(barrier, inc=1, device_id=peer, device_id_type=MESH)
    loads = [pltpu.make_async_copy(v.fine, v.field.at[pl.ds(4, 32), pl.ds(0, 128)], v.s_l.at[1]),
             pltpu.make_async_copy(v.w_qkv_in, v.w_qkv, v.s_l.at[2]),
             pltpu.make_async_copy(v.w_out_in, v.w_out, v.s_l.at[3]),
             pltpu.make_async_copy(v.w_conv_in, v.w_conv, v.s_l.at[4])]
    for c in loads:
        c.start()
    v.bins16[...] = v.bins[...].astype(F32).astype(B16)
    pl.semaphore_wait(barrier, len(peers))
    cols_finish = exchange_tokens(v, row, col, loads)
    loads[1].wait()
    loads[2].wait()
    attend(v)

    finish = spread_out("cols", 16, col, v.raised, v.slots, v.s_lc, v.r_lc, v.s_lx, v.r_lx)
    cols_finish()
    for q in range(5):
        edge = dot(v.spread_hi[...], v.edge_in[0, q]) + dot(v.spread_lo[...], v.edge_in[1, q])
        v.field[8 * q:8 * q + 8, 128:144] = edge.astype(B16).reshape(8, 16, 128)
    edge_targets(v)
    for s in range(2):
        for t in range(4):
            v.query_turned[s * 4 + t] = heads_across(v.qkv[s * 128:s * 128 + 128, t * 128:t * 128 + 128])
    finish()
    v.lift_turned[...] = dot(v.back[...], v.slots[...].reshape(288, 128)).astype(B16).reshape(8, 48, 128)
    finish = spread_out("rows", 8, row, v.lift_turned, v.lifted, v.s_lr, v.r_lr, v.s_ly, v.r_ly)
    v.tok_turned[...] = v.tok[...].astype(F32).T.astype(B16)
    loads[3].wait()
    back_weights(v)
    finish()

    convolve(v, row, col)

    results = [pltpu.make_async_copy(v.grad_fine, v.grad_fine_out, v.s_l.at[5]),
               pltpu.make_async_copy(v.quantiles, v.quantiles_out, v.s_l.at[6])]
    sends = scatter_out("rows", 8, v.dlift, v.fold_got, v.s_fr, v.r_fr, row)
    v.fold_got[row] = v.dlift[row]
    for c in results:
        c.start()
    local_units(v)
    wait_all(sends)
    v.fold_turned[...] = dot(v.mid[...], v.fold_got[...].reshape(256, 128)).astype(B16).reshape(16, 16, 128)
    sends = scatter_out("cols", 16, v.fold_turned, v.folded, v.s_fc, v.r_fc, col)
    v.folded[col] = v.fold_turned[col]
    wait_all(sends)

    early = reducer(me, EARLY, v.a_g, v.early, v.a_got0, v.a_sum0, v.a_got1, v.a_sum1, v.a_got2, v.a_sum2, v.a_got3,
                    [getattr(v, "a_sem" + str(n)) for n in range(16)])
    late = reducer(me, LATE, v.b_g, v.late, v.b_got0, v.b_sum0, v.b_got1, v.b_sum1, v.b_got2, v.b_sum2, v.b_got3,
                   [getattr(v, "b_sem" + str(n)) for n in range(16)])
    lift_wide = dot(v.group[...], v.folded[...].reshape(256, 128))
    lift, lift_turned = lift_wide.astype(B16), lift_wide.T.astype(B16)
    put(v.a_g, 0, dot(lift_turned, v.mixed[...]))
    put(v.a_g, 64, dot(lift_turned, v.context[...]))
    early[0]()
    dcontext = dot_nt(lift, v.w_up[...]).astype(B16)
    mix_grad = dot_nt(dcontext, v.w_out[...]).astype(B16)
    attend_back(v, mix_grad, 0)
    early[1]()
    attend_back(v, mix_grad, 1)
    early[2]()
    put(v.b_g, 0, dot(v.tok_turned[...], v.dquery[...]))
    put(v.b_g, 256, dot_nt(v.tok_turned[...], v.dkey[...]))
    put(v.b_g, 512, dot_nt(v.tok_turned[...], v.dvalue[...]))
    late[0]()
    early[3]()
    late[1]()
    early[4]()
    late[2]()
    early[5]()
    late[3]()
    early[6]()
    late[4]()
    early[7]()
    late[5]()
    early[8]()
    for step in late[6:]:
        step()
    wait_all(results)


def unpack_kernel(early, late, fine, quantiles, w_up, w_head_t, eye,
                  grad_qkv, grad_out, grad_up, grad_conv, grad_head, loss, fine_out, quantiles_out,
                  late_in, early_in, wide, square, tall, flat, sems):
    through = [pltpu.make_async_copy(fine, fine_out, sems.at[0]), pltpu.make_async_copy(quantiles, quantiles_out, sems.at[1])]
    reads = [pltpu.make_async_copy(late.at[pl.ds(n * 256, 256)], late_in.at[pl.ds(n * 256, 256)], sems.at[2 + n]) for n in range(3)]
    reads.append(pltpu.make_async_copy(early, early_in, sems.at[5]))
    for c in reads + through:
        c.start()
    writes = []

    def write(src, dst, n):
        c = pltpu.make_async_copy(src, dst, sems.at[n])
        c.start()
        writes.append(c)

    for n in range(3):
        reads[n].wait()
        for m in range(4):
            at = n * 4 + m
            wide[n, :, m * 128:(m + 1) * 128] = late_in[at * 64:(at + 1) * 64].astype(F32).reshape(512, 128)
        write(wide.at[n], grad_qkv.at[:, pl.ds(n * 512, 512)], 6 + n)
    reads[3].wait()
    for n in range(4):
        mixed = early_in[n * 16:(n + 1) * 16].astype(F32).reshape(128, 128).T.astype(B16)
        square[n * 128:(n + 1) * 128] = dot_nt(mixed, w_up[...])
        tall[n * 128:(n + 1) * 128] = early_in[64 + n * 16:64 + (n + 1) * 16].astype(F32).reshape(128, 128).T
    write(square, grad_out, 9)
    write(tall, grad_up, 10)
    head_t = dot(eye[...], w_head_t[...]).astype(B16)
    for a in range(3):
        for b in range(3):
            at = 128 + (2 - a) * 6 + (2 - b) * 2
            seen = early_in[at:at + 2].astype(F32).reshape(16, 128).T.astype(B16)
            flat[(a * 3 + b) * 128:(a * 3 + b + 1) * 128] = dot(seen, head_t)
    write(flat, grad_conv, 11)
    tail = early_in[146:148].astype(F32).reshape(16, 128)
    grad_head[...] = tail[:QUANT]
    loss[...] = jnp.sum(tail[QUANT:QUANT + 1], axis=1, keepdims=True) * (1.0 / (1048576.0 * QUANT))
    wait_all(writes + through)


def body(fine_input, coarse, rain_bins, w_qkv, w_out, w_up, w_conv, w_head):
    group = group_table()
    eye = onehot(16, QUANT, [(q, q) for q in range(QUANT)])
    args = [coarse[0], fine_input[0], rain_bins[0], w_qkv, w_out, w_up, w_conv, w_head.T,
            mid_table(), group, group.T, back_table(), pick_table(0), pick_table(14), spread_table(0), spread_table(14),
            bins_table(), up_table(), sum_table(), eye]
    spaces = scratch()
    names = INPUTS + tuple(name for name, _, _ in OUTPUTS) + tuple(name for name, _ in spaces)
    vmem, anywhere = pl.BlockSpec(memory_space=pltpu.VMEM), pl.BlockSpec(memory_space=pl.ANY)

    def kernel(*refs):
        whole_kernel(names, *refs)

    quantiles, grad_fine, early, late = pl.pallas_call(
        kernel,
        out_shape=[jax.ShapeDtypeStruct(shape, dtype) for _, shape, dtype in OUTPUTS],
        in_specs=[pl.BlockSpec(memory_space=pl.ANY) if name in IN_HBM else vmem for name in INPUTS],
        out_specs=[anywhere, anywhere, vmem, vmem],
        scratch_shapes=[space for _, space in spaces],
        compiler_params=pltpu.CompilerParams(vmem_limit_bytes=LIMIT, collective_id=1, has_side_effects=True),
    )(*args)
    shapes = ((512, 1536), (512, 512), (512, 128), (1152, 128), (QUANT, 128), (1, 1), (32, 128, 128), (9, 32, 128))
    grad_qkv, grad_out, grad_up, grad_conv, grad_head, loss, fine, bands = pl.pallas_call(
        unpack_kernel,
        out_shape=[jax.ShapeDtypeStruct(shape, F32) for shape in shapes],
        in_specs=[anywhere] * 4 + [vmem] * 3,
        out_specs=[anywhere] * 4 + [vmem] * 2 + [anywhere] * 2,
        scratch_shapes=[pltpu.VMEM((LATE, 8, 128), B16), pltpu.VMEM((EARLY, 8, 128), B16), pltpu.VMEM((3, 512, 512), F32),
                        pltpu.VMEM((512, 512), F32), pltpu.VMEM((512, 128), F32), pltpu.VMEM((1152, 128), F32), DMA((12,))],
        compiler_params=pltpu.CompilerParams(vmem_limit_bytes=LIMIT),
    )(early, late, grad_fine, quantiles, w_up, w_head.T, eye)
    return (bands[None], loss.reshape(()), grad_qkv, grad_out, grad_up, grad_conv.reshape(3, 3, 128, 128),
            grad_head.T, fine[None])


def solution(mesh):
    placed = (
        P("batch", "rows", "cols", None),
        P("batch", "rows", "cols", None),
        P("batch", "rows", "cols"),
        P(),
        P(),
        P(),
        P(),
        P(),
    )
    return jax.shard_map(
        body,
        mesh=mesh,
        in_specs=placed,
        out_specs=(
            P("batch", None, "rows", "cols"),
            P(),
            P(),
            P(),
            P(),
            P(),
            P(),
            P("batch", "rows", "cols", None),
        ),
        check_vma=False,
    )
```

```python
import jax
import jax.numpy as jnp
import numpy as np
from types import SimpleNamespace
from jax import lax
from jax.experimental import pallas as pl
from jax.experimental.pallas import tpu as pltpu
from jax.sharding import PartitionSpec as P

HEAD_DIM = 32
QUANT = 9
MESH = pl.DeviceIdType.MESH
F32, B16 = jnp.float32, jnp.bfloat16
DMA = pltpu.SemaphoreType.DMA
SCALE = HEAD_DIM ** (-0.5)
ROOT_2_PI = 0.7978845608028654
LIMIT = 58 * 1024 * 1024
HALF = 512


def onehot(rows, cols, pairs):
    table = np.zeros((rows, cols), np.float32)
    for row, col in pairs:
        table[row, col] = 1.0
    return jnp.asarray(table, B16)


def mid_table():
    return onehot(256, 256, [(p * 16 + r * 2 + m, r * 32 + p * 2 + m)
                             for p in range(16) for r in range(8) for m in range(2)])


def group_table():
    return onehot(256, 256, [(m * 128 + c * 8 + r, c * 16 + r * 2 + m)
                             for m in range(2) for c in range(16) for r in range(8)])


def back_table():
    pairs = []
    for r in range(8):
        for j in range(32):
            pairs.append((r * 48 + j, (1 + j // 2) * 16 + r * 2 + j % 2))
        pairs.append((r * 48 + 32, 17 * 16 + r * 2))
        pairs.append((r * 48 + 35, r * 2 + 1))
    return onehot(384, 288, pairs)


def pick_table(first):
    return onehot(16, 128, [(2 * i + s, 16 * i + first + s) for i in range(8) for s in range(2)])


def spread_table(first):
    return onehot(128, 16, [(16 * i + first + s, 2 * i + s) for i in range(8) for s in range(2)])


def bins_table():
    return onehot(48, 64, [(0, 15)] + [(1 + y, 16 + y) for y in range(32)] + [(33, 48)])


def up_table():
    return onehot(144, 48, [(p, p // 4) for p in range(144)])


def sum_table():
    return onehot(32, 128, [(p // 4, p) for p in range(128)])


def dot(a, b):
    return jnp.dot(a, b, preferred_element_type=F32)


def dot_nt(a, b):
    return lax.dot_general(a, b, (((1,), (1,)), ((), ())), preferred_element_type=F32)


def rcopy(src, dst, send, recv, to):
    return pltpu.make_async_remote_copy(src_ref=src, dst_ref=dst, send_sem=send, recv_sem=recv,
                                        device_id=to, device_id_type=MESH)


def wait_all(copies):
    for c in copies:
        c.wait()


def peer_order(axis, me):
    if axis == "rows":
        steps = [(2, 0), (2, 1), (1, 0), (3, 0), (1, 1), (3, 1), (0, 1)]
        return [((me // 2 + a) % 4) * 2 + (me + b) % 2 for a, b in steps]
    steps = [(a, b) for a in range(4) for b in range(4) if a + b > 0]
    steps.sort(key=lambda step: -min(step[0], 4 - step[0]) - min(step[1], 4 - step[1]))
    return [((me // 4 + a) % 4) * 4 + (me + b) % 4 for a, b in steps]


def scatter_out(axis, src, got, send, recv, me):
    copies = []
    for n, p in enumerate(peer_order(axis, me)):
        c = rcopy(src.at[p], got.at[me], send.at[n], recv.at[n], {axis: p})
        c.start()
        copies.append(c)
    return copies


def spread_out(axis, count, me, src, main, send, recv, send_x, recv_x):
    copies = []
    for n, p in enumerate(peer_order(axis, me)):
        c = rcopy(src.at[p], main.at[1 + me], send.at[n], recv.at[n], {axis: p})
        c.start()
        copies.append(c)
    main[1 + me] = src[me]

    def after(t):
        return rcopy(src.at[t - 1], main.at[0], send_x.at[t], recv_x.at[0], {axis: t})

    def before(t):
        return rcopy(src.at[t + 1], main.at[count + 1], send_x.at[t], recv_x.at[1], {axis: t})

    @pl.when(me == count - 1)
    def _():
        for t in range(1, count - 1):
            after(t).start()
        main[0] = src[count - 2]
        main[count + 1] = jnp.zeros(main.shape[1:], B16)

    @pl.when(me == 0)
    def _():
        for t in range(1, count - 1):
            before(t).start()
        main[count + 1] = src[1]
        main[0] = jnp.zeros(main.shape[1:], B16)

    def finish():
        @pl.when(me == count - 1)
        def _():
            for t in range(1, count - 1):
                after(t).wait_send()

        @pl.when(me == 0)
        def _():
            for t in range(1, count - 1):
                before(t).wait_send()

        @pl.when((me > 0) & (me < count - 1))
        def _():
            after(1).wait_recv()
            before(1).wait_recv()

        wait_all(copies)

    return finish


def head_mask(h):
    lane = lax.broadcasted_iota(jnp.int32, (1, 128), 1)
    return jnp.where((lane >> 5) == h, 1.0, 0.0).astype(B16)


def heads_down(tile):
    return jnp.concatenate([tile * head_mask(h) for h in range(4)], axis=0)


def heads_across(tile):
    turned = tile.astype(F32).T
    line = lax.broadcasted_iota(jnp.int32, (128, 1), 0) >> 5
    return jnp.concatenate([jnp.where(line == h, turned, 0.0) for h in range(4)], axis=1).astype(B16)


def side_by_side(stack):
    return jnp.concatenate([stack[h * 128:(h + 1) * 128] for h in range(4)], axis=1)


def put(g, at, value):
    rows, cols = value.shape
    size = rows // 8
    for n in range(cols // 128):
        g[at + n * size:at + (n + 1) * size] = value[:, n * 128:(n + 1) * 128].reshape(size, 8, 128).astype(B16)


def shifted(line):
    return jnp.concatenate([pltpu.roll(line, 1, 0), line, pltpu.roll(line, 143, 0)], axis=1)


def reducer(me, axes, units, g, out, got0, sum0, got1, sum1, got2, sum2, got3, sems):
    core, deep = me.core, me.deep
    (first, in_first), (second, in_second) = axes
    u0, u1, u2, u3 = units // 2, units // 8, units // 32, units // 256
    s0, r0, s1, r1, s2, r2, s3, r3, as3, ar3, as2, ar2, as1, ar1, as0, ar0 = sems
    place = core * u0 + first * u1 + second * u2
    held = {}

    def sum_up(terms):
        total = terms[0].astype(F32)
        for term in terms[1:]:
            total = total + term.astype(F32)
        return total

    def near_start():
        held["near"] = []
        for n, k in enumerate((1, 2, 3, 0)):
            p = (first + k) % 4
            c = rcopy(g.at[pl.ds((1 - core) * u0 + p * u1, u1)], got0.at[p], s0.at[n], r0.at[n], me.other)
            c.start()
            held["near"].append(c)

    def first_start():
        held["first"] = []
        for n, k in enumerate((1, 2, 3)):
            p = (first + k) % 4
            held["near"][n].wait_recv()
            sum0[p] = sum_up([g[pl.ds(core * u0 + p * u1, u1)], got0[p]]).astype(B16)
            c = rcopy(sum0.at[p], got1.at[k - 1], s1.at[k - 1], r1.at[k - 1], in_first(k))
            c.start()
            held["first"].append(c)
        held["near"][3].wait_recv()

    def second_start():
        wait_all(held["first"])
        sum1[...] = sum_up([g[pl.ds(core * u0 + first * u1, u1)], got0[first], got1[0], got1[1], got1[2]]).astype(B16)
        held["second"] = []
        for k in (1, 2, 3):
            p = (second + k) % 4
            c = rcopy(sum1.at[pl.ds(p * u2, u2)], got2.at[k - 1], s2.at[k - 1], r2.at[k - 1], in_second(k))
            c.start()
            held["second"].append(c)
        for c in held["near"]:
            c.wait_send()

    def deep_start():
        wait_all(held["second"])
        sum2[...] = sum_up([sum1[pl.ds(second * u2, u2)], got2[0], got2[1], got2[2]]).astype(B16)
        held["deep"] = []
        for k in (4, 3, 5, 2, 6, 1, 7):
            p = (deep + k) % 8
            c = rcopy(sum2.at[pl.ds(p * u3, u3)], got3.at[k - 1], s3.at[k - 1], r3.at[k - 1], me.in_deep(k))
            c.start()
            held["deep"].append(c)

    def deep_gather():
        wait_all(held["deep"])
        mine = sum_up([sum2[pl.ds(deep * u3, u3)]] + [got3[k] for k in range(7)])
        out[pl.ds(place + deep * u3, u3)] = mine.astype(B16)
        block = out.at[pl.ds(place + deep * u3, u3)]
        held["deep"] = []
        for k in (4, 3, 5, 2, 6, 1, 7):
            c = rcopy(block, block, as3.at[k - 1], ar3.at[k - 1], me.in_deep(k))
            c.start()
            held["deep"].append(c)

    def second_gather():
        wait_all(held["deep"])
        block = out.at[pl.ds(place, u2)]
        held["second"] = []
        for k in (1, 2, 3):
            c = rcopy(block, block, as2.at[k - 1], ar2.at[k - 1], in_second(k))
            c.start()
            held["second"].append(c)

    def forward(n, p):
        block = out.at[pl.ds(core * u0 + p * u1, u1)]
        c = rcopy(block, block, as0.at[n], ar0.at[n], me.other)
        c.start()
        held["near"].append(c)

    def first_gather():
        wait_all(held["second"])
        block = out.at[pl.ds(core * u0 + first * u1, u1)]
        held["first"], held["near"] = [], []
        for k in (1, 2, 3):
            c = rcopy(block, block, as1.at[k - 1], ar1.at[k - 1], in_first(k))
            c.start()
            held["first"].append(c)
        forward(0, first)

    def near_gather():
        for k in (1, 2, 3):
            held["first"][k - 1].wait_recv()
            forward(k, (first + 4 - k) % 4)

    def finish():
        for c in held["first"]:
            c.wait_send()
        wait_all(held["near"])

    return [near_start, first_start, second_start, deep_start, deep_gather, second_gather, first_gather,
            near_gather, finish]


def reducer_scratch(tag, units):
    unit = (8, 128)
    u1, u2, u3 = units // 8, units // 32, units // 256
    shapes = [("g", (units,) + unit), ("got0", (4, u1) + unit), ("sum0", (4, u1) + unit), ("got1", (3, u1) + unit),
              ("sum1", (u1,) + unit), ("got2", (3, u2) + unit), ("sum2", (u2,) + unit), ("got3", (7, u3) + unit)]
    result = [(tag + name, pltpu.VMEM(shape, B16)) for name, shape in shapes]
    for n, count in enumerate((4, 4, 3, 3, 3, 3, 7, 7, 7, 7, 3, 3, 3, 3, 4, 4)):
        result.append((tag + "sem" + str(n), DMA((count,))))
    return result


INPUTS = ("coarse", "fine", "bins", "w_qkv_in", "w_out_in", "w_up", "w_conv_in", "w_head_t",
          "mid", "group", "ungroup", "back", "pick_lo", "pick_hi", "spread_lo", "spread_hi", "place", "up", "fold", "eye")
IN_HBM = ("coarse", "fine", "w_qkv_in", "w_out_in", "w_conv_in")
OUTPUTS = (("quantiles_out", (9, 32, 128), F32), ("grad_fine_out", (32, 128, 128), F32),
           ("low_half", (HALF, 8, 128), B16), ("high_half", (HALF, 8, 128), B16))


def scratch():
    buffers = [
        ("w_qkv", (512, 1536), B16), ("w_out", (512, 512), B16), ("w_conv", (3, 3, 128, 128), B16),
        ("got", (8, 32, 512), B16), ("turned", (16, 16, 512), B16), ("tokens", (16, 16, 512), B16),
        ("field", (40, 144, 128), B16), ("bins16", (32, 128), B16), ("bin_got", (64, 128), B16),
        ("edge_out", (2, 5, 16, 128), B16), ("edge_in", (2, 5, 16, 128), B16), ("bin_out", (2, 48, 128), B16),
        ("bin_in", (2, 48, 128), B16), ("rain", (48, 128), F32), ("edge_bins", (16, 128), F32),
        ("tok", (256, 512), B16), ("qkv", (256, 1536), B16), ("prob", (8, 512, 128), F32), ("mixed", (256, 512), B16),
        ("context", (256, 512), B16), ("raised", (16, 16, 128), B16),
        ("slots", (18, 16, 128), B16), ("lift_turned", (8, 48, 128), B16), ("lifted", (10, 48, 128), B16),
        ("query_turned", (8, 128, 512), B16), ("tok_turned", (512, 256), B16),
        ("hidden", (40, 144, 128), F32), ("slope", (40, 128, 128), F32), ("active", (40, 144, 384), B16),
        ("outer", (36, 144, 128), B16), ("taps", (36, 48, 128), B16), ("taps_turned", (36, 128, 48), B16),
        ("back_low", (48, 128), B16), ("back_mid", (48, 256), B16), ("back_high", (48, 128), B16),
        ("tap_sum", (144, 128), F32), ("loss_sum", (16, 128), F32), ("head_sum", (16, 128), F32),
        ("dlift", (8, 32, 128), B16), ("grad_fine", (32, 128, 128), F32), ("quantiles", (9, 32, 128), F32),
        ("fold_got", (8, 32, 128), B16), ("fold_turned", (16, 16, 128), B16), ("folded", (16, 16, 128), B16),
        ("dquery", (256, 512), B16), ("dkey", (512, 256), B16), ("dvalue", (512, 256), B16),
    ]
    sems = [("s_l", 7), ("s_tr", 7), ("r_tr", 7), ("s_tc", 15), ("r_tc", 15), ("s_h", 4), ("r_h", 4), ("s_e", 4), ("r_e", 4),
            ("s_lc", 15), ("r_lc", 15), ("s_lx", 16), ("r_lx", 2), ("s_lr", 7), ("r_lr", 7), ("s_ly", 8), ("r_ly", 2),
            ("s_fr", 7), ("r_fr", 7), ("s_fc", 15), ("r_fc", 15)]
    return ([(name, pltpu.VMEM(shape, dtype)) for name, shape, dtype in buffers]
            + [(name, DMA((count,))) for name, count in sems]
            + reducer_scratch("a_", HALF) + reducer_scratch("b_", HALF))


def halo_rows(v, row):
    sends = [
        ((v.fine.at[pl.ds(30, 2)], v.field.at[pl.ds(2, 2), pl.ds(0, 128)], v.s_h.at[0], v.r_h.at[0]),
         (v.bins16.at[pl.ds(16, 16)], v.bin_got.at[pl.ds(0, 16)], v.s_h.at[1], v.r_h.at[1])),
        ((v.fine.at[pl.ds(0, 2)], v.field.at[pl.ds(36, 2), pl.ds(0, 128)], v.s_h.at[2], v.r_h.at[2]),
         (v.bins16.at[pl.ds(0, 16)], v.bin_got.at[pl.ds(48, 16)], v.s_h.at[3], v.r_h.at[3])),
    ]

    def start():
        @pl.when(row < 7)
        def _():
            for args in sends[0]:
                rcopy(*args, {"rows": row + 1}).start()

        @pl.when(row > 0)
        def _():
            for args in sends[1]:
                rcopy(*args, {"rows": row - 1}).start()

    def finish():
        @pl.when(row < 7)
        def _():
            for args in sends[0]:
                rcopy(*args, {"rows": row + 1}).wait_send()
            for args in sends[1]:
                rcopy(*args, {"rows": row + 1}).wait_recv()

        @pl.when(row > 0)
        def _():
            for args in sends[1]:
                rcopy(*args, {"rows": row - 1}).wait_send()
            for args in sends[0]:
                rcopy(*args, {"rows": row - 1}).wait_recv()

    return start, finish


def halo_cols(v, col):
    sends = [((v.edge_out.at[n], v.edge_in.at[n], v.s_e.at[2 * n], v.r_e.at[2 * n]),
              (v.bin_out.at[n], v.bin_in.at[n], v.s_e.at[2 * n + 1], v.r_e.at[2 * n + 1])) for n in range(2)]

    def start():
        @pl.when(col < 15)
        def _():
            for args in sends[0]:
                rcopy(*args, {"cols": col + 1}).start()

        @pl.when(col > 0)
        def _():
            for args in sends[1]:
                rcopy(*args, {"cols": col - 1}).start()

    def finish():
        @pl.when(col < 15)
        def _():
            for args in sends[0]:
                rcopy(*args, {"cols": col + 1}).wait_send()
            for args in sends[1]:
                rcopy(*args, {"cols": col + 1}).wait_recv()

        @pl.when(col > 0)
        def _():
            for args in sends[1]:
                rcopy(*args, {"cols": col - 1}).wait_send()
            for args in sends[0]:
                rcopy(*args, {"cols": col - 1}).wait_recv()

    return start, finish


def exchange_tokens(v, row, col, loads):
    sends = scatter_out("rows", v.coarse, v.got, v.s_tr, v.r_tr, row)
    own = pltpu.make_async_copy(v.coarse.at[row], v.got.at[row], v.s_l.at[0])
    own.start()
    rows_start, rows_finish = halo_rows(v, row)
    rows_start()

    @pl.when(row == 0)
    def _():
        v.field[pl.ds(2, 2), :128] = jnp.zeros((2, 128, 128), B16)
        v.bin_got[pl.ds(0, 16)] = jnp.zeros((16, 128), B16)

    @pl.when(row == 7)
    def _():
        v.field[pl.ds(36, 2), :128] = jnp.zeros((2, 128, 128), B16)
        v.bin_got[pl.ds(48, 16)] = jnp.zeros((16, 128), B16)

    v.field[pl.ds(0, 2), :128] = jnp.zeros((2, 128, 128), B16)
    v.field[pl.ds(38, 2), :128] = jnp.zeros((2, 128, 128), B16)
    v.bin_got[pl.ds(16, 32)] = v.bins16[...]

    own.wait()
    wait_all(sends)
    v.turned[...] = dot(v.mid[...], v.got[...].reshape(256, 512)).astype(B16).reshape(16, 16, 512)
    sends = scatter_out("cols", v.turned, v.tokens, v.s_tc, v.r_tc, col)
    v.tokens[col] = v.turned[col]

    loads[0].wait()
    rows_finish()
    rows = dot(v.place[...], v.bin_got[...])
    v.rain[...] = rows
    v.bin_out[0] = jnp.broadcast_to(rows[:, 127:128], (48, 128)).astype(B16)
    v.bin_out[1] = jnp.broadcast_to(rows[:, 0:1], (48, 128)).astype(B16)
    for q in range(5):
        v.edge_out[0, q] = dot(v.pick_hi[...], v.field[8 * q:8 * q + 8, 112:128].reshape(128, 128)).astype(B16)
        v.edge_out[1, q] = dot(v.pick_lo[...], v.field[8 * q:8 * q + 8, 0:16].reshape(128, 128)).astype(B16)
    cols_start, cols_finish = halo_cols(v, col)
    cols_start()

    @pl.when(col == 0)
    def _():
        v.edge_in[0] = jnp.zeros((5, 16, 128), B16)
        v.bin_in[0] = jnp.zeros((48, 128), B16)

    @pl.when(col == 15)
    def _():
        v.edge_in[1] = jnp.zeros((5, 16, 128), B16)
        v.bin_in[1] = jnp.zeros((48, 128), B16)

    wait_all(sends)
    return cols_finish


def attend(v):
    v.tok[...] = dot(v.group[...], v.tokens[...].reshape(256, 512)).astype(B16)
    for n in range(3):
        v.qkv[:, n * 512:(n + 1) * 512] = dot(v.tok[...], v.w_qkv[:, n * 512:(n + 1) * 512]).astype(B16)
    for g in range(2):
        for t in range(4):
            rows, at = slice(g * 128, g * 128 + 128), t * 128
            query = v.qkv[rows, at:at + 128]
            keyed = v.qkv[rows, 512 + at:512 + at + 128]
            valued = v.qkv[rows, 1024 + at:1024 + at + 128]
            scores = dot_nt(heads_down(query), keyed) * SCALE
            peak = jnp.max(scores, axis=-1, keepdims=True)
            powers = jnp.exp(scores - peak)
            share = powers / jnp.sum(powers, axis=-1, keepdims=True)
            v.prob[g * 4 + t] = share
            v.mixed[rows, at:at + 128] = dot(side_by_side(share.astype(B16)), heads_down(valued)).astype(B16)
    attended = dot(v.mixed[...], v.w_out[...]).astype(B16)
    v.context[...] = (v.tok[...].astype(F32) + attended.astype(F32)).astype(B16)
    lifted = dot(v.context[...], v.w_up[...]).astype(B16)
    v.raised[...] = dot(v.ungroup[...], lifted).astype(B16).reshape(16, 16, 128)


def edge_targets(v):
    lane = lax.broadcasted_iota(jnp.int32, (48, 128), 1)
    line = lax.broadcasted_iota(jnp.int32, (48, 128), 0)
    low, high = v.bin_in[0].astype(F32), v.bin_in[1].astype(F32)
    picked = jnp.where((lane & 15) == 0, high, jnp.where((lane & 15) == 15, low, 0.0))
    for b in range(9):
        here = line == 4 * b + (lane >> 4)
        v.edge_bins[b:b + 1] = jnp.sum(jnp.where(here, picked, 0.0), axis=0, keepdims=True)


def convolve(v, row, col):
    head_t = dot(v.eye[...], v.w_head_t[...]).astype(B16)
    place = lax.broadcasted_iota(jnp.int32, (144, 1), 0)
    right = jnp.where(col < 15, 130, 128)
    left = jnp.where(col > 0, 142, 144)
    inside = (place < right) | (place >= left)
    level = (lax.broadcasted_iota(jnp.int32, (16, 1), 0) + 1).astype(F32) / 10.0
    quant = lax.broadcasted_iota(jnp.int32, (16, 1), 0) < QUANT
    v.loss_sum[...] = jnp.zeros((16, 128), F32)
    v.head_sum[...] = jnp.zeros((16, 128), F32)
    v.tap_sum[...] = jnp.zeros((144, 128), F32)
    v.active[pl.ds(38, 2)] = jnp.zeros((2, 144, 384), B16)
    v.hidden[pl.ds(38, 2)] = jnp.zeros((2, 144, 128), F32)

    def start(i):
        raised = dot(v.up[...], v.lifted[i])
        rims = {0: (2, 3), 9: (0, 1)}.get(i, range(4)) if isinstance(i, int) else range(4)
        for s in rims:
            y = 4 * i + s - 4
            x = v.field[4 * i + s].astype(F32) + raised
            square = x * x
            bend = jnp.tanh(ROOT_2_PI * x * (1.0 + 0.044715 * square))
            half = 0.5 * (1.0 + bend)
            act = x * half
            if isinstance(i, int) and i in (0, 9):
                act = jnp.where(inside & (row * 32 + y >= 0) & (row * 32 + y < 256), act, 0.0)
            else:
                act = jnp.concatenate([act[:128], jnp.where(inside[128:], act[128:], 0.0)], axis=0)
            v.hidden[4 * i + s] = x
            v.active[4 * i + s] = shifted(act).astype(B16)
            v.slope[4 * i + s] = half[:128] + (0.5 * ROOT_2_PI) * x[:128] * (1.0 - bend[:128] * bend[:128]) * (
                1.0 + (3 * 0.044715) * square[:128])

    def forward(i):
        total = v.hidden[pl.ds(4 * i + 3, 4)].reshape(576, 128)
        windows = [v.active[pl.ds(4 * i + 2 + a, 4)].reshape(576, 384) for a in range(3)]
        total = total + dot(jnp.concatenate(windows, axis=1), v.w_conv[...].reshape(1152, 128))
        v.outer[pl.ds(4 * i, 4)] = total.astype(B16).reshape(4, 144, 128)

    def turn(i):
        own = v.outer[pl.ds(4 * i, 4), :128].reshape(512, 128)
        edge = v.outer[pl.ds(4 * i, 4), 128:144].reshape(64, 128)
        pixels = jnp.concatenate([own, edge, jnp.zeros((64, 128), B16)], axis=0)
        predicted = dot_nt(head_t, pixels)
        lines = [v.rain[pl.ds(4 * i + s, 1), :] for s in range(4)] + [v.edge_bins[pl.ds(i, 1), :]]
        target = jnp.concatenate(lines, axis=1) * (1.0 / 16.0) - 1.0
        lane = lax.broadcasted_iota(jnp.int32, (1, 640), 1)
        spot = lane - 512
        inner = lane < 512
        y = 4 * i - 1 + jnp.where(inner, lane >> 7, spot >> 4)
        side = (((spot & 15) == 0) & (col < 15)) | (((spot & 15) == 15) & (col > 0))
        seen = (row * 32 + y >= 0) & (row * 32 + y < 256) & (y < 33) & (inner | (side & (spot < 64)))
        mine = inner & (y >= 0) & (y < 32)
        error = target - predicted
        weight = jnp.where(error < 0.0, 1.0 - level, level)
        down = jnp.where(seen & quant, -weight * jnp.clip(error, -1.0, 1.0) * (1.0 / 1024.0), 0.0)
        size = jnp.abs(error)
        loss = weight * jnp.where(size <= 1.0, 0.5 * error * error, size - 0.5)
        loss = jnp.where(mine & quant, loss, 0.0)
        v.loss_sum[...] += loss[:, :128] + loss[:, 128:256] + loss[:, 256:384] + loss[:, 384:512]
        v.head_sum[...] += dot(jnp.where(mine, down, 0.0).astype(B16)[:, :512], own)
        edge = down[:, 512:]
        at = lax.broadcasted_iota(jnp.int32, (1, 128), 1)
        sets = []
        for s in range(4):
            line = down[:, s * 128:(s + 1) * 128]
            before = jnp.where(at == 0, pltpu.roll(edge, 113 - 16 * s, 1), pltpu.roll(line, 1, 1))
            after = jnp.where(at == 127, pltpu.roll(edge, 127 - 16 * s, 1), pltpu.roll(line, 127, 1))
            sets.append(jnp.concatenate([before, line, after], axis=0))
            v.taps[4 * i + s] = sets[s].astype(B16)
            row_y = 4 * i + s - 1
            value = predicted[:, s * 128:(s + 1) * 128]
            if not isinstance(i, int) or 0 <= row_y < 32:
                for q in range(QUANT):
                    v.quantiles[q, pl.ds(row_y, 1), :] = value[q:q + 1]
        v.taps_turned[pl.ds(4 * i, 4)] = jnp.concatenate(sets, axis=1).T.astype(B16).reshape(4, 128, 48)

    def back(i):
        windows = [v.taps_turned[pl.ds(4 * i + a, 4)].reshape(512, 48) for a in range(3)]
        both = dot(windows[1], v.back_mid[...])
        dactive = both[:, :128] + dot(windows[0], v.back_low[...]) + dot(windows[2], v.back_high[...])
        dhidden = (both[:, 128:] + v.slope[pl.ds(4 * i + 4, 4)].reshape(512, 128) * dactive).reshape(4, 128, 128)
        v.grad_fine[pl.ds(4 * i, 4)] = dhidden * 1024.0
        summed = dhidden[0] + dhidden[1] + dhidden[2] + dhidden[3]
        high = summed.astype(B16)
        low = (summed - high.astype(F32)).astype(B16)
        v.dlift[i] = (dot(v.fold[...], high) + dot(v.fold[...], low)).astype(B16)
        lines = [jnp.concatenate([v.taps[4 * i + a + s] for s in range(4)], axis=1) for a in range(3)]
        seen = v.active[pl.ds(4 * i + 4, 4), :128, 128:256].reshape(512, 128)
        v.tap_sum[...] += dot(jnp.concatenate(lines, axis=0), seen)

    def step(t):
        known = isinstance(t, int)
        if not known or 0 <= t - 5 <= 7:
            back(t - 5)
        if not known or 0 <= t - 3 <= 8:
            turn(t - 3)
        if not known or 0 <= t - 2 <= 8:
            forward(t - 2)
        if not known or t <= 9:
            start(t)

    for t in range(5):
        step(t)

    def loop(t, carry):
        step(t)
        return carry

    lax.fori_loop(5, 9, loop, 0)
    for t in range(9, 13):
        step(t)


def back_weights(v):
    head_t = dot(v.eye[...], v.w_head_t[...]).astype(B16)
    for a, name in enumerate(("back_low", "back_mid", "back_high")):
        parts = [dot_nt(head_t, v.w_conv[2 - a, 2 - b]).astype(B16) for b in range(3)]
        getattr(v, name)[:, :128] = jnp.concatenate(parts, axis=0)
    blank = jnp.zeros((16, 128), B16)
    v.back_mid[:, 128:] = jnp.concatenate([blank, head_t, blank], axis=0)


def local_units(v):
    v.b_g[384:402] = v.tap_sum[...].reshape(18, 8, 128).astype(B16)
    spot = lax.broadcasted_iota(jnp.int32, (16, 1), 0)
    total = jnp.sum(v.loss_sum[...], axis=0, keepdims=True)
    tail = jnp.where(spot < QUANT, v.head_sum[...], jnp.where(spot == QUANT, total, 0.0))
    v.b_g[402:404] = tail.reshape(2, 8, 128).astype(B16)
    v.b_g[404:HALF] = jnp.zeros((HALF - 404, 8, 128), B16)


def attend_back(v, mix_grad, g, tiles):
    for s, t in [(s, t) for s in range(2) for t in tiles]:
        rows, at = slice(s * 128, s * 128 + 128), t * 128
        keyed = v.qkv[rows, 512 + at:512 + at + 128]
        valued = v.qkv[rows, 1024 + at:1024 + at + 128]
        mine = mix_grad[rows, at:at + 128]
        dprob = dot_nt(heads_down(mine), valued)
        share = v.prob[s * 4 + t]
        inner = jnp.sum(share * dprob, axis=-1, keepdims=True)
        dscore = (share * (dprob - inner) * SCALE).astype(B16)
        v.dquery[rows, at:at + 128] = dot(side_by_side(dscore), heads_down(keyed)).astype(B16)
        v.dkey[at:at + 128, rows] = dot(v.query_turned[s * 4 + t], dscore).astype(B16)
        v.dvalue[at:at + 128, rows] = dot(heads_across(mine), share.astype(B16)).astype(B16)
    at = tiles[0] * 128
    put(g, 0, dot(v.tok_turned[...], v.dquery[:, at:at + 256]))
    put(g, 128, dot_nt(v.tok_turned[...], v.dkey[at:at + 256]))
    put(g, 256, dot_nt(v.tok_turned[...], v.dvalue[at:at + 256]))


def whole_kernel(names, *refs):
    v = SimpleNamespace(**dict(zip(names, refs)))
    row, col, batch = lax.axis_index("rows"), lax.axis_index("cols"), lax.axis_index("batch")
    core, deep = row % 2, (row // 2) * 2 + batch
    x, y = col // 4, col % 4
    me = SimpleNamespace(
        core=core, deep=deep, other={"rows": row + 1 - 2 * core},
    )
    x_axis = (x, lambda k: {"cols": ((x + k) % 4) * 4 + y})
    y_axis = (y, lambda k: {"cols": x * 4 + (y + k) % 4})

    def in_deep(k):
        p = (deep + k) % 8
        return {"rows": (p // 2) * 2 + core, "batch": p % 2}

    me.in_deep = in_deep

    peers = [{"rows": (row + k) % 8} for k in range(1, 8)] + [{"cols": (col + k) % 16} for k in range(1, 16)]
    peers += [{"rows": (row + 2 * k) % 8, "batch": 1 - batch} for k in range(4)]
    barrier = pltpu.get_barrier_semaphore()
    for peer in peers:
        pl.semaphore_signal(barrier, inc=1, device_id=peer, device_id_type=MESH)
    loads = [pltpu.make_async_copy(v.fine, v.field.at[pl.ds(4, 32), pl.ds(0, 128)], v.s_l.at[1]),
             pltpu.make_async_copy(v.w_qkv_in, v.w_qkv, v.s_l.at[2]),
             pltpu.make_async_copy(v.w_out_in, v.w_out, v.s_l.at[3]),
             pltpu.make_async_copy(v.w_conv_in, v.w_conv, v.s_l.at[4])]
    for c in loads:
        c.start()
    v.bins16[...] = v.bins[...].astype(F32).astype(B16)
    pl.semaphore_wait(barrier, len(peers))
    cols_finish = exchange_tokens(v, row, col, loads)
    loads[1].wait()
    loads[2].wait()
    attend(v)

    finish = spread_out("cols", 16, col, v.raised, v.slots, v.s_lc, v.r_lc, v.s_lx, v.r_lx)
    cols_finish()
    for q in range(5):
        edge = dot(v.spread_hi[...], v.edge_in[0, q]) + dot(v.spread_lo[...], v.edge_in[1, q])
        v.field[8 * q:8 * q + 8, 128:144] = edge.astype(B16).reshape(8, 16, 128)
    edge_targets(v)
    for s in range(2):
        for t in range(4):
            v.query_turned[s * 4 + t] = heads_across(v.qkv[s * 128:s * 128 + 128, t * 128:t * 128 + 128])
    finish()
    v.lift_turned[...] = dot(v.back[...], v.slots[...].reshape(288, 128)).astype(B16).reshape(8, 48, 128)
    finish = spread_out("rows", 8, row, v.lift_turned, v.lifted, v.s_lr, v.r_lr, v.s_ly, v.r_ly)
    v.tok_turned[...] = v.tok[...].astype(F32).T.astype(B16)
    loads[3].wait()
    back_weights(v)
    finish()

    convolve(v, row, col)

    results = [pltpu.make_async_copy(v.grad_fine, v.grad_fine_out, v.s_l.at[5]),
               pltpu.make_async_copy(v.quantiles, v.quantiles_out, v.s_l.at[6])]
    sends = scatter_out("rows", v.dlift, v.fold_got, v.s_fr, v.r_fr, row)
    v.fold_got[row] = v.dlift[row]
    for c in results:
        c.start()
    local_units(v)
    wait_all(sends)
    v.fold_turned[...] = dot(v.mid[...], v.fold_got[...].reshape(256, 128)).astype(B16).reshape(16, 16, 128)
    sends = scatter_out("cols", v.fold_turned, v.folded, v.s_fc, v.r_fc, col)
    v.folded[col] = v.fold_turned[col]
    wait_all(sends)

    low = reducer(me, (x_axis, y_axis), HALF, v.a_g, v.low_half, v.a_got0, v.a_sum0, v.a_got1, v.a_sum1, v.a_got2, v.a_sum2,
                  v.a_got3, [getattr(v, "a_sem" + str(n)) for n in range(16)])
    high = reducer(me, (y_axis, x_axis), HALF, v.b_g, v.high_half, v.b_got0, v.b_sum0, v.b_got1, v.b_sum1, v.b_got2, v.b_sum2,
                   v.b_got3, [getattr(v, "b_sem" + str(n)) for n in range(16)])
    lift_wide = dot(v.group[...], v.folded[...].reshape(256, 128))
    lift, lift_turned = lift_wide.astype(B16), lift_wide.T.astype(B16)
    dcontext = dot_nt(lift, v.w_up[...]).astype(B16)
    mix_grad = dot_nt(dcontext, v.w_out[...]).astype(B16)
    put(v.a_g, 384, dot(lift_turned, v.mixed[...]))
    put(v.a_g, 448, dot(lift_turned, v.context[...]))
    attend_back(v, mix_grad, v.a_g, (0, 1))
    low[0]()
    attend_back(v, mix_grad, v.b_g, (2, 3))
    high[0]()
    low[1]()
    high[1]()
    for n in range(2, 9):
        low[n]()
        high[n]()
    wait_all(results)


def unpack_kernel(low, high, fine, quantiles, w_up, w_head_t, eye,
                  grad_qkv, grad_out, grad_up, grad_conv, grad_head, loss, fine_out, quantiles_out,
                  held, wide, square, tall, flat, fine_in, bands_in, sems):
    through = [(fine.at[pl.ds(n * 8, 8)], fine_in.at[pl.ds(n * 8, 8)], fine_out.at[pl.ds(n * 8, 8)]) for n in range(4)]
    through.append((quantiles, bands_in, quantiles_out))
    passing = [pltpu.make_async_copy(src, held, sems.at[12 + n]) for n, (src, held, _) in enumerate(through)]
    reads = [pltpu.make_async_copy((low, high)[h].at[pl.ds(a, b)], held.at[h, pl.ds(a, b)], sems.at[2 * n + h])
             for n, (a, b) in enumerate(((0, 384), (384, 128))) for h in range(2)]
    for c in reads[:2] + passing + reads[2:]:
        c.start()
    writes = []

    def write(src, dst, n):
        c = pltpu.make_async_copy(src, dst, sems.at[n])
        c.start()
        writes.append(c)

    for h in range(2):
        reads[h].wait()
        for n in range(3):
            for m in range(2):
                at = n * 128 + m * 64
                wide[n, :, h * 256 + m * 128:h * 256 + (m + 1) * 128] = held[h, at:at + 64].astype(F32).reshape(512, 128)
            if h == 1:
                write(wide.at[n], grad_qkv.at[:, pl.ds(n * 512, 512)], 6 + n)
        for m in ((0, 1, 2), (3, 4))[h]:
            passing[m].wait()
            write(through[m][1], through[m][2], 17 + m)
    reads[2].wait()
    reads[3].wait()
    for n in range(4):
        mixed = held[0, 384 + n * 16:384 + (n + 1) * 16].astype(F32).reshape(128, 128).T.astype(B16)
        square[n * 128:(n + 1) * 128] = dot_nt(mixed, w_up[...])
        tall[n * 128:(n + 1) * 128] = held[0, 448 + n * 16:448 + (n + 1) * 16].astype(F32).reshape(128, 128).T
    write(square, grad_out, 9)
    write(tall, grad_up, 10)
    head_t = dot(eye[...], w_head_t[...]).astype(B16)
    for a in range(3):
        for b in range(3):
            at = 384 + (2 - a) * 6 + (2 - b) * 2
            seen = held[1, at:at + 2].astype(F32).reshape(16, 128).T.astype(B16)
            flat[(a * 3 + b) * 128:(a * 3 + b + 1) * 128] = dot(seen, head_t)
    write(flat, grad_conv, 11)
    tail = held[1, 402:404].astype(F32).reshape(16, 128)
    grad_head[...] = tail[:QUANT]
    loss[...] = jnp.sum(tail[QUANT:QUANT + 1], axis=1, keepdims=True) * (1.0 / (1048576.0 * QUANT))
    wait_all(writes)


def body(fine_input, coarse, rain_bins, w_qkv, w_out, w_up, w_conv, w_head):
    group = group_table()
    eye = onehot(16, QUANT, [(q, q) for q in range(QUANT)])
    args = [coarse[0], fine_input[0], rain_bins[0], w_qkv, w_out, w_up, w_conv, w_head.T,
            mid_table(), group, group.T, back_table(), pick_table(0), pick_table(14), spread_table(0), spread_table(14),
            bins_table(), up_table(), sum_table(), eye]
    spaces = scratch()
    names = INPUTS + tuple(name for name, _, _ in OUTPUTS) + tuple(name for name, _ in spaces)
    vmem, anywhere = pl.BlockSpec(memory_space=pltpu.VMEM), pl.BlockSpec(memory_space=pl.ANY)

    def kernel(*refs):
        whole_kernel(names, *refs)

    quantiles, grad_fine, low, high = pl.pallas_call(
        kernel,
        out_shape=[jax.ShapeDtypeStruct(shape, dtype) for _, shape, dtype in OUTPUTS],
        in_specs=[pl.BlockSpec(memory_space=pl.ANY) if name in IN_HBM else vmem for name in INPUTS],
        out_specs=[anywhere, anywhere, vmem, vmem],
        scratch_shapes=[space for _, space in spaces],
        compiler_params=pltpu.CompilerParams(vmem_limit_bytes=LIMIT, collective_id=1, has_side_effects=True),
    )(*args)
    shapes = ((512, 1536), (512, 512), (512, 128), (1152, 128), (QUANT, 128), (1, 1), (32, 128, 128), (9, 32, 128))
    grad_qkv, grad_out, grad_up, grad_conv, grad_head, loss, fine, bands = pl.pallas_call(
        unpack_kernel,
        out_shape=[jax.ShapeDtypeStruct(shape, F32) for shape in shapes],
        in_specs=[anywhere] * 4 + [vmem] * 3,
        out_specs=[anywhere] * 4 + [vmem] * 2 + [anywhere] * 2,
        scratch_shapes=[pltpu.VMEM((2, HALF, 8, 128), B16), pltpu.VMEM((3, 512, 512), F32),
                        pltpu.VMEM((512, 512), F32), pltpu.VMEM((512, 128), F32), pltpu.VMEM((1152, 128), F32),
                        pltpu.VMEM((32, 128, 128), F32), pltpu.VMEM((9, 32, 128), F32), DMA((22,))],
        compiler_params=pltpu.CompilerParams(vmem_limit_bytes=LIMIT),
    )(low, high, grad_fine, quantiles, w_up, w_head.T, eye)
    return (bands[None], loss.reshape(()), grad_qkv, grad_out, grad_up, grad_conv.reshape(3, 3, 128, 128),
            grad_head.T, fine[None])


def solution(mesh):
    placed = (
        P("batch", "rows", "cols", None),
        P("batch", "rows", "cols", None),
        P("batch", "rows", "cols"),
        P(),
        P(),
        P(),
        P(),
        P(),
    )
    return jax.shard_map(
        body,
        mesh=mesh,
        in_specs=placed,
        out_specs=(
            P("batch", None, "rows", "cols"),
            P(),
            P(),
            P(),
            P(),
            P(),
            P(),
            P("batch", "rows", "cols", None),
        ),
        check_vma=False,
    )
```

```python
import jax
import jax.numpy as jnp
import numpy as np
from types import SimpleNamespace
from jax import lax
from jax.experimental import pallas as pl
from jax.experimental.pallas import tpu as pltpu
from jax.sharding import PartitionSpec as P

HEAD_DIM = 32
QUANT = 9
MESH = pl.DeviceIdType.MESH
F32, B16 = jnp.float32, jnp.bfloat16
DMA = pltpu.SemaphoreType.DMA
SCALE = HEAD_DIM ** (-0.5)
ROOT_2_PI = 0.7978845608028654
LIMIT = 58 * 1024 * 1024
HALF = 512


def onehot(rows, cols, pairs):
    table = np.zeros((rows, cols), np.float32)
    for row, col in pairs:
        table[row, col] = 1.0
    return jnp.asarray(table, B16)


def mid_table():
    return onehot(256, 256, [(p * 16 + r * 2 + m, r * 32 + p * 2 + m)
                             for p in range(16) for r in range(8) for m in range(2)])


def group_table():
    return onehot(256, 256, [(m * 128 + c * 8 + r, c * 16 + r * 2 + m)
                             for m in range(2) for c in range(16) for r in range(8)])


def cross_table():
    return onehot(256, 256, [(m * 128 + c * 8 + r, r * 32 + c * 2 + m)
                             for m in range(2) for c in range(16) for r in range(8)])


def back_table():
    pairs = []
    for r in range(8):
        for j in range(32):
            pairs.append((r * 48 + j, (1 + j // 2) * 16 + r * 2 + j % 2))
        pairs.append((r * 48 + 32, 17 * 16 + r * 2))
        pairs.append((r * 48 + 35, r * 2 + 1))
    return onehot(384, 288, pairs)


def pick_table(first):
    return onehot(16, 128, [(2 * i + s, 16 * i + first + s) for i in range(8) for s in range(2)])


def spread_table(first):
    return onehot(128, 16, [(16 * i + first + s, 2 * i + s) for i in range(8) for s in range(2)])


def bins_table():
    return onehot(48, 64, [(0, 15)] + [(1 + y, 16 + y) for y in range(32)] + [(33, 48)])


def up_table():
    return onehot(144, 48, [(p, p // 4) for p in range(144)])


def sum_table():
    return onehot(32, 128, [(p // 4, p) for p in range(128)])


def dot(a, b):
    return jnp.dot(a, b, preferred_element_type=F32)


def dot_nt(a, b):
    return lax.dot_general(a, b, (((1,), (1,)), ((), ())), preferred_element_type=F32)


def rcopy(src, dst, send, recv, to):
    return pltpu.make_async_remote_copy(src_ref=src, dst_ref=dst, send_sem=send, recv_sem=recv,
                                        device_id=to, device_id_type=MESH)


def wait_all(copies):
    for c in copies:
        c.wait()


def peer_order(axis, me):
    if axis == "rows":
        steps = [(2, 0), (2, 1), (1, 0), (3, 0), (1, 1), (3, 1), (0, 1)]
        return [((me // 2 + a) % 4) * 2 + (me + b) % 2 for a, b in steps]
    steps = [(a, b) for a in range(4) for b in range(4) if a + b > 0]
    steps.sort(key=lambda step: -min(step[0], 4 - step[0]) - min(step[1], 4 - step[1]))
    return [((me // 4 + a) % 4) * 4 + (me + b) % 4 for a, b in steps]


def scatter_out(axis, src, got, send, recv, me):
    copies = []
    for n, p in enumerate(peer_order(axis, me)):
        c = rcopy(src.at[p], got.at[me], send.at[n], recv.at[n], {axis: p})
        c.start()
        copies.append(c)
    return copies


def spread_out(axis, count, me, src, main, send, recv, send_x, recv_x):
    copies = []
    for n, p in enumerate(peer_order(axis, me)):
        c = rcopy(src.at[p], main.at[1 + me], send.at[n], recv.at[n], {axis: p})
        c.start()
        copies.append(c)
    main[1 + me] = src[me]

    def after(t):
        return rcopy(src.at[t - 1], main.at[0], send_x.at[t], recv_x.at[0], {axis: t})

    def before(t):
        return rcopy(src.at[t + 1], main.at[count + 1], send_x.at[t], recv_x.at[1], {axis: t})

    @pl.when(me == count - 1)
    def _():
        for t in range(1, count - 1):
            after(t).start()
        main[0] = src[count - 2]
        main[count + 1] = jnp.zeros(main.shape[1:], B16)

    @pl.when(me == 0)
    def _():
        for t in range(1, count - 1):
            before(t).start()
        main[count + 1] = src[1]
        main[0] = jnp.zeros(main.shape[1:], B16)

    def finish():
        @pl.when(me == count - 1)
        def _():
            for t in range(1, count - 1):
                after(t).wait_send()

        @pl.when(me == 0)
        def _():
            for t in range(1, count - 1):
                before(t).wait_send()

        @pl.when((me > 0) & (me < count - 1))
        def _():
            after(1).wait_recv()
            before(1).wait_recv()

        wait_all(copies)

    return finish


def head_mask(h):
    lane = lax.broadcasted_iota(jnp.int32, (1, 128), 1)
    return jnp.where((lane >> 5) == h, 1.0, 0.0).astype(B16)


def heads_down(tile):
    return jnp.concatenate([tile * head_mask(h) for h in range(4)], axis=0)


def heads_across(tile):
    turned = tile.astype(F32).T
    line = lax.broadcasted_iota(jnp.int32, (128, 1), 0) >> 5
    return jnp.concatenate([jnp.where(line == h, turned, 0.0) for h in range(4)], axis=1).astype(B16)


def side_by_side(stack):
    return jnp.concatenate([stack[h * 128:(h + 1) * 128] for h in range(4)], axis=1)


def put(g, at, value):
    rows, cols = value.shape
    size = rows // 8
    for n in range(cols // 128):
        g[at + n * size:at + (n + 1) * size] = value[:, n * 128:(n + 1) * 128].reshape(size, 8, 128).astype(B16)


def shifted(line):
    return jnp.concatenate([pltpu.roll(line, 1, 0), line, pltpu.roll(line, 143, 0)], axis=1)


def reducer(me, axes, units, g, out, got0, sum0, got1, sum1, got2, sum2, got3, sems):
    core, deep = me.core, me.deep
    (first, in_first), (second, in_second) = axes
    u0, u1, u2, u3 = units // 2, units // 8, units // 32, units // 256
    s0, r0, s1, r1, s2, r2, s3, r3, as3, ar3, as2, ar2, as1, ar1, as0, ar0 = sems
    place = core * u0 + first * u1 + second * u2
    held = {}

    def sum_up(terms):
        total = terms[0].astype(F32)
        for term in terms[1:]:
            total = total + term.astype(F32)
        return total

    def near_start():
        held["near"] = []
        for n, k in enumerate((1, 2, 3, 0)):
            p = (first + k) % 4
            c = rcopy(g.at[pl.ds((1 - core) * u0 + p * u1, u1)], got0.at[p], s0.at[n], r0.at[n], me.other)
            c.start()
            held["near"].append(c)

    def first_start():
        held["first"] = []
        for n, k in enumerate((1, 2, 3)):
            p = (first + k) % 4
            held["near"][n].wait_recv()
            sum0[p] = sum_up([g[pl.ds(core * u0 + p * u1, u1)], got0[p]]).astype(B16)
            c = rcopy(sum0.at[p], got1.at[k - 1], s1.at[k - 1], r1.at[k - 1], in_first(k))
            c.start()
            held["first"].append(c)
        held["near"][3].wait_recv()

    def second_start():
        wait_all(held["first"])
        sum1[...] = sum_up([g[pl.ds(core * u0 + first * u1, u1)], got0[first], got1[0], got1[1], got1[2]]).astype(B16)
        held["second"] = []
        for k in (1, 2, 3):
            p = (second + k) % 4
            c = rcopy(sum1.at[pl.ds(p * u2, u2)], got2.at[k - 1], s2.at[k - 1], r2.at[k - 1], in_second(k))
            c.start()
            held["second"].append(c)
        for c in held["near"]:
            c.wait_send()

    def deep_start():
        wait_all(held["second"])
        sum2[...] = sum_up([sum1[pl.ds(second * u2, u2)], got2[0], got2[1], got2[2]]).astype(B16)
        held["deep"] = []
        for k in (4, 3, 5, 2, 6, 1, 7):
            p = (deep + k) % 8
            c = rcopy(sum2.at[pl.ds(p * u3, u3)], got3.at[k - 1], s3.at[k - 1], r3.at[k - 1], me.in_deep(k))
            c.start()
            held["deep"].append(c)

    def deep_gather():
        wait_all(held["deep"])
        mine = sum_up([sum2[pl.ds(deep * u3, u3)]] + [got3[k] for k in range(7)])
        out[pl.ds(place + deep * u3, u3)] = mine.astype(B16)
        block = out.at[pl.ds(place + deep * u3, u3)]
        held["deep"] = []
        for k in (4, 3, 5, 2, 6, 1, 7):
            c = rcopy(block, block, as3.at[k - 1], ar3.at[k - 1], me.in_deep(k))
            c.start()
            held["deep"].append(c)

    def second_gather():
        wait_all(held["deep"])
        block = out.at[pl.ds(place, u2)]
        held["second"] = []
        for k in (1, 2, 3):
            c = rcopy(block, block, as2.at[k - 1], ar2.at[k - 1], in_second(k))
            c.start()
            held["second"].append(c)

    def forward(n, p):
        block = out.at[pl.ds(core * u0 + p * u1, u1)]
        c = rcopy(block, block, as0.at[n], ar0.at[n], me.other)
        c.start()
        held["near"].append(c)

    def first_gather():
        wait_all(held["second"])
        block = out.at[pl.ds(core * u0 + first * u1, u1)]
        held["first"], held["near"] = [], []
        for k in (1, 2, 3):
            c = rcopy(block, block, as1.at[k - 1], ar1.at[k - 1], in_first(k))
            c.start()
            held["first"].append(c)
        forward(0, first)

    def near_gather():
        for k in (1, 2, 3):
            held["first"][k - 1].wait_recv()
            forward(k, (first + 4 - k) % 4)

    def finish():
        for c in held["first"]:
            c.wait_send()
        wait_all(held["near"])

    return [near_start, first_start, second_start, deep_start, deep_gather, second_gather, first_gather,
            near_gather, finish]


def reducer_scratch(tag, units):
    unit = (8, 128)
    u1, u2, u3 = units // 8, units // 32, units // 256
    shapes = [("g", (units,) + unit), ("got0", (4, u1) + unit), ("sum0", (4, u1) + unit), ("got1", (3, u1) + unit),
              ("sum1", (u1,) + unit), ("got2", (3, u2) + unit), ("sum2", (u2,) + unit), ("got3", (7, u3) + unit)]
    result = [(tag + name, pltpu.VMEM(shape, B16)) for name, shape in shapes]
    for n, count in enumerate((4, 4, 3, 3, 3, 3, 7, 7, 7, 7, 3, 3, 3, 3, 4, 4)):
        result.append((tag + "sem" + str(n), DMA((count,))))
    return result


INPUTS = ("coarse", "fine", "bins", "w_qkv_in", "w_out_in", "w_up_in", "w_conv_in", "w_head_t",
          "turns_in", "back_in", "pick_lo", "pick_hi", "spread_lo", "spread_hi", "place", "up", "fold", "eye")
IN_HBM = ("coarse", "fine", "w_qkv_in", "w_out_in", "w_up_in", "w_conv_in", "turns_in", "back_in")
OUTPUTS = (("quantiles_out", (9, 32, 128), F32), ("grad_fine_out", (32, 128, 128), F32),
           ("low_half", (HALF, 8, 128), B16), ("high_half", (HALF, 8, 128), B16))


def scratch():
    buffers = [
        ("w_qkv", (512, 1536), B16), ("w_out", (512, 512), B16), ("w_conv", (3, 3, 128, 128), B16),
        ("w_up", (512, 128), B16), ("turns", (5, 256, 256), B16), ("back", (384, 288), B16),
        ("got", (8, 32, 256), B16), ("turned", (16, 16, 256), B16), ("tokens", (16, 16, 256), B16),
        ("half", (8, 32, 256), B16), ("half_turned", (16, 16, 256), B16), ("half_got", (16, 16, 256), B16),
        ("half_cross", (8, 32, 256), B16), ("half_tokens", (8, 32, 256), B16),
        ("field", (40, 144, 128), B16), ("bins16", (32, 128), B16), ("bin_got", (64, 128), B16),
        ("edge_out", (2, 5, 16, 128), B16), ("edge_in", (2, 5, 16, 128), B16), ("bin_out", (2, 48, 128), B16),
        ("bin_in", (2, 48, 128), B16), ("rain", (48, 128), F32), ("edge_bins", (16, 128), F32),
        ("tok", (256, 512), B16), ("qkv", (256, 1536), B16), ("prob", (8, 512, 128), F32), ("mixed", (256, 512), B16),
        ("context", (256, 512), B16), ("raised", (16, 16, 128), B16),
        ("slots", (18, 16, 128), B16), ("lift_turned", (8, 48, 128), B16), ("lifted", (10, 48, 128), B16),
        ("query_turned", (8, 128, 512), B16), ("tok_turned", (512, 256), B16),
        ("hidden", (40, 144, 128), F32), ("slope", (40, 128, 128), F32), ("active", (40, 144, 384), B16),
        ("outer", (36, 144, 128), B16), ("taps", (36, 48, 128), B16), ("taps_turned", (36, 128, 48), B16),
        ("back_low", (48, 128), B16), ("back_mid", (48, 256), B16), ("back_high", (48, 128), B16),
        ("tap_sum", (144, 128), F32), ("pair", (1536, 256), B16), ("loss_sum", (16, 128), F32), ("head_sum", (16, 128), F32),
        ("dlift", (8, 32, 128), B16), ("grad_fine", (32, 128, 128), F32), ("quantiles", (9, 32, 128), F32),
        ("fold_got", (8, 32, 128), B16), ("fold_turned", (16, 16, 128), B16), ("folded", (16, 16, 128), B16),
        ("dquery", (256, 512), B16), ("dkey", (512, 256), B16), ("dvalue", (512, 256), B16),
    ]
    sems = [("s_l", 11), ("s_ur", 7), ("r_ur", 7), ("s_uc", 15), ("r_uc", 15), ("s_tr", 7), ("r_tr", 7), ("s_tc", 15), ("r_tc", 15), ("s_h", 4), ("r_h", 4), ("s_e", 4), ("r_e", 4),
            ("s_lc", 15), ("r_lc", 15), ("s_lx", 16), ("r_lx", 2), ("s_lr", 7), ("r_lr", 7), ("s_ly", 8), ("r_ly", 2),
            ("s_fr", 8), ("r_fr", 8), ("s_fc", 15), ("r_fc", 15)]
    return ([(name, pltpu.VMEM(shape, dtype)) for name, shape, dtype in buffers]
            + [(name, DMA((count,))) for name, count in sems]
            + reducer_scratch("a_", HALF) + reducer_scratch("b_", HALF))


def halo_rows(v, row):
    sends = [
        ((v.fine.at[pl.ds(30, 2)], v.field.at[pl.ds(2, 2), pl.ds(0, 128)], v.s_h.at[0], v.r_h.at[0]),
         (v.bins16.at[pl.ds(16, 16)], v.bin_got.at[pl.ds(0, 16)], v.s_h.at[1], v.r_h.at[1])),
        ((v.fine.at[pl.ds(0, 2)], v.field.at[pl.ds(36, 2), pl.ds(0, 128)], v.s_h.at[2], v.r_h.at[2]),
         (v.bins16.at[pl.ds(0, 16)], v.bin_got.at[pl.ds(48, 16)], v.s_h.at[3], v.r_h.at[3])),
    ]

    def start():
        @pl.when(row < 7)
        def _():
            for args in sends[0]:
                rcopy(*args, {"rows": row + 1}).start()

        @pl.when(row > 0)
        def _():
            for args in sends[1]:
                rcopy(*args, {"rows": row - 1}).start()

    def finish():
        @pl.when(row < 7)
        def _():
            for args in sends[0]:
                rcopy(*args, {"rows": row + 1}).wait_send()
            for args in sends[1]:
                rcopy(*args, {"rows": row + 1}).wait_recv()

        @pl.when(row > 0)
        def _():
            for args in sends[1]:
                rcopy(*args, {"rows": row - 1}).wait_send()
            for args in sends[0]:
                rcopy(*args, {"rows": row - 1}).wait_recv()

    return start, finish


def halo_cols(v, col):
    sends = [((v.edge_out.at[n], v.edge_in.at[n], v.s_e.at[2 * n], v.r_e.at[2 * n]),
              (v.bin_out.at[n], v.bin_in.at[n], v.s_e.at[2 * n + 1], v.r_e.at[2 * n + 1])) for n in range(2)]

    def start():
        @pl.when(col < 15)
        def _():
            for args in sends[0]:
                rcopy(*args, {"cols": col + 1}).start()

        @pl.when(col > 0)
        def _():
            for args in sends[1]:
                rcopy(*args, {"cols": col - 1}).start()

    def finish():
        @pl.when(col < 15)
        def _():
            for args in sends[0]:
                rcopy(*args, {"cols": col + 1}).wait_send()
            for args in sends[1]:
                rcopy(*args, {"cols": col + 1}).wait_recv()

        @pl.when(col > 0)
        def _():
            for args in sends[1]:
                rcopy(*args, {"cols": col - 1}).wait_send()
            for args in sends[0]:
                rcopy(*args, {"cols": col - 1}).wait_recv()

    return start, finish


def exchange_tokens(v, row, col, loads):
    low = [rcopy(v.coarse.at[p, :, pl.ds(0, 256)], v.got.at[row], v.s_tr.at[n], v.r_tr.at[n], {"rows": p})
           for n, p in enumerate(peer_order("rows", row))]
    for c in low:
        c.start()
    high = scatter_out("cols", v.half_turned, v.half_got, v.s_uc, v.r_uc, col)
    own = pltpu.make_async_copy(v.coarse.at[row, :, pl.ds(0, 256)], v.got.at[row], v.s_l.at[0])
    own.start()
    v.half_got[col] = v.half_turned[col]
    rows_start, rows_finish = halo_rows(v, row)
    rows_start()

    @pl.when(row == 0)
    def _():
        v.field[pl.ds(2, 2), :128] = jnp.zeros((2, 128, 128), B16)
        v.bin_got[pl.ds(0, 16)] = jnp.zeros((16, 128), B16)

    @pl.when(row == 7)
    def _():
        v.field[pl.ds(36, 2), :128] = jnp.zeros((2, 128, 128), B16)
        v.bin_got[pl.ds(48, 16)] = jnp.zeros((16, 128), B16)

    v.field[pl.ds(0, 2), :128] = jnp.zeros((2, 128, 128), B16)
    v.field[pl.ds(38, 2), :128] = jnp.zeros((2, 128, 128), B16)
    v.bin_got[pl.ds(16, 32)] = v.bins16[...]

    own.wait()
    wait_all(high)
    v.half_cross[...] = dot(v.turns[1], v.half_got[...].reshape(256, 256)).astype(B16).reshape(8, 32, 256)
    high = scatter_out("rows", v.half_cross, v.half_tokens, v.s_ur, v.r_ur, row)
    v.half_tokens[row] = v.half_cross[row]
    wait_all(low)
    v.turned[...] = dot(v.turns[0], v.got[...].reshape(256, 256)).astype(B16).reshape(16, 16, 256)
    low = scatter_out("cols", v.turned, v.tokens, v.s_tc, v.r_tc, col)
    v.tokens[col] = v.turned[col]

    loads[0].wait()
    rows_finish()
    rows = dot(v.place[...], v.bin_got[...])
    v.rain[...] = rows
    v.bin_out[0] = jnp.broadcast_to(rows[:, 127:128], (48, 128)).astype(B16)
    v.bin_out[1] = jnp.broadcast_to(rows[:, 0:1], (48, 128)).astype(B16)
    for q in range(5):
        v.edge_out[0, q] = dot(v.pick_hi[...], v.field[8 * q:8 * q + 8, 112:128].reshape(128, 128)).astype(B16)
        v.edge_out[1, q] = dot(v.pick_lo[...], v.field[8 * q:8 * q + 8, 0:16].reshape(128, 128)).astype(B16)
    cols_start, cols_finish = halo_cols(v, col)
    cols_start()

    @pl.when(col == 0)
    def _():
        v.edge_in[0] = jnp.zeros((5, 16, 128), B16)
        v.bin_in[0] = jnp.zeros((48, 128), B16)

    @pl.when(col == 15)
    def _():
        v.edge_in[1] = jnp.zeros((5, 16, 128), B16)
        v.bin_in[1] = jnp.zeros((48, 128), B16)

    wait_all(low)
    wait_all(high)
    return cols_finish


def attend(v):
    v.tok[:, :256] = dot(v.turns[2], v.tokens[...].reshape(256, 256)).astype(B16)
    v.tok[:, 256:] = dot(v.turns[3], v.half_tokens[...].reshape(256, 256)).astype(B16)
    for n in range(3):
        v.qkv[:, n * 512:(n + 1) * 512] = dot(v.tok[...], v.w_qkv[:, n * 512:(n + 1) * 512]).astype(B16)
    for g in range(2):
        for t in range(4):
            rows, at = slice(g * 128, g * 128 + 128), t * 128
            query = v.qkv[rows, at:at + 128]
            keyed = v.qkv[rows, 512 + at:512 + at + 128]
            valued = v.qkv[rows, 1024 + at:1024 + at + 128]
            scores = dot_nt(heads_down(query), keyed) * SCALE
            peak = jnp.max(scores, axis=-1, keepdims=True)
            powers = jnp.exp(scores - peak)
            share = powers / jnp.sum(powers, axis=-1, keepdims=True)
            v.prob[g * 4 + t] = share
            v.mixed[rows, at:at + 128] = dot(side_by_side(share.astype(B16)), heads_down(valued)).astype(B16)
    attended = dot(v.mixed[...], v.w_out[...]).astype(B16)
    v.context[...] = (v.tok[...].astype(F32) + attended.astype(F32)).astype(B16)
    lifted = dot(v.context[...], v.w_up[...]).astype(B16)
    v.raised[...] = dot(v.turns[4], lifted).astype(B16).reshape(16, 16, 128)


def edge_targets(v):
    lane = lax.broadcasted_iota(jnp.int32, (48, 128), 1)
    line = lax.broadcasted_iota(jnp.int32, (48, 128), 0)
    low, high = v.bin_in[0].astype(F32), v.bin_in[1].astype(F32)
    picked = jnp.where((lane & 15) == 0, high, jnp.where((lane & 15) == 15, low, 0.0))
    for b in range(9):
        here = line == 4 * b + (lane >> 4)
        v.edge_bins[b:b + 1] = jnp.sum(jnp.where(here, picked, 0.0), axis=0, keepdims=True)


def fold_copy(v, row, target, source):
    return rcopy(v.dlift.at[target], v.fold_got.at[source], v.s_fr.at[target], v.r_fr.at[source], {"rows": target})


def send_fold(v, row, target):
    @pl.when(row != target)
    def _():
        fold_copy(v, row, target, row).start()


def convolve(v, row, col):
    head_t = dot(v.eye[...], v.w_head_t[...]).astype(B16)
    place = lax.broadcasted_iota(jnp.int32, (144, 1), 0)
    right = jnp.where(col < 15, 130, 128)
    left = jnp.where(col > 0, 142, 144)
    inside = (place < right) | (place >= left)
    level = (lax.broadcasted_iota(jnp.int32, (16, 1), 0) + 1).astype(F32) / 10.0
    quant = lax.broadcasted_iota(jnp.int32, (16, 1), 0) < QUANT
    v.loss_sum[...] = jnp.zeros((16, 128), F32)
    v.head_sum[...] = jnp.zeros((16, 128), F32)
    v.tap_sum[...] = jnp.zeros((144, 128), F32)
    v.active[pl.ds(38, 2)] = jnp.zeros((2, 144, 384), B16)
    v.hidden[pl.ds(38, 2)] = jnp.zeros((2, 144, 128), F32)

    def start(i):
        raised = dot(v.up[...], v.lifted[i])
        rims = {0: (2, 3), 9: (0, 1)}.get(i, range(4)) if isinstance(i, int) else range(4)
        for s in rims:
            y = 4 * i + s - 4
            x = v.field[4 * i + s].astype(F32) + raised
            square = x * x
            bend = jnp.tanh(ROOT_2_PI * x * (1.0 + 0.044715 * square))
            half = 0.5 * (1.0 + bend)
            act = x * half
            if isinstance(i, int) and i in (0, 9):
                act = jnp.where(inside & (row * 32 + y >= 0) & (row * 32 + y < 256), act, 0.0)
            else:
                act = jnp.concatenate([act[:128], jnp.where(inside[128:], act[128:], 0.0)], axis=0)
            v.hidden[4 * i + s] = x
            v.active[4 * i + s] = shifted(act).astype(B16)
            v.slope[4 * i + s] = half[:128] + (0.5 * ROOT_2_PI) * x[:128] * (1.0 - bend[:128] * bend[:128]) * (
                1.0 + (3 * 0.044715) * square[:128])

    def forward(i):
        windows = [jnp.concatenate([v.active[4 * i + 2 + a], v.active[4 * i + 4 + a]], axis=0) for a in range(4)]
        both = dot(jnp.concatenate(windows, axis=1), v.pair[...])
        for s in range(4):
            at, part = s // 2 * 144, s % 2 * 128
            v.outer[4 * i + s] = (v.hidden[4 * i + 3 + s] + both[at:at + 144, part:part + 128]).astype(B16)

    def turn(i):
        own = v.outer[pl.ds(4 * i, 4), :128].reshape(512, 128)
        edge = v.outer[pl.ds(4 * i, 4), 128:144].reshape(64, 128)
        pixels = jnp.concatenate([own, edge, jnp.zeros((64, 128), B16)], axis=0)
        predicted = dot_nt(head_t, pixels)
        lines = [v.rain[pl.ds(4 * i + s, 1), :] for s in range(4)] + [v.edge_bins[pl.ds(i, 1), :]]
        target = jnp.concatenate(lines, axis=1) * (1.0 / 16.0) - 1.0
        lane = lax.broadcasted_iota(jnp.int32, (1, 640), 1)
        spot = lane - 512
        inner = lane < 512
        y = 4 * i - 1 + jnp.where(inner, lane >> 7, spot >> 4)
        side = (((spot & 15) == 0) & (col < 15)) | (((spot & 15) == 15) & (col > 0))
        seen = (row * 32 + y >= 0) & (row * 32 + y < 256) & (y < 33) & (inner | (side & (spot < 64)))
        mine = inner & (y >= 0) & (y < 32)
        error = target - predicted
        weight = jnp.where(error < 0.0, 1.0 - level, level)
        down = jnp.where(seen & quant, -weight * jnp.clip(error, -1.0, 1.0) * (1.0 / 1024.0), 0.0)
        size = jnp.abs(error)
        loss = weight * jnp.where(size <= 1.0, 0.5 * error * error, size - 0.5)
        loss = jnp.where(mine & quant, loss, 0.0)
        v.loss_sum[...] += loss[:, :128] + loss[:, 128:256] + loss[:, 256:384] + loss[:, 384:512]
        v.head_sum[...] += dot(jnp.where(mine, down, 0.0).astype(B16)[:, :512], own)
        edge = down[:, 512:]
        at = lax.broadcasted_iota(jnp.int32, (1, 128), 1)
        sets = []
        for s in range(4):
            line = down[:, s * 128:(s + 1) * 128]
            before = jnp.where(at == 0, pltpu.roll(edge, 113 - 16 * s, 1), pltpu.roll(line, 1, 1))
            after = jnp.where(at == 127, pltpu.roll(edge, 127 - 16 * s, 1), pltpu.roll(line, 127, 1))
            sets.append(jnp.concatenate([before, line, after], axis=0))
            v.taps[4 * i + s] = sets[s].astype(B16)
            row_y = 4 * i + s - 1
            value = predicted[:, s * 128:(s + 1) * 128]
            if not isinstance(i, int) or 0 <= row_y < 32:
                for q in range(QUANT):
                    v.quantiles[q, pl.ds(row_y, 1), :] = value[q:q + 1]
        v.taps_turned[pl.ds(4 * i, 4)] = jnp.concatenate(sets, axis=1).T.astype(B16).reshape(4, 128, 48)

    def back(i):
        windows = [v.taps_turned[pl.ds(4 * i + a, 4)].reshape(512, 48) for a in range(3)]
        both = dot(windows[1], v.back_mid[...])
        dactive = both[:, :128] + dot(windows[0], v.back_low[...]) + dot(windows[2], v.back_high[...])
        dhidden = (both[:, 128:] + v.slope[pl.ds(4 * i + 4, 4)].reshape(512, 128) * dactive).reshape(4, 128, 128)
        v.grad_fine[pl.ds(4 * i, 4)] = dhidden * 1024.0
        summed = dhidden[0] + dhidden[1] + dhidden[2] + dhidden[3]
        high = summed.astype(B16)
        low = (summed - high.astype(F32)).astype(B16)
        v.dlift[i] = (dot(v.fold[...], high) + dot(v.fold[...], low)).astype(B16)
        lines = [jnp.concatenate([v.taps[4 * i + a + s] for s in range(4)], axis=1) for a in range(3)]
        seen = v.active[pl.ds(4 * i + 4, 4), :128, 128:256].reshape(512, 128)
        v.tap_sum[...] += dot(jnp.concatenate(lines, axis=0), seen)

    def step(t):
        known = isinstance(t, int)
        if not known or 0 <= t - 5 <= 7:
            back(t - 5)
        if not known or 0 <= t - 3 <= 8:
            turn(t - 3)
        if not known or 0 <= t - 2 <= 8:
            forward(t - 2)
        if not known or t <= 9:
            start(t)

    for t in range(5):
        step(t)

    def loop(t, carry):
        step(t)
        return carry

    lax.fori_loop(5, 9, loop, 0)
    for n in range(4):
        send_fold(v, row, n)
    for t in range(9, 13):
        step(t)
        send_fold(v, row, t - 5)


def back_weights(v):
    head_t = dot(v.eye[...], v.w_head_t[...]).astype(B16)
    for a, name in enumerate(("back_low", "back_mid", "back_high")):
        parts = [dot_nt(head_t, v.w_conv[2 - a, 2 - b]).astype(B16) for b in range(3)]
        getattr(v, name)[:, :128] = jnp.concatenate(parts, axis=0)
    for a in range(4):
        for b in range(2):
            block = v.w_conv[a - b].reshape(384, 128) if 0 <= a - b < 3 else jnp.zeros((384, 128), B16)
            v.pair[a * 384:(a + 1) * 384, b * 128:(b + 1) * 128] = block
    blank = jnp.zeros((16, 128), B16)
    v.back_mid[:, 128:] = jnp.concatenate([blank, head_t, blank], axis=0)


def local_units(v):
    v.b_g[384:402] = v.tap_sum[...].reshape(18, 8, 128).astype(B16)
    spot = lax.broadcasted_iota(jnp.int32, (16, 1), 0)
    total = jnp.sum(v.loss_sum[...], axis=0, keepdims=True)
    tail = jnp.where(spot < QUANT, v.head_sum[...], jnp.where(spot == QUANT, total, 0.0))
    v.b_g[402:404] = tail.reshape(2, 8, 128).astype(B16)
    v.b_g[404:HALF] = jnp.zeros((HALF - 404, 8, 128), B16)


def attend_back(v, mix_grad, g, tiles):
    for s, t in [(s, t) for s in range(2) for t in tiles]:
        rows, at = slice(s * 128, s * 128 + 128), t * 128
        keyed = v.qkv[rows, 512 + at:512 + at + 128]
        valued = v.qkv[rows, 1024 + at:1024 + at + 128]
        mine = mix_grad[rows, at:at + 128]
        dprob = dot_nt(heads_down(mine), valued)
        share = v.prob[s * 4 + t]
        inner = jnp.sum(share * dprob, axis=-1, keepdims=True)
        dscore = (share * (dprob - inner) * SCALE).astype(B16)
        v.dquery[rows, at:at + 128] = dot(side_by_side(dscore), heads_down(keyed)).astype(B16)
        v.dkey[at:at + 128, rows] = dot(v.query_turned[s * 4 + t], dscore).astype(B16)
        v.dvalue[at:at + 128, rows] = dot(heads_across(mine), share.astype(B16)).astype(B16)
    at = tiles[0] * 128
    put(g, 0, dot(v.tok_turned[...], v.dquery[:, at:at + 256]))
    put(g, 128, dot_nt(v.tok_turned[...], v.dkey[at:at + 256]))
    put(g, 256, dot_nt(v.tok_turned[...], v.dvalue[at:at + 256]))


def whole_kernel(names, *refs):
    v = SimpleNamespace(**dict(zip(names, refs)))
    row, col, batch = lax.axis_index("rows"), lax.axis_index("cols"), lax.axis_index("batch")
    core, deep = row % 2, (row // 2) * 2 + batch
    x, y = col // 4, col % 4
    me = SimpleNamespace(
        core=core, deep=deep, other={"rows": row + 1 - 2 * core},
    )
    x_axis = (x, lambda k: {"cols": ((x + k) % 4) * 4 + y})
    y_axis = (y, lambda k: {"cols": x * 4 + (y + k) % 4})

    def in_deep(k):
        p = (deep + k) % 8
        return {"rows": (p // 2) * 2 + core, "batch": p % 2}

    me.in_deep = in_deep

    peers = [{"rows": p} for p in peer_order("rows", row)]
    peers = peers[:2] + [{"rows": (row + 2 * k) % 8, "batch": 1 - batch} for k in (2, 1, 3, 0)] + peers[2:6] + [
        {"cols": p} for p in peer_order("cols", col)] + peers[6:]
    barrier = pltpu.get_barrier_semaphore()
    for peer in peers:
        pl.semaphore_signal(barrier, inc=1, device_id=peer, device_id_type=MESH)
    loads = [pltpu.make_async_copy(v.fine, v.field.at[pl.ds(4, 32), pl.ds(0, 128)], v.s_l.at[1]),
             pltpu.make_async_copy(v.w_qkv_in, v.w_qkv, v.s_l.at[2]),
             pltpu.make_async_copy(v.w_out_in, v.w_out, v.s_l.at[3]),
             pltpu.make_async_copy(v.w_conv_in, v.w_conv, v.s_l.at[4]),
             pltpu.make_async_copy(v.coarse.at[:, :, pl.ds(256, 256)], v.half, v.s_l.at[7]),
             pltpu.make_async_copy(v.turns_in, v.turns, v.s_l.at[8]),
             pltpu.make_async_copy(v.w_up_in, v.w_up, v.s_l.at[9]),
             pltpu.make_async_copy(v.back_in, v.back, v.s_l.at[10])]
    for n in (4, 5, 0, 1, 2, 6, 3, 7):
        loads[n].start()
    v.bins16[...] = v.bins[...].astype(F32).astype(B16)
    loads[4].wait()
    loads[5].wait()
    v.half_turned[...] = dot(v.turns[0], v.half[...].reshape(256, 256)).astype(B16).reshape(16, 16, 256)
    pl.semaphore_wait(barrier, len(peers))
    cols_finish = exchange_tokens(v, row, col, loads)
    loads[1].wait()
    loads[2].wait()
    loads[6].wait()
    loads[7].wait()
    attend(v)

    finish = spread_out("cols", 16, col, v.raised, v.slots, v.s_lc, v.r_lc, v.s_lx, v.r_lx)
    cols_finish()
    for q in range(5):
        edge = dot(v.spread_hi[...], v.edge_in[0, q]) + dot(v.spread_lo[...], v.edge_in[1, q])
        v.field[8 * q:8 * q + 8, 128:144] = edge.astype(B16).reshape(8, 16, 128)
    edge_targets(v)
    for s in range(2):
        for t in range(4):
            v.query_turned[s * 4 + t] = heads_across(v.qkv[s * 128:s * 128 + 128, t * 128:t * 128 + 128])
    finish()
    v.lift_turned[...] = dot(v.back[...], v.slots[...].reshape(288, 128)).astype(B16).reshape(8, 48, 128)
    finish = spread_out("rows", 8, row, v.lift_turned, v.lifted, v.s_lr, v.r_lr, v.s_ly, v.r_ly)
    v.tok_turned[...] = v.tok[...].astype(F32).T.astype(B16)
    loads[3].wait()
    back_weights(v)
    finish()

    convolve(v, row, col)

    results = [pltpu.make_async_copy(v.grad_fine, v.grad_fine_out, v.s_l.at[5]),
               pltpu.make_async_copy(v.quantiles, v.quantiles_out, v.s_l.at[6])]
    v.fold_got[row] = v.dlift[row]
    for c in results:
        c.start()
    local_units(v)
    for p in peer_order("rows", row):
        fold_copy(v, row, p, p).wait()
    v.fold_turned[...] = dot(v.turns[0], v.fold_got[...].reshape(256, 128)).astype(B16).reshape(16, 16, 128)
    sends = scatter_out("cols", v.fold_turned, v.folded, v.s_fc, v.r_fc, col)
    v.folded[col] = v.fold_turned[col]
    wait_all(sends)

    low = reducer(me, (x_axis, y_axis), HALF, v.a_g, v.low_half, v.a_got0, v.a_sum0, v.a_got1, v.a_sum1, v.a_got2, v.a_sum2,
                  v.a_got3, [getattr(v, "a_sem" + str(n)) for n in range(16)])
    high = reducer(me, (y_axis, x_axis), HALF, v.b_g, v.high_half, v.b_got0, v.b_sum0, v.b_got1, v.b_sum1, v.b_got2, v.b_sum2,
                   v.b_got3, [getattr(v, "b_sem" + str(n)) for n in range(16)])
    lift_wide = dot(v.turns[2], v.folded[...].reshape(256, 128))
    lift, lift_turned = lift_wide.astype(B16), lift_wide.T.astype(B16)
    dcontext = dot_nt(lift, v.w_up[...]).astype(B16)
    mix_grad = dot_nt(dcontext, v.w_out[...]).astype(B16)
    put(v.a_g, 384, dot(lift_turned, v.mixed[...]))
    put(v.a_g, 448, dot(lift_turned, v.context[...]))
    attend_back(v, mix_grad, v.a_g, (0, 1))
    low[0]()
    attend_back(v, mix_grad, v.b_g, (2, 3))
    high[0]()
    low[1]()
    high[1]()
    for n in range(2, 9):
        low[n]()
        high[n]()
    wait_all(results)


def unpack_kernel(low, high, fine, quantiles, w_up, w_head_t, eye,
                  grad_qkv, grad_out, grad_up, grad_conv, grad_head, loss, fine_out, quantiles_out,
                  held, wide, square, tall, flat, fine_in, bands_in, sems):
    through = [(fine.at[pl.ds(n * 8, 8)], fine_in.at[pl.ds(n * 8, 8)], fine_out.at[pl.ds(n * 8, 8)]) for n in range(4)]
    through.append((quantiles, bands_in, quantiles_out))
    passing = [pltpu.make_async_copy(src, held, sems.at[12 + n]) for n, (src, held, _) in enumerate(through)]
    reads = [pltpu.make_async_copy((low, high)[h].at[pl.ds(a, b)], held.at[h, pl.ds(a, b)], sems.at[2 * n + h])
             for n, (a, b) in enumerate(((0, 384), (384, 128))) for h in range(2)]
    for c in reads[2:] + reads[:2] + passing:
        c.start()
    writes = []

    def write(src, dst, n):
        c = pltpu.make_async_copy(src, dst, sems.at[n])
        c.start()
        writes.append(c)

    reads[2].wait()
    reads[3].wait()
    for n in range(4):
        mixed = held[0, 384 + n * 16:384 + (n + 1) * 16].astype(F32).reshape(128, 128).T.astype(B16)
        square[n * 128:(n + 1) * 128] = dot_nt(mixed, w_up[...])
        tall[n * 128:(n + 1) * 128] = held[0, 448 + n * 16:448 + (n + 1) * 16].astype(F32).reshape(128, 128).T
    write(square, grad_out, 9)
    write(tall, grad_up, 10)
    head_t = dot(eye[...], w_head_t[...]).astype(B16)
    for a in range(3):
        for b in range(3):
            at = 384 + (2 - a) * 6 + (2 - b) * 2
            seen = held[1, at:at + 2].astype(F32).reshape(16, 128).T.astype(B16)
            flat[(a * 3 + b) * 128:(a * 3 + b + 1) * 128] = dot(seen, head_t)
    write(flat, grad_conv, 11)
    for h in range(2):
        reads[h].wait()
        for n in range(3):
            for m in range(2):
                at = n * 128 + m * 64
                wide[n, :, h * 256 + m * 128:h * 256 + (m + 1) * 128] = held[h, at:at + 64].astype(F32).reshape(512, 128)
            if h == 1:
                write(wide.at[n], grad_qkv.at[:, pl.ds(n * 512, 512)], 6 + n)
        for m in ((0, 1, 2), (3, 4))[h]:
            passing[m].wait()
            write(through[m][1], through[m][2], 17 + m)
    tail = held[1, 402:404].astype(F32).reshape(16, 128)
    grad_head[...] = tail[:QUANT]
    loss[...] = jnp.sum(tail[QUANT:QUANT + 1], axis=1, keepdims=True) * (1.0 / (1048576.0 * QUANT))
    wait_all(writes)


def body(fine_input, coarse, rain_bins, w_qkv, w_out, w_up, w_conv, w_head):
    mid, group = mid_table(), group_table()
    turns = jnp.stack([mid, mid.T, group, cross_table(), group.T])
    eye = onehot(16, QUANT, [(q, q) for q in range(QUANT)])
    args = [coarse[0], fine_input[0], rain_bins[0], w_qkv, w_out, w_up, w_conv, w_head.T,
            turns, back_table(), pick_table(0), pick_table(14), spread_table(0), spread_table(14),
            bins_table(), up_table(), sum_table(), eye]
    spaces = scratch()
    names = INPUTS + tuple(name for name, _, _ in OUTPUTS) + tuple(name for name, _ in spaces)
    vmem, anywhere = pl.BlockSpec(memory_space=pltpu.VMEM), pl.BlockSpec(memory_space=pl.ANY)

    def kernel(*refs):
        whole_kernel(names, *refs)

    quantiles, grad_fine, low, high = pl.pallas_call(
        kernel,
        out_shape=[jax.ShapeDtypeStruct(shape, dtype) for _, shape, dtype in OUTPUTS],
        in_specs=[pl.BlockSpec(memory_space=pl.ANY) if name in IN_HBM else vmem for name in INPUTS],
        out_specs=[anywhere, anywhere, vmem, vmem],
        scratch_shapes=[space for _, space in spaces],
        compiler_params=pltpu.CompilerParams(vmem_limit_bytes=LIMIT, collective_id=1, has_side_effects=True),
    )(*args)
    shapes = ((512, 1536), (512, 512), (512, 128), (1152, 128), (QUANT, 128), (1, 1), (32, 128, 128), (9, 32, 128))
    grad_qkv, grad_out, grad_up, grad_conv, grad_head, loss, fine, bands = pl.pallas_call(
        unpack_kernel,
        out_shape=[jax.ShapeDtypeStruct(shape, F32) for shape in shapes],
        in_specs=[anywhere] * 4 + [vmem] * 3,
        out_specs=[anywhere] * 4 + [vmem] * 2 + [anywhere] * 2,
        scratch_shapes=[pltpu.VMEM((2, HALF, 8, 128), B16), pltpu.VMEM((3, 512, 512), F32),
                        pltpu.VMEM((512, 512), F32), pltpu.VMEM((512, 128), F32), pltpu.VMEM((1152, 128), F32),
                        pltpu.VMEM((32, 128, 128), F32), pltpu.VMEM((9, 32, 128), F32), DMA((22,))],
        compiler_params=pltpu.CompilerParams(vmem_limit_bytes=LIMIT),
    )(low, high, grad_fine, quantiles, w_up, w_head.T, eye)
    return (bands[None], loss.reshape(()), grad_qkv, grad_out, grad_up, grad_conv.reshape(3, 3, 128, 128),
            grad_head.T, fine[None])


def solution(mesh):
    placed = (
        P("batch", "rows", "cols", None),
        P("batch", "rows", "cols", None),
        P("batch", "rows", "cols"),
        P(),
        P(),
        P(),
        P(),
        P(),
    )
    return jax.shard_map(
        body,
        mesh=mesh,
        in_specs=placed,
        out_specs=(
            P("batch", None, "rows", "cols"),
            P(),
            P(),
            P(),
            P(),
            P(),
            P(),
            P("batch", "rows", "cols", None),
        ),
        check_vma=False,
    )
```

```python
import jax
import jax.numpy as jnp
import numpy as np
from types import SimpleNamespace
from jax import lax
from jax.experimental import pallas as pl
from jax.experimental.pallas import tpu as pltpu
from jax.sharding import PartitionSpec as P

HEAD_DIM = 32
QUANT = 9
MESH = pl.DeviceIdType.MESH
F32, B16 = jnp.float32, jnp.bfloat16
DMA = pltpu.SemaphoreType.DMA
SCALE = HEAD_DIM ** (-0.5)
ROOT_2_PI = 0.7978845608028654
LIMIT = 58 * 1024 * 1024
HALF = 512


def onehot(rows, cols, pairs):
    table = np.zeros((rows, cols), np.float32)
    for row, col in pairs:
        table[row, col] = 1.0
    return jnp.asarray(table, B16)


def mid_table():
    return onehot(256, 256, [(p * 16 + r * 2 + m, r * 32 + p * 2 + m)
                             for p in range(16) for r in range(8) for m in range(2)])


def group_table():
    return onehot(256, 256, [(m * 128 + c * 8 + r, c * 16 + r * 2 + m)
                             for m in range(2) for c in range(16) for r in range(8)])


def cross_table():
    return onehot(256, 256, [(m * 128 + c * 8 + r, r * 32 + c * 2 + m)
                             for m in range(2) for c in range(16) for r in range(8)])


def back_table():
    pairs = []
    for r in range(8):
        for j in range(32):
            pairs.append((r * 48 + j, (1 + j // 2) * 16 + r * 2 + j % 2))
        pairs.append((r * 48 + 32, 17 * 16 + r * 2))
        pairs.append((r * 48 + 35, r * 2 + 1))
    return onehot(384, 288, pairs)


def pick_table(first):
    return onehot(16, 128, [(2 * i + s, 16 * i + first + s) for i in range(8) for s in range(2)])


def spread_table(first):
    return onehot(128, 16, [(16 * i + first + s, 2 * i + s) for i in range(8) for s in range(2)])


def bins_table():
    return onehot(48, 64, [(0, 15)] + [(1 + y, 16 + y) for y in range(32)] + [(33, 48)])


def up_table():
    return onehot(144, 48, [(p, p // 4) for p in range(144)])


def sum_table():
    return onehot(32, 128, [(p // 4, p) for p in range(128)])


def dot(a, b):
    return jnp.dot(a, b, preferred_element_type=F32)


def dot_nt(a, b):
    return lax.dot_general(a, b, (((1,), (1,)), ((), ())), preferred_element_type=F32)


def rcopy(src, dst, send, recv, to):
    return pltpu.make_async_remote_copy(src_ref=src, dst_ref=dst, send_sem=send, recv_sem=recv,
                                        device_id=to, device_id_type=MESH)


def wait_all(copies):
    for c in copies:
        c.wait()


def peer_order(axis, me):
    if axis == "rows":
        steps = [(2, 0), (2, 1), (1, 0), (3, 0), (1, 1), (3, 1), (0, 1)]
        return [((me // 2 + a) % 4) * 2 + (me + b) % 2 for a, b in steps]
    steps = [(a, b) for a in range(4) for b in range(4) if a + b > 0]
    steps.sort(key=lambda step: -min(step[0], 4 - step[0]) - min(step[1], 4 - step[1]))
    return [((me // 4 + a) % 4) * 4 + (me + b) % 4 for a, b in steps]


def scatter_out(axis, src, got, send, recv, me):
    copies = []
    for n, p in enumerate(peer_order(axis, me)):
        c = rcopy(src.at[p], got.at[me], send.at[n], recv.at[n], {axis: p})
        c.start()
        copies.append(c)
    return copies


def spread_out(axis, count, me, src, main, send, recv, send_x, recv_x):
    copies = []
    for n, p in enumerate(peer_order(axis, me)):
        c = rcopy(src.at[p], main.at[1 + me], send.at[n], recv.at[n], {axis: p})
        c.start()
        copies.append(c)
    main[1 + me] = src[me]

    def after(t):
        return rcopy(src.at[t - 1], main.at[0], send_x.at[t], recv_x.at[0], {axis: t})

    def before(t):
        return rcopy(src.at[t + 1], main.at[count + 1], send_x.at[t], recv_x.at[1], {axis: t})

    @pl.when(me == count - 1)
    def _():
        for t in range(1, count - 1):
            after(t).start()
        main[0] = src[count - 2]
        main[count + 1] = jnp.zeros(main.shape[1:], B16)

    @pl.when(me == 0)
    def _():
        for t in range(1, count - 1):
            before(t).start()
        main[count + 1] = src[1]
        main[0] = jnp.zeros(main.shape[1:], B16)

    def finish():
        @pl.when(me == count - 1)
        def _():
            for t in range(1, count - 1):
                after(t).wait_send()

        @pl.when(me == 0)
        def _():
            for t in range(1, count - 1):
                before(t).wait_send()

        @pl.when((me > 0) & (me < count - 1))
        def _():
            after(1).wait_recv()
            before(1).wait_recv()

        wait_all(copies)

    return finish


def head_mask(h):
    lane = lax.broadcasted_iota(jnp.int32, (1, 128), 1)
    return jnp.where((lane >> 5) == h, 1.0, 0.0).astype(B16)


def heads_down(tile):
    return jnp.concatenate([tile * head_mask(h) for h in range(4)], axis=0)


def heads_across(tile):
    turned = tile.astype(F32).T
    line = lax.broadcasted_iota(jnp.int32, (128, 1), 0) >> 5
    return jnp.concatenate([jnp.where(line == h, turned, 0.0) for h in range(4)], axis=1).astype(B16)


def side_by_side(stack):
    return jnp.concatenate([stack[h * 128:(h + 1) * 128] for h in range(4)], axis=1)


def put(g, at, value):
    rows, cols = value.shape
    size = rows // 8
    for n in range(cols // 128):
        g[at + n * size:at + (n + 1) * size] = value[:, n * 128:(n + 1) * 128].reshape(size, 8, 128).astype(B16)


def shifted(line):
    return jnp.concatenate([pltpu.roll(line, 1, 0), line, pltpu.roll(line, 143, 0)], axis=1)


def reducer(me, axes, units, g, out, got0, sum0, got1, sum1, got2, sum2, got3, sems):
    core, deep = me.core, me.deep
    (first, in_first), (second, in_second) = axes
    u0, u1, u2, u3 = units // 2, units // 8, units // 32, units // 256
    s0, r0, s1, r1, s2, r2, s3, r3, as3, ar3, as2, ar2, as1, ar1, as0, ar0 = sems
    place = core * u0 + first * u1 + second * u2
    held = {}

    def sum_up(terms):
        total = terms[0].astype(F32)
        for term in terms[1:]:
            total = total + term.astype(F32)
        return total

    def near_start():
        held["near"] = []
        for n, k in enumerate((1, 2, 3, 0)):
            p = (first + k) % 4
            c = rcopy(g.at[pl.ds((1 - core) * u0 + p * u1, u1)], got0.at[p], s0.at[n], r0.at[n], me.other)
            c.start()
            held["near"].append(c)

    def first_start():
        held["first"] = []
        for n, k in enumerate((1, 2, 3)):
            p = (first + k) % 4
            held["near"][n].wait_recv()
            sum0[p] = sum_up([g[pl.ds(core * u0 + p * u1, u1)], got0[p]]).astype(B16)
            c = rcopy(sum0.at[p], got1.at[k - 1], s1.at[k - 1], r1.at[k - 1], in_first(k))
            c.start()
            held["first"].append(c)
        held["near"][3].wait_recv()

    def second_start():
        wait_all(held["first"])
        sum1[...] = sum_up([g[pl.ds(core * u0 + first * u1, u1)], got0[first], got1[0], got1[1], got1[2]]).astype(B16)
        held["second"] = []
        for k in (1, 2, 3):
            p = (second + k) % 4
            c = rcopy(sum1.at[pl.ds(p * u2, u2)], got2.at[k - 1], s2.at[k - 1], r2.at[k - 1], in_second(k))
            c.start()
            held["second"].append(c)
        for c in held["near"]:
            c.wait_send()

    def deep_start():
        wait_all(held["second"])
        sum2[...] = sum_up([sum1[pl.ds(second * u2, u2)], got2[0], got2[1], got2[2]]).astype(B16)
        held["deep"] = []
        for k in (4, 3, 5, 2, 6, 1, 7):
            p = (deep + k) % 8
            c = rcopy(sum2.at[pl.ds(p * u3, u3)], got3.at[k - 1], s3.at[k - 1], r3.at[k - 1], me.in_deep(k))
            c.start()
            held["deep"].append(c)

    def deep_gather():
        wait_all(held["deep"])
        mine = sum_up([sum2[pl.ds(deep * u3, u3)]] + [got3[k] for k in range(7)])
        out[pl.ds(place + deep * u3, u3)] = mine.astype(B16)
        block = out.at[pl.ds(place + deep * u3, u3)]
        held["deep"] = []
        for k in (4, 3, 5, 2, 6, 1, 7):
            c = rcopy(block, block, as3.at[k - 1], ar3.at[k - 1], me.in_deep(k))
            c.start()
            held["deep"].append(c)

    def second_gather():
        wait_all(held["deep"])
        block = out.at[pl.ds(place, u2)]
        held["second"] = []
        for k in (1, 2, 3):
            c = rcopy(block, block, as2.at[k - 1], ar2.at[k - 1], in_second(k))
            c.start()
            held["second"].append(c)

    def forward(n, p):
        block = out.at[pl.ds(core * u0 + p * u1, u1)]
        c = rcopy(block, block, as0.at[n], ar0.at[n], me.other)
        c.start()
        held["near"].append(c)

    def first_gather():
        wait_all(held["second"])
        block = out.at[pl.ds(core * u0 + first * u1, u1)]
        held["first"], held["near"] = [], []
        for k in (1, 2, 3):
            c = rcopy(block, block, as1.at[k - 1], ar1.at[k - 1], in_first(k))
            c.start()
            held["first"].append(c)
        forward(0, first)

    def near_gather():
        for k in (1, 2, 3):
            held["first"][k - 1].wait_recv()
            forward(k, (first + 4 - k) % 4)

    def finish():
        for c in held["first"]:
            c.wait_send()
        wait_all(held["near"])

    return [near_start, first_start, second_start, deep_start, deep_gather, second_gather, first_gather,
            near_gather, finish]


def reducer_scratch(tag, units):
    unit = (8, 128)
    u1, u2, u3 = units // 8, units // 32, units // 256
    shapes = [("g", (units,) + unit), ("got0", (4, u1) + unit), ("sum0", (4, u1) + unit), ("got1", (3, u1) + unit),
              ("sum1", (u1,) + unit), ("got2", (3, u2) + unit), ("sum2", (u2,) + unit), ("got3", (7, u3) + unit)]
    result = [(tag + name, pltpu.VMEM(shape, B16)) for name, shape in shapes]
    for n, count in enumerate((4, 4, 3, 3, 3, 3, 7, 7, 7, 7, 3, 3, 3, 3, 4, 4)):
        result.append((tag + "sem" + str(n), DMA((count,))))
    return result


INPUTS = ("coarse", "fine", "bins", "w_qkv_in", "w_out_in", "w_up_in", "w_conv_in", "w_head_t",
          "turns_in", "back_in", "pick_lo", "pick_hi", "spread_lo", "spread_hi", "place", "up", "fold", "eye")
IN_HBM = ("coarse", "fine", "w_qkv_in", "w_out_in", "w_up_in", "w_conv_in", "turns_in", "back_in")
OUTPUTS = (("quantiles_out", (9, 32, 128), F32), ("grad_fine_out", (32, 128, 128), F32),
           ("low_half", (HALF, 8, 128), B16), ("high_half", (HALF, 8, 128), B16))


def scratch():
    buffers = [
        ("w_qkv", (512, 1536), B16), ("w_out", (512, 512), B16), ("w_conv", (3, 3, 128, 128), B16),
        ("w_up", (512, 128), B16), ("turns", (5, 256, 256), B16), ("back", (384, 288), B16),
        ("got", (8, 32, 256), B16), ("turned", (16, 16, 256), B16), ("tokens", (16, 16, 256), B16),
        ("half", (8, 32, 256), B16), ("half_turned", (16, 16, 256), B16), ("half_got", (16, 16, 256), B16),
        ("half_cross", (8, 32, 256), B16), ("half_tokens", (8, 32, 256), B16),
        ("field", (40, 144, 128), B16), ("bins16", (32, 128), B16), ("bin_got", (64, 128), B16),
        ("edge_out", (2, 5, 16, 128), B16), ("edge_in", (2, 5, 16, 128), B16), ("bin_out", (2, 48, 128), B16),
        ("bin_in", (2, 48, 128), B16), ("rain", (48, 128), F32), ("edge_bins", (16, 128), F32),
        ("tok", (256, 512), B16), ("qkv", (256, 1536), B16), ("prob", (8, 512, 128), F32), ("mixed", (256, 512), B16),
        ("context", (256, 512), B16), ("raised", (16, 16, 128), B16),
        ("slots", (18, 16, 128), B16), ("lift_turned", (8, 48, 128), B16), ("lifted", (10, 48, 128), B16),
        ("query_turned", (8, 128, 512), B16), ("tok_turned", (512, 256), B16),
        ("hidden", (40, 144, 128), F32), ("slope", (40, 128, 128), F32), ("active", (40, 144, 384), B16),
        ("outer", (36, 144, 128), B16), ("taps", (36, 48, 128), B16), ("taps_turned", (36, 128, 48), B16),
        ("back_low", (48, 128), B16), ("back_mid", (48, 256), B16), ("back_high", (48, 128), B16),
        ("tap_sum", (144, 128), F32), ("pair", (1536, 256), B16), ("loss_sum", (16, 128), F32), ("head_sum", (16, 128), F32),
        ("dlift", (8, 32, 128), B16), ("grad_fine", (32, 128, 128), F32), ("quantiles", (9, 32, 128), F32),
        ("fold_got", (8, 32, 128), B16), ("fold_turned", (16, 16, 128), B16), ("folded", (16, 16, 128), B16),
        ("dquery", (256, 512), B16), ("dkey", (512, 256), B16), ("dvalue", (512, 256), B16),
    ]
    sems = [("s_l", 11), ("s_ur", 7), ("r_ur", 7), ("s_uc", 15), ("r_uc", 15), ("s_tr", 7), ("r_tr", 7), ("s_tc", 15), ("r_tc", 15), ("s_h", 4), ("r_h", 4), ("s_e", 4), ("r_e", 4),
            ("s_lc", 15), ("r_lc", 15), ("s_lx", 16), ("r_lx", 2), ("s_lr", 7), ("r_lr", 7), ("s_ly", 8), ("r_ly", 2),
            ("s_fr", 8), ("r_fr", 8), ("s_fc", 15), ("r_fc", 15)]
    return ([(name, pltpu.VMEM(shape, dtype)) for name, shape, dtype in buffers]
            + [(name, DMA((count,))) for name, count in sems]
            + reducer_scratch("a_", HALF) + reducer_scratch("b_", HALF))


def halo_rows(v, row):
    sends = [
        ((v.fine.at[pl.ds(30, 2)], v.field.at[pl.ds(2, 2), pl.ds(0, 128)], v.s_h.at[0], v.r_h.at[0]),
         (v.bins16.at[pl.ds(16, 16)], v.bin_got.at[pl.ds(0, 16)], v.s_h.at[1], v.r_h.at[1])),
        ((v.fine.at[pl.ds(0, 2)], v.field.at[pl.ds(36, 2), pl.ds(0, 128)], v.s_h.at[2], v.r_h.at[2]),
         (v.bins16.at[pl.ds(0, 16)], v.bin_got.at[pl.ds(48, 16)], v.s_h.at[3], v.r_h.at[3])),
    ]

    def start():
        @pl.when(row < 7)
        def _():
            for args in sends[0]:
                rcopy(*args, {"rows": row + 1}).start()

        @pl.when(row > 0)
        def _():
            for args in sends[1]:
                rcopy(*args, {"rows": row - 1}).start()

    def finish():
        @pl.when(row < 7)
        def _():
            for args in sends[0]:
                rcopy(*args, {"rows": row + 1}).wait_send()
            for args in sends[1]:
                rcopy(*args, {"rows": row + 1}).wait_recv()

        @pl.when(row > 0)
        def _():
            for args in sends[1]:
                rcopy(*args, {"rows": row - 1}).wait_send()
            for args in sends[0]:
                rcopy(*args, {"rows": row - 1}).wait_recv()

    return start, finish


def halo_cols(v, col):
    sends = [((v.edge_out.at[n], v.edge_in.at[n], v.s_e.at[2 * n], v.r_e.at[2 * n]),
              (v.bin_out.at[n], v.bin_in.at[n], v.s_e.at[2 * n + 1], v.r_e.at[2 * n + 1])) for n in range(2)]

    def start():
        @pl.when(col < 15)
        def _():
            for args in sends[0]:
                rcopy(*args, {"cols": col + 1}).start()

        @pl.when(col > 0)
        def _():
            for args in sends[1]:
                rcopy(*args, {"cols": col - 1}).start()

    def finish():
        @pl.when(col < 15)
        def _():
            for args in sends[0]:
                rcopy(*args, {"cols": col + 1}).wait_send()
            for args in sends[1]:
                rcopy(*args, {"cols": col + 1}).wait_recv()

        @pl.when(col > 0)
        def _():
            for args in sends[1]:
                rcopy(*args, {"cols": col - 1}).wait_send()
            for args in sends[0]:
                rcopy(*args, {"cols": col - 1}).wait_recv()

    return start, finish


def exchange_tokens(v, row, col, loads):
    low = [rcopy(v.coarse.at[p, :, pl.ds(0, 256)], v.got.at[row], v.s_tr.at[n], v.r_tr.at[n], {"rows": p})
           for n, p in enumerate(peer_order("rows", row))]
    for c in low:
        c.start()
    high = scatter_out("cols", v.half_turned, v.half_got, v.s_uc, v.r_uc, col)
    own = pltpu.make_async_copy(v.coarse.at[row, :, pl.ds(0, 256)], v.got.at[row], v.s_l.at[0])
    own.start()
    v.half_got[col] = v.half_turned[col]
    rows_start, rows_finish = halo_rows(v, row)
    rows_start()

    @pl.when(row == 0)
    def _():
        v.field[pl.ds(2, 2), :128] = jnp.zeros((2, 128, 128), B16)
        v.bin_got[pl.ds(0, 16)] = jnp.zeros((16, 128), B16)

    @pl.when(row == 7)
    def _():
        v.field[pl.ds(36, 2), :128] = jnp.zeros((2, 128, 128), B16)
        v.bin_got[pl.ds(48, 16)] = jnp.zeros((16, 128), B16)

    v.field[pl.ds(0, 2), :128] = jnp.zeros((2, 128, 128), B16)
    v.field[pl.ds(38, 2), :128] = jnp.zeros((2, 128, 128), B16)
    v.bin_got[pl.ds(16, 32)] = v.bins16[...]

    own.wait()
    wait_all(high)
    v.half_cross[...] = dot(v.turns[1], v.half_got[...].reshape(256, 256)).astype(B16).reshape(8, 32, 256)
    high = scatter_out("rows", v.half_cross, v.half_tokens, v.s_ur, v.r_ur, row)
    v.half_tokens[row] = v.half_cross[row]
    wait_all(low)
    v.turned[...] = dot(v.turns[0], v.got[...].reshape(256, 256)).astype(B16).reshape(16, 16, 256)
    low = scatter_out("cols", v.turned, v.tokens, v.s_tc, v.r_tc, col)
    v.tokens[col] = v.turned[col]

    loads[0].wait()
    rows_finish()
    rows = dot(v.place[...], v.bin_got[...])
    v.rain[...] = rows
    v.bin_out[0] = jnp.broadcast_to(rows[:, 127:128], (48, 128)).astype(B16)
    v.bin_out[1] = jnp.broadcast_to(rows[:, 0:1], (48, 128)).astype(B16)
    for q in range(5):
        v.edge_out[0, q] = dot(v.pick_hi[...], v.field[8 * q:8 * q + 8, 112:128].reshape(128, 128)).astype(B16)
        v.edge_out[1, q] = dot(v.pick_lo[...], v.field[8 * q:8 * q + 8, 0:16].reshape(128, 128)).astype(B16)
    cols_start, cols_finish = halo_cols(v, col)
    cols_start()

    @pl.when(col == 0)
    def _():
        v.edge_in[0] = jnp.zeros((5, 16, 128), B16)
        v.bin_in[0] = jnp.zeros((48, 128), B16)

    @pl.when(col == 15)
    def _():
        v.edge_in[1] = jnp.zeros((5, 16, 128), B16)
        v.bin_in[1] = jnp.zeros((48, 128), B16)

    wait_all(low)
    wait_all(high)
    return cols_finish


def attend(v):
    v.tok[:, :256] = dot(v.turns[2], v.tokens[...].reshape(256, 256)).astype(B16)
    v.tok[:, 256:] = dot(v.turns[3], v.half_tokens[...].reshape(256, 256)).astype(B16)
    for n in range(3):
        v.qkv[:, n * 512:(n + 1) * 512] = dot(v.tok[...], v.w_qkv[:, n * 512:(n + 1) * 512]).astype(B16)
    for g in range(2):
        for t in range(4):
            rows, at = slice(g * 128, g * 128 + 128), t * 128
            query = v.qkv[rows, at:at + 128]
            keyed = v.qkv[rows, 512 + at:512 + at + 128]
            valued = v.qkv[rows, 1024 + at:1024 + at + 128]
            scores = dot_nt(heads_down(query), keyed) * SCALE
            peak = jnp.max(scores, axis=-1, keepdims=True)
            powers = jnp.exp(scores - peak)
            share = powers / jnp.sum(powers, axis=-1, keepdims=True)
            v.prob[g * 4 + t] = share
            v.mixed[rows, at:at + 128] = dot(side_by_side(share.astype(B16)), heads_down(valued)).astype(B16)
    attended = dot(v.mixed[...], v.w_out[...]).astype(B16)
    v.context[...] = (v.tok[...].astype(F32) + attended.astype(F32)).astype(B16)
    lifted = dot(v.context[...], v.w_up[...]).astype(B16)
    v.raised[...] = dot(v.turns[4], lifted).astype(B16).reshape(16, 16, 128)


def edge_targets(v):
    lane = lax.broadcasted_iota(jnp.int32, (48, 128), 1)
    line = lax.broadcasted_iota(jnp.int32, (48, 128), 0)
    low, high = v.bin_in[0].astype(F32), v.bin_in[1].astype(F32)
    picked = jnp.where((lane & 15) == 0, high, jnp.where((lane & 15) == 15, low, 0.0))
    for b in range(9):
        here = line == 4 * b + (lane >> 4)
        v.edge_bins[b:b + 1] = jnp.sum(jnp.where(here, picked, 0.0), axis=0, keepdims=True)


def fold_copy(v, row, target, source):
    return rcopy(v.dlift.at[target], v.fold_got.at[source], v.s_fr.at[target], v.r_fr.at[source], {"rows": target})


def send_fold(v, row, target):
    @pl.when(row != target)
    def _():
        fold_copy(v, row, target, row).start()


def convolve(v, row, col):
    head_t = dot(v.eye[...], v.w_head_t[...]).astype(B16)
    place = lax.broadcasted_iota(jnp.int32, (144, 1), 0)
    right = jnp.where(col < 15, 130, 128)
    left = jnp.where(col > 0, 142, 144)
    inside = (place < right) | (place >= left)
    level = (lax.broadcasted_iota(jnp.int32, (16, 1), 0) + 1).astype(F32) / 10.0
    quant = lax.broadcasted_iota(jnp.int32, (16, 1), 0) < QUANT
    v.loss_sum[...] = jnp.zeros((16, 128), F32)
    v.head_sum[...] = jnp.zeros((16, 128), F32)
    v.tap_sum[...] = jnp.zeros((144, 128), F32)
    v.active[pl.ds(38, 2)] = jnp.zeros((2, 144, 384), B16)
    v.hidden[pl.ds(38, 2)] = jnp.zeros((2, 144, 128), F32)

    def start(i):
        raised = dot(v.up[...], v.lifted[i])
        rims = {0: (2, 3), 9: (0, 1)}.get(i, range(4))
        for s in rims:
            y = 4 * i + s - 4
            x = v.field[4 * i + s].astype(F32) + raised
            square = x * x
            bend = jnp.tanh(ROOT_2_PI * x * (1.0 + 0.044715 * square))
            half = 0.5 * (1.0 + bend)
            act = x * half
            if i in (0, 9):
                act = jnp.where(inside & (row * 32 + y >= 0) & (row * 32 + y < 256), act, 0.0)
            else:
                act = jnp.concatenate([act[:128], jnp.where(inside[128:], act[128:], 0.0)], axis=0)
            v.hidden[4 * i + s] = x
            v.active[4 * i + s] = shifted(act).astype(B16)
            v.slope[4 * i + s] = half[:128] + (0.5 * ROOT_2_PI) * x[:128] * (1.0 - bend[:128] * bend[:128]) * (
                1.0 + (3 * 0.044715) * square[:128])

    def forward(i):
        windows = [jnp.concatenate([v.active[4 * i + 2 + a], v.active[4 * i + 4 + a]], axis=0) for a in range(4)]
        both = dot(jnp.concatenate(windows, axis=1), v.pair[...])
        for s in range(4):
            at, part = s // 2 * 144, s % 2 * 128
            v.outer[4 * i + s] = (v.hidden[4 * i + 3 + s] + both[at:at + 144, part:part + 128]).astype(B16)

    def turn(i):
        own = v.outer[pl.ds(4 * i, 4), :128].reshape(512, 128)
        edge = v.outer[pl.ds(4 * i, 4), 128:144].reshape(64, 128)
        pixels = jnp.concatenate([own, edge, jnp.zeros((64, 128), B16)], axis=0)
        predicted = dot_nt(head_t, pixels)
        lines = [v.rain[pl.ds(4 * i + s, 1), :] for s in range(4)] + [v.edge_bins[pl.ds(i, 1), :]]
        target = jnp.concatenate(lines, axis=1) * (1.0 / 16.0) - 1.0
        lane = lax.broadcasted_iota(jnp.int32, (1, 640), 1)
        spot = lane - 512
        inner = lane < 512
        y = 4 * i - 1 + jnp.where(inner, lane >> 7, spot >> 4)
        side = (((spot & 15) == 0) & (col < 15)) | (((spot & 15) == 15) & (col > 0))
        seen = (row * 32 + y >= 0) & (row * 32 + y < 256) & (y < 33) & (inner | (side & (spot < 64)))
        mine = inner & (y >= 0) & (y < 32)
        error = target - predicted
        weight = jnp.where(error < 0.0, 1.0 - level, level)
        down = jnp.where(seen & quant, -weight * jnp.clip(error, -1.0, 1.0) * (1.0 / 1024.0), 0.0)
        size = jnp.abs(error)
        loss = weight * jnp.where(size <= 1.0, 0.5 * error * error, size - 0.5)
        loss = jnp.where(mine & quant, loss, 0.0)
        v.loss_sum[...] += loss[:, :128] + loss[:, 128:256] + loss[:, 256:384] + loss[:, 384:512]
        v.head_sum[...] += dot(jnp.where(mine, down, 0.0).astype(B16)[:, :512], own)
        edge = down[:, 512:]
        at = lax.broadcasted_iota(jnp.int32, (1, 128), 1)
        sets = []
        for s in range(4):
            line = down[:, s * 128:(s + 1) * 128]
            before = jnp.where(at == 0, pltpu.roll(edge, 113 - 16 * s, 1), pltpu.roll(line, 1, 1))
            after = jnp.where(at == 127, pltpu.roll(edge, 127 - 16 * s, 1), pltpu.roll(line, 127, 1))
            sets.append(jnp.concatenate([before, line, after], axis=0))
            v.taps[4 * i + s] = sets[s].astype(B16)
            row_y = 4 * i + s - 1
            value = predicted[:, s * 128:(s + 1) * 128]
            if 0 <= row_y < 32:
                for q in range(QUANT):
                    v.quantiles[q, pl.ds(row_y, 1), :] = value[q:q + 1]
        v.taps_turned[pl.ds(4 * i, 4)] = jnp.concatenate(sets, axis=1).T.astype(B16).reshape(4, 128, 48)

    def back(i):
        windows = [v.taps_turned[pl.ds(4 * i + a, 4)].reshape(512, 48) for a in range(3)]
        both = dot(windows[1], v.back_mid[...])
        dactive = both[:, :128] + dot(windows[0], v.back_low[...]) + dot(windows[2], v.back_high[...])
        dhidden = (both[:, 128:] + v.slope[pl.ds(4 * i + 4, 4)].reshape(512, 128) * dactive).reshape(4, 128, 128)
        v.grad_fine[pl.ds(4 * i, 4)] = dhidden * 1024.0
        summed = dhidden[0] + dhidden[1] + dhidden[2] + dhidden[3]
        high = summed.astype(B16)
        low = (summed - high.astype(F32)).astype(B16)
        v.dlift[i] = (dot(v.fold[...], high) + dot(v.fold[...], low)).astype(B16)
        lines = [jnp.concatenate([v.taps[4 * i + a + s] for s in range(4)], axis=1) for a in range(3)]
        seen = v.active[pl.ds(4 * i + 4, 4), :128, 128:256].reshape(512, 128)
        v.tap_sum[...] += dot(jnp.concatenate(lines, axis=0), seen)

    for t in range(10):
        start(t)
    for t in range(9):
        forward(t)
    for t in range(9):
        turn(t)
    for t in range(8):
        back(t)
        if t % 4 == 3:
            for n in range(t - 3, t + 1):
                send_fold(v, row, n)


def back_weights(v):
    head_t = dot(v.eye[...], v.w_head_t[...]).astype(B16)
    for a, name in enumerate(("back_low", "back_mid", "back_high")):
        parts = [dot_nt(head_t, v.w_conv[2 - a, 2 - b]).astype(B16) for b in range(3)]
        getattr(v, name)[:, :128] = jnp.concatenate(parts, axis=0)
    for a in range(4):
        for b in range(2):
            block = v.w_conv[a - b].reshape(384, 128) if 0 <= a - b < 3 else jnp.zeros((384, 128), B16)
            v.pair[a * 384:(a + 1) * 384, b * 128:(b + 1) * 128] = block
    blank = jnp.zeros((16, 128), B16)
    v.back_mid[:, 128:] = jnp.concatenate([blank, head_t, blank], axis=0)


def local_units(v):
    v.b_g[384:402] = v.tap_sum[...].reshape(18, 8, 128).astype(B16)
    spot = lax.broadcasted_iota(jnp.int32, (16, 1), 0)
    total = jnp.sum(v.loss_sum[...], axis=0, keepdims=True)
    tail = jnp.where(spot < QUANT, v.head_sum[...], jnp.where(spot == QUANT, total, 0.0))
    v.b_g[402:404] = tail.reshape(2, 8, 128).astype(B16)
    v.b_g[404:HALF] = jnp.zeros((HALF - 404, 8, 128), B16)


def attend_back(v, mix_grad, g, tiles):
    for s, t in [(s, t) for s in range(2) for t in tiles]:
        rows, at = slice(s * 128, s * 128 + 128), t * 128
        keyed = v.qkv[rows, 512 + at:512 + at + 128]
        valued = v.qkv[rows, 1024 + at:1024 + at + 128]
        mine = mix_grad[rows, at:at + 128]
        dprob = dot_nt(heads_down(mine), valued)
        share = v.prob[s * 4 + t]
        inner = jnp.sum(share * dprob, axis=-1, keepdims=True)
        dscore = (share * (dprob - inner) * SCALE).astype(B16)
        v.dquery[rows, at:at + 128] = dot(side_by_side(dscore), heads_down(keyed)).astype(B16)
        v.dkey[at:at + 128, rows] = dot(v.query_turned[s * 4 + t], dscore).astype(B16)
        v.dvalue[at:at + 128, rows] = dot(heads_across(mine), share.astype(B16)).astype(B16)
    at = tiles[0] * 128
    put(g, 0, dot(v.tok_turned[...], v.dquery[:, at:at + 256]))
    put(g, 128, dot_nt(v.tok_turned[...], v.dkey[at:at + 256]))
    put(g, 256, dot_nt(v.tok_turned[...], v.dvalue[at:at + 256]))


def whole_kernel(names, *refs):
    v = SimpleNamespace(**dict(zip(names, refs)))
    row, col, batch = lax.axis_index("rows"), lax.axis_index("cols"), lax.axis_index("batch")
    core, deep = row % 2, (row // 2) * 2 + batch
    x, y = col // 4, col % 4
    me = SimpleNamespace(
        core=core, deep=deep, other={"rows": row + 1 - 2 * core},
    )
    x_axis = (x, lambda k: {"cols": ((x + k) % 4) * 4 + y})
    y_axis = (y, lambda k: {"cols": x * 4 + (y + k) % 4})

    def in_deep(k):
        p = (deep + k) % 8
        return {"rows": (p // 2) * 2 + core, "batch": p % 2}

    me.in_deep = in_deep

    peers = [{"rows": p} for p in peer_order("rows", row)]
    peers = peers[:2] + [{"rows": (row + 2 * k) % 8, "batch": 1 - batch} for k in (2, 1, 3, 0)] + peers[2:6] + [
        {"cols": p} for p in peer_order("cols", col)] + peers[6:]
    barrier = pltpu.get_barrier_semaphore()
    for peer in peers:
        pl.semaphore_signal(barrier, inc=1, device_id=peer, device_id_type=MESH)
    loads = [pltpu.make_async_copy(v.fine, v.field.at[pl.ds(4, 32), pl.ds(0, 128)], v.s_l.at[1]),
             pltpu.make_async_copy(v.w_qkv_in, v.w_qkv, v.s_l.at[2]),
             pltpu.make_async_copy(v.w_out_in, v.w_out, v.s_l.at[3]),
             pltpu.make_async_copy(v.w_conv_in, v.w_conv, v.s_l.at[4]),
             pltpu.make_async_copy(v.coarse.at[:, :, pl.ds(256, 256)], v.half, v.s_l.at[7]),
             pltpu.make_async_copy(v.turns_in, v.turns, v.s_l.at[8]),
             pltpu.make_async_copy(v.w_up_in, v.w_up, v.s_l.at[9]),
             pltpu.make_async_copy(v.back_in, v.back, v.s_l.at[10])]
    for n in (4, 5, 0, 1, 2, 6, 3, 7):
        loads[n].start()
    v.bins16[...] = v.bins[...].astype(F32).astype(B16)
    loads[4].wait()
    loads[5].wait()
    v.half_turned[...] = dot(v.turns[0], v.half[...].reshape(256, 256)).astype(B16).reshape(16, 16, 256)
    pl.semaphore_wait(barrier, len(peers))
    cols_finish = exchange_tokens(v, row, col, loads)
    loads[1].wait()
    loads[2].wait()
    loads[6].wait()
    loads[7].wait()
    attend(v)

    finish = spread_out("cols", 16, col, v.raised, v.slots, v.s_lc, v.r_lc, v.s_lx, v.r_lx)
    cols_finish()
    for q in range(5):
        edge = dot(v.spread_hi[...], v.edge_in[0, q]) + dot(v.spread_lo[...], v.edge_in[1, q])
        v.field[8 * q:8 * q + 8, 128:144] = edge.astype(B16).reshape(8, 16, 128)
    edge_targets(v)
    for s in range(2):
        for t in range(4):
            v.query_turned[s * 4 + t] = heads_across(v.qkv[s * 128:s * 128 + 128, t * 128:t * 128 + 128])
    finish()
    v.lift_turned[...] = dot(v.back[...], v.slots[...].reshape(288, 128)).astype(B16).reshape(8, 48, 128)
    finish = spread_out("rows", 8, row, v.lift_turned, v.lifted, v.s_lr, v.r_lr, v.s_ly, v.r_ly)
    v.tok_turned[...] = v.tok[...].astype(F32).T.astype(B16)
    loads[3].wait()
    back_weights(v)
    finish()

    convolve(v, row, col)

    results = [pltpu.make_async_copy(v.grad_fine, v.grad_fine_out, v.s_l.at[5]),
               pltpu.make_async_copy(v.quantiles, v.quantiles_out, v.s_l.at[6])]
    v.fold_got[row] = v.dlift[row]
    for c in results:
        c.start()
    local_units(v)
    for p in peer_order("rows", row):
        fold_copy(v, row, p, p).wait()
    v.fold_turned[...] = dot(v.turns[0], v.fold_got[...].reshape(256, 128)).astype(B16).reshape(16, 16, 128)
    sends = scatter_out("cols", v.fold_turned, v.folded, v.s_fc, v.r_fc, col)
    v.folded[col] = v.fold_turned[col]
    wait_all(sends)

    low = reducer(me, (x_axis, y_axis), HALF, v.a_g, v.low_half, v.a_got0, v.a_sum0, v.a_got1, v.a_sum1, v.a_got2, v.a_sum2,
                  v.a_got3, [getattr(v, "a_sem" + str(n)) for n in range(16)])
    high = reducer(me, (y_axis, x_axis), HALF, v.b_g, v.high_half, v.b_got0, v.b_sum0, v.b_got1, v.b_sum1, v.b_got2, v.b_sum2,
                   v.b_got3, [getattr(v, "b_sem" + str(n)) for n in range(16)])
    lift_wide = dot(v.turns[2], v.folded[...].reshape(256, 128))
    lift, lift_turned = lift_wide.astype(B16), lift_wide.T.astype(B16)
    dcontext = dot_nt(lift, v.w_up[...]).astype(B16)
    mix_grad = dot_nt(dcontext, v.w_out[...]).astype(B16)
    put(v.a_g, 384, dot(lift_turned, v.mixed[...]))
    put(v.a_g, 448, dot(lift_turned, v.context[...]))
    attend_back(v, mix_grad, v.a_g, (0, 1))
    low[0]()
    attend_back(v, mix_grad, v.b_g, (2, 3))
    high[0]()
    low[1]()
    high[1]()
    for n in range(2, 9):
        low[n]()
        high[n]()
    wait_all(results)


def unpack_kernel(low, high, fine, quantiles, w_up, w_head_t, eye,
                  grad_qkv, grad_out, grad_up, grad_conv, grad_head, loss, fine_out, quantiles_out,
                  held, wide, square, tall, flat, fine_in, bands_in, sems):
    through = [(fine.at[pl.ds(n * 8, 8)], fine_in.at[pl.ds(n * 8, 8)], fine_out.at[pl.ds(n * 8, 8)]) for n in range(4)]
    through.append((quantiles, bands_in, quantiles_out))
    passing = [pltpu.make_async_copy(src, held, sems.at[12 + n]) for n, (src, held, _) in enumerate(through)]
    reads = [pltpu.make_async_copy((low, high)[h].at[pl.ds(a, b)], held.at[h, pl.ds(a, b)], sems.at[2 * n + h])
             for n, (a, b) in enumerate(((0, 384), (384, 128))) for h in range(2)]
    for c in passing + reads[2:] + reads[:2]:
        c.start()
    writes = []

    def write(src, dst, n):
        c = pltpu.make_async_copy(src, dst, sems.at[n])
        c.start()
        writes.append(c)

    for m in range(5):
        passing[m].wait()
        write(through[m][1], through[m][2], 17 + m)
    reads[2].wait()
    reads[3].wait()
    for n in range(4):
        mixed = held[0, 384 + n * 16:384 + (n + 1) * 16].astype(F32).reshape(128, 128).T.astype(B16)
        square[n * 128:(n + 1) * 128] = dot_nt(mixed, w_up[...])
        tall[n * 128:(n + 1) * 128] = held[0, 448 + n * 16:448 + (n + 1) * 16].astype(F32).reshape(128, 128).T
    write(square, grad_out, 9)
    write(tall, grad_up, 10)
    head_t = dot(eye[...], w_head_t[...]).astype(B16)
    for a in range(3):
        for b in range(3):
            at = 384 + (2 - a) * 6 + (2 - b) * 2
            seen = held[1, at:at + 2].astype(F32).reshape(16, 128).T.astype(B16)
            flat[(a * 3 + b) * 128:(a * 3 + b + 1) * 128] = dot(seen, head_t)
    write(flat, grad_conv, 11)
    for h in range(2):
        reads[h].wait()
        for n in range(3):
            for m in range(2):
                at = n * 128 + m * 64
                wide[h * 3 + n, :, m * 128:(m + 1) * 128] = held[h, at:at + 64].astype(F32).reshape(512, 128)
            write(wide.at[h * 3 + n], grad_qkv.at[:, pl.ds(n * 512 + h * 256, 256)], 22 + h * 3 + n)
    tail = held[1, 402:404].astype(F32).reshape(16, 128)
    grad_head[...] = tail[:QUANT]
    loss[...] = jnp.sum(tail[QUANT:QUANT + 1], axis=1, keepdims=True) * (1.0 / (1048576.0 * QUANT))
    wait_all(writes)


def body(fine_input, coarse, rain_bins, w_qkv, w_out, w_up, w_conv, w_head):
    mid, group = mid_table(), group_table()
    turns = jnp.stack([mid, mid.T, group, cross_table(), group.T])
    eye = onehot(16, QUANT, [(q, q) for q in range(QUANT)])
    args = [coarse[0], fine_input[0], rain_bins[0], w_qkv, w_out, w_up, w_conv, w_head.T,
            turns, back_table(), pick_table(0), pick_table(14), spread_table(0), spread_table(14),
            bins_table(), up_table(), sum_table(), eye]
    spaces = scratch()
    names = INPUTS + tuple(name for name, _, _ in OUTPUTS) + tuple(name for name, _ in spaces)
    vmem, anywhere = pl.BlockSpec(memory_space=pltpu.VMEM), pl.BlockSpec(memory_space=pl.ANY)

    def kernel(*refs):
        whole_kernel(names, *refs)

    quantiles, grad_fine, low, high = pl.pallas_call(
        kernel,
        out_shape=[jax.ShapeDtypeStruct(shape, dtype) for _, shape, dtype in OUTPUTS],
        in_specs=[pl.BlockSpec(memory_space=pl.ANY) if name in IN_HBM else vmem for name in INPUTS],
        out_specs=[anywhere, anywhere, vmem, vmem],
        scratch_shapes=[space for _, space in spaces],
        compiler_params=pltpu.CompilerParams(vmem_limit_bytes=LIMIT, collective_id=1, has_side_effects=True),
    )(*args)
    shapes = ((512, 1536), (512, 512), (512, 128), (1152, 128), (QUANT, 128), (1, 1), (32, 128, 128), (9, 32, 128))
    grad_qkv, grad_out, grad_up, grad_conv, grad_head, loss, fine, bands = pl.pallas_call(
        unpack_kernel,
        out_shape=[jax.ShapeDtypeStruct(shape, F32) for shape in shapes],
        in_specs=[anywhere] * 4 + [vmem] * 3,
        out_specs=[anywhere] * 4 + [vmem] * 2 + [anywhere] * 2,
        scratch_shapes=[pltpu.VMEM((2, HALF, 8, 128), B16), pltpu.VMEM((6, 512, 256), F32),
                        pltpu.VMEM((512, 512), F32), pltpu.VMEM((512, 128), F32), pltpu.VMEM((1152, 128), F32),
                        pltpu.VMEM((32, 128, 128), F32), pltpu.VMEM((9, 32, 128), F32), DMA((28,))],
        compiler_params=pltpu.CompilerParams(vmem_limit_bytes=LIMIT),
    )(low, high, grad_fine, quantiles, w_up, w_head.T, eye)
    return (bands[None], loss.reshape(()), grad_qkv, grad_out, grad_up, grad_conv.reshape(3, 3, 128, 128),
            grad_head.T, fine[None])


def solution(mesh):
    placed = (
        P("batch", "rows", "cols", None),
        P("batch", "rows", "cols", None),
        P("batch", "rows", "cols"),
        P(),
        P(),
        P(),
        P(),
        P(),
    )
    return jax.shard_map(
        body,
        mesh=mesh,
        in_specs=placed,
        out_specs=(
            P("batch", None, "rows", "cols"),
            P(),
            P(),
            P(),
            P(),
            P(),
            P(),
            P("batch", "rows", "cols", None),
        ),
        check_vma=False,
    )
```

```python
import functools
import jax
import jax.numpy as jnp
import numpy as np
from types import SimpleNamespace
from jax import lax
from jax.experimental import pallas as pl
from jax.experimental.pallas import tpu as pltpu
from jax.sharding import PartitionSpec as P

HEAD_DIM = 32
QUANT = 9
MESH = pl.DeviceIdType.MESH
F32, B16 = jnp.float32, jnp.bfloat16
DMA = pltpu.SemaphoreType.DMA
SCALE = HEAD_DIM ** (-0.5)
ROOT_2_PI = 0.7978845608028654
LIMIT = 58 * 1024 * 1024
HALF, SHARES = 480, 5


def onehot(rows, cols, pairs):
    table = np.zeros((rows, cols), np.float32)
    for row, col in pairs:
        table[row, col] = 1.0
    return jnp.asarray(table, B16)


def mid_table():
    return onehot(256, 256, [(p * 16 + r * 2 + m, r * 32 + p * 2 + m)
                             for p in range(16) for r in range(8) for m in range(2)])


def group_table():
    return onehot(256, 256, [(m * 128 + c * 8 + r, c * 16 + r * 2 + m)
                             for m in range(2) for c in range(16) for r in range(8)])


def cross_table():
    return onehot(256, 256, [(m * 128 + c * 8 + r, r * 32 + c * 2 + m)
                             for m in range(2) for c in range(16) for r in range(8)])


def back_table():
    pairs = []
    for r in range(8):
        for j in range(32):
            pairs.append((r * 48 + j, (1 + j // 2) * 16 + r * 2 + j % 2))
        pairs.append((r * 48 + 32, 17 * 16 + r * 2))
        pairs.append((r * 48 + 35, r * 2 + 1))
    return onehot(384, 288, pairs)


def pick_table(first):
    return onehot(16, 128, [(2 * i + s, 16 * i + first + s) for i in range(8) for s in range(2)])


def spread_table(first):
    return onehot(128, 16, [(16 * i + first + s, 2 * i + s) for i in range(8) for s in range(2)])


def bins_table():
    return onehot(48, 64, [(0, 15)] + [(1 + y, 16 + y) for y in range(32)] + [(33, 48)])


def up_table():
    return onehot(144, 48, [(p, p // 4) for p in range(144)])


def sum_table():
    return onehot(32, 128, [(p // 4, p) for p in range(128)])


def dot(a, b):
    return jnp.dot(a, b, preferred_element_type=F32)


def dot_nt(a, b):
    return lax.dot_general(a, b, (((1,), (1,)), ((), ())), preferred_element_type=F32)


def rcopy(src, dst, send, recv, to):
    return pltpu.make_async_remote_copy(src_ref=src, dst_ref=dst, send_sem=send, recv_sem=recv,
                                        device_id=to, device_id_type=MESH)


def wait_all(copies):
    for c in copies:
        c.wait()


def peer_order(axis, me):
    if axis == "rows":
        steps = [(2, 0), (2, 1), (1, 0), (3, 0), (1, 1), (3, 1), (0, 1)]
        return [((me // 2 + a) % 4) * 2 + (me + b) % 2 for a, b in steps]
    steps = [(a, b) for a in range(4) for b in range(4) if a + b > 0]
    steps.sort(key=lambda step: -min(step[0], 4 - step[0]) - min(step[1], 4 - step[1]))
    return [((me // 4 + a) % 4) * 4 + (me + b) % 4 for a, b in steps]


def scatter_out(axis, src, got, send, recv, me):
    copies = []
    for n, p in enumerate(peer_order(axis, me)):
        c = rcopy(src.at[p], got.at[me], send.at[n], recv.at[n], {axis: p})
        c.start()
        copies.append(c)
    return copies


def spread_out(axis, count, me, src, main, send, recv, send_x, recv_x):
    copies = []
    for n, p in enumerate(peer_order(axis, me)):
        c = rcopy(src.at[p], main.at[1 + me], send.at[n], recv.at[n], {axis: p})
        c.start()
        copies.append(c)
    main[1 + me] = src[me]

    def after(t):
        return rcopy(src.at[t - 1], main.at[0], send_x.at[t], recv_x.at[0], {axis: t})

    def before(t):
        return rcopy(src.at[t + 1], main.at[count + 1], send_x.at[t], recv_x.at[1], {axis: t})

    @pl.when(me == count - 1)
    def _():
        for t in range(1, count - 1):
            after(t).start()
        main[0] = src[count - 2]
        main[count + 1] = jnp.zeros(main.shape[1:], B16)

    @pl.when(me == 0)
    def _():
        for t in range(1, count - 1):
            before(t).start()
        main[count + 1] = src[1]
        main[0] = jnp.zeros(main.shape[1:], B16)

    def finish():
        @pl.when(me == count - 1)
        def _():
            for t in range(1, count - 1):
                after(t).wait_send()

        @pl.when(me == 0)
        def _():
            for t in range(1, count - 1):
                before(t).wait_send()

        @pl.when((me > 0) & (me < count - 1))
        def _():
            after(1).wait_recv()
            before(1).wait_recv()

        wait_all(copies)

    return finish


def head_mask(h):
    lane = lax.broadcasted_iota(jnp.int32, (1, 128), 1)
    return jnp.where((lane >> 5) == h, 1.0, 0.0).astype(B16)


def heads_down(tile):
    return jnp.concatenate([tile * head_mask(h) for h in range(4)], axis=0)


def heads_across(tile):
    turned = tile.astype(F32).T
    line = lax.broadcasted_iota(jnp.int32, (128, 1), 0) >> 5
    return jnp.concatenate([jnp.where(line == h, turned, 0.0) for h in range(4)], axis=1).astype(B16)


def side_by_side(stack):
    return jnp.concatenate([stack[h * 128:(h + 1) * 128] for h in range(4)], axis=1)


def put(g, at, value):
    rows, cols = value.shape
    size = rows // 8
    for n in range(cols // 128):
        g[at + n * size:at + (n + 1) * size] = value[:, n * 128:(n + 1) * 128].reshape(size, 8, 128).astype(B16)


def shifted(line):
    return jnp.concatenate([pltpu.roll(line, 1, 0), line, pltpu.roll(line, 143, 0)], axis=1)


def reducer(me, axes, units, g, out, dest, got0, sum0, got1, sum1, got2, sum2, got3, sems):
    core, deep = me.core, me.deep
    (first, in_first), (second, in_second) = axes
    u0, u1, u2, u3 = units // 2, units // 8, units // 32, units // (32 * SHARES)
    s0, r0, s1, r1, s2, r2, s3, r3, as3, ar3, as2, ar2, as1, ar1, as0, ar0, w0, w1 = sems
    place = core * u0 + first * u1 + second * u2
    held = {}

    def sum_up(terms):
        total = terms[0].astype(F32)
        for term in terms[1:]:
            total = total + term.astype(F32)
        return total

    def near_start():
        held["near"] = []
        for n, k in enumerate((1, 2, 3, 0)):
            p = (first + k) % 4
            c = rcopy(g.at[pl.ds((1 - core) * u0 + p * u1, u1)], got0.at[p], s0.at[n], r0.at[n], me.other)
            c.start()
            held["near"].append(c)

    def first_start():
        held["first"] = []
        for n, k in enumerate((1, 2, 3)):
            p = (first + k) % 4
            held["near"][n].wait_recv()
            sum0[p] = sum_up([g[pl.ds(core * u0 + p * u1, u1)], got0[p]]).astype(B16)
            c = rcopy(sum0.at[p], got1.at[k - 1], s1.at[k - 1], r1.at[k - 1], in_first(k))
            c.start()
            held["first"].append(c)
        held["near"][3].wait_recv()

    def second_start():
        wait_all(held["first"])
        sum1[...] = sum_up([g[pl.ds(core * u0 + first * u1, u1)], got0[first], got1[0], got1[1], got1[2]]).astype(B16)
        held["second"] = []
        for k in (1, 2, 3):
            p = (second + k) % 4
            c = rcopy(sum1.at[pl.ds(p * u2, u2)], got2.at[k - 1], s2.at[k - 1], r2.at[k - 1], in_second(k))
            c.start()
            held["second"].append(c)
        for c in held["near"]:
            c.wait_send()

    def deep_start():
        wait_all(held["second"])
        sum2[...] = sum_up([sum1[pl.ds(second * u2, u2)], got2[0], got2[1], got2[2]]).astype(B16)
        for k in (4, 3, 5, 2, 6, 1, 7):
            pl.when((deep + k) % 8 < SHARES)(functools.partial(deep_send, k))

    def deep_copy(k, share):
        return rcopy(sum2.at[pl.ds(share * u3, u3)], got3.at[k - 1], s3.at[k - 1], r3.at[k - 1], me.in_deep(k))

    def deep_send(k):
        deep_copy(k, (deep + k) % 8).start()

    def deep_sent(k):
        deep_copy(k, 0).wait_send()

    def deep_back(k, share):
        block = out.at[pl.ds(place + share * u3, u3)]
        return rcopy(block, block, as3.at[k - 1], ar3.at[k - 1], me.in_deep(k))

    def deep_here(k):
        deep_back(k, 0).wait_recv()

    def deep_gather():
        for k in range(1, 8):
            pl.when((deep + k) % 8 < SHARES)(functools.partial(deep_sent, k))

        @pl.when(deep < SHARES)
        def _():
            for k in range(1, 8):
                deep_copy(k, 0).wait_recv()
            mine = sum_up([sum2[pl.ds(deep * u3, u3)]] + [got3[k] for k in range(7)])
            out[pl.ds(place + deep * u3, u3)] = mine.astype(B16)
            for k in (4, 3, 5, 2, 6, 1, 7):
                deep_back(k, deep).start()

    def second_gather():
        @pl.when(deep < SHARES)
        def _():
            for k in range(1, 8):
                deep_back(k, 0).wait_send()

        for k in range(1, 8):
            pl.when((deep + 8 - k) % 8 < SHARES)(functools.partial(deep_here, k))
        block = out.at[pl.ds(place, u2)]
        held["second"] = []
        for k in (1, 2, 3):
            c = rcopy(block, block, as2.at[k - 1], ar2.at[k - 1], in_second(k))
            c.start()
            held["second"].append(c)

    def leave(at, sem):
        block = pl.ds(at, u1)
        c = pltpu.make_async_copy(out.at[block], dest.at[block], sem)
        c.start()
        held["leave"].append(c)

    def forward(n, p):
        block = out.at[pl.ds(core * u0 + p * u1, u1)]
        c = rcopy(block, block, as0.at[n], ar0.at[n], me.other)
        c.start()
        held["near"].append(c)
        leave(core * u0 + p * u1, w0.at[n])

    def first_gather():
        wait_all(held["second"])
        block = out.at[pl.ds(core * u0 + first * u1, u1)]
        held["first"], held["near"], held["leave"] = [], [], []
        for k in (1, 2, 3):
            c = rcopy(block, block, as1.at[k - 1], ar1.at[k - 1], in_first(k))
            c.start()
            held["first"].append(c)
        forward(0, first)

    def near_gather():
        for k in (1, 2, 3):
            held["first"][k - 1].wait_recv()
            forward(k, (first + 4 - k) % 4)

    def finish():
        for n, c in enumerate(held["near"]):
            c.wait_recv()
            leave((1 - core) * u0 + (first + 4 - n) % 4 * u1, w1.at[n])
        for c in held["first"] + held["near"]:
            c.wait_send()
        wait_all(held["leave"])

    return [near_start, first_start, second_start, deep_start, deep_gather, second_gather, first_gather,
            near_gather, finish]


def reducer_scratch(tag, units):
    unit = (8, 128)
    u1, u2, u3 = units // 8, units // 32, units // (32 * SHARES)
    shapes = [("g", (units,) + unit), ("out", (units,) + unit), ("got0", (4, u1) + unit), ("sum0", (4, u1) + unit), ("got1", (3, u1) + unit),
              ("sum1", (u1,) + unit), ("got2", (3, u2) + unit), ("sum2", (u2,) + unit), ("got3", (7, u3) + unit)]
    result = [(tag + name, pltpu.VMEM(shape, B16)) for name, shape in shapes]
    for n, count in enumerate((4, 4, 3, 3, 3, 3, 7, 7, 7, 7, 3, 3, 3, 3, 4, 4, 4, 4)):
        result.append((tag + "sem" + str(n), DMA((count,))))
    return result


INPUTS = ("coarse", "fine", "bins", "w_qkv_in", "w_out_in", "w_up_in", "w_conv_in", "w_head_t",
          "turns_in", "back_in", "pick_lo", "pick_hi", "spread_lo", "spread_hi", "place", "up", "fold", "eye")
IN_HBM = ("coarse", "fine", "w_qkv_in", "w_out_in", "w_up_in", "w_conv_in", "turns_in", "back_in")
OUTPUTS = (("quantiles_out", (9, 32, 128), F32), ("grad_fine_out", (32, 128, 128), F32),
           ("low_half", (HALF, 8, 128), B16), ("high_half", (HALF, 8, 128), B16))


def scratch():
    buffers = [
        ("w_qkv", (512, 1536), B16), ("w_out", (512, 512), B16), ("w_conv", (3, 3, 128, 128), B16),
        ("w_up", (512, 128), B16), ("turns", (5, 256, 256), B16), ("back", (384, 288), B16),
        ("got", (8, 32, 256), B16), ("turned", (16, 16, 256), B16), ("tokens", (16, 16, 256), B16),
        ("half", (8, 32, 256), B16), ("half_turned", (16, 16, 256), B16), ("half_got", (16, 16, 256), B16),
        ("half_cross", (8, 32, 256), B16), ("half_tokens", (8, 32, 256), B16),
        ("field", (40, 144, 128), B16), ("bins16", (32, 128), B16), ("bin_got", (64, 128), B16),
        ("edge_out", (2, 5, 16, 128), B16), ("edge_in", (2, 5, 16, 128), B16), ("bin_out", (2, 48, 128), B16),
        ("bin_in", (2, 48, 128), B16), ("rain", (48, 128), F32), ("edge_bins", (16, 128), F32),
        ("tok", (256, 512), B16), ("qkv", (256, 1536), B16), ("prob", (8, 512, 128), F32), ("mixed", (256, 512), B16),
        ("context", (256, 512), B16), ("raised", (16, 16, 128), B16),
        ("slots", (18, 16, 128), B16), ("lift_turned", (8, 48, 128), B16), ("lifted", (10, 48, 128), B16),
        ("query_turned", (8, 128, 512), B16), ("tok_turned", (512, 256), B16),
        ("hidden", (40, 144, 128), F32), ("slope", (40, 128, 128), F32), ("active", (40, 144, 384), B16),
        ("outer", (36, 144, 128), B16), ("taps", (36, 48, 128), B16), ("taps_turned", (36, 128, 48), B16),
        ("back_low", (48, 128), B16), ("back_mid", (48, 256), B16), ("back_high", (48, 128), B16),
        ("tap_sum", (144, 128), F32), ("pair", (1536, 256), B16), ("loss_sum", (16, 128), F32), ("head_sum", (16, 128), F32),
        ("dlift", (8, 32, 128), B16), ("grad_fine", (32, 128, 128), F32), ("quantiles", (9, 32, 128), F32),
        ("fold_got", (8, 32, 128), B16), ("fold_turned", (16, 16, 128), B16), ("folded", (16, 16, 128), B16),
        ("dquery", (256, 512), B16), ("dkey", (512, 256), B16), ("dvalue", (512, 256), B16),
    ]
    sems = [("s_l", 11), ("s_ur", 7), ("r_ur", 7), ("s_uc", 15), ("r_uc", 15), ("s_tr", 7), ("r_tr", 7), ("s_tc", 15), ("r_tc", 15), ("s_h", 4), ("r_h", 4), ("s_e", 4), ("r_e", 4),
            ("s_lc", 15), ("r_lc", 15), ("s_lx", 16), ("r_lx", 2), ("s_lr", 7), ("r_lr", 7), ("s_ly", 8), ("r_ly", 2),
            ("s_fr", 8), ("r_fr", 8), ("s_fc", 15), ("r_fc", 15)]
    return ([(name, pltpu.VMEM(shape, dtype)) for name, shape, dtype in buffers]
            + [(name, DMA((count,))) for name, count in sems]
            + reducer_scratch("a_", HALF) + reducer_scratch("b_", HALF))


def halo_rows(v, row):
    sends = [
        ((v.fine.at[pl.ds(30, 2)], v.field.at[pl.ds(2, 2), pl.ds(0, 128)], v.s_h.at[0], v.r_h.at[0]),
         (v.bins16.at[pl.ds(16, 16)], v.bin_got.at[pl.ds(0, 16)], v.s_h.at[1], v.r_h.at[1])),
        ((v.fine.at[pl.ds(0, 2)], v.field.at[pl.ds(36, 2), pl.ds(0, 128)], v.s_h.at[2], v.r_h.at[2]),
         (v.bins16.at[pl.ds(0, 16)], v.bin_got.at[pl.ds(48, 16)], v.s_h.at[3], v.r_h.at[3])),
    ]

    def start():
        @pl.when(row < 7)
        def _():
            for args in sends[0]:
                rcopy(*args, {"rows": row + 1}).start()

        @pl.when(row > 0)
        def _():
            for args in sends[1]:
                rcopy(*args, {"rows": row - 1}).start()

    def finish():
        @pl.when(row < 7)
        def _():
            for args in sends[0]:
                rcopy(*args, {"rows": row + 1}).wait_send()
            for args in sends[1]:
                rcopy(*args, {"rows": row + 1}).wait_recv()

        @pl.when(row > 0)
        def _():
            for args in sends[1]:
                rcopy(*args, {"rows": row - 1}).wait_send()
            for args in sends[0]:
                rcopy(*args, {"rows": row - 1}).wait_recv()

    return start, finish


def halo_cols(v, col):
    sends = [((v.edge_out.at[n], v.edge_in.at[n], v.s_e.at[2 * n], v.r_e.at[2 * n]),
              (v.bin_out.at[n], v.bin_in.at[n], v.s_e.at[2 * n + 1], v.r_e.at[2 * n + 1])) for n in range(2)]

    def start():
        @pl.when(col < 15)
        def _():
            for args in sends[0]:
                rcopy(*args, {"cols": col + 1}).start()

        @pl.when(col > 0)
        def _():
            for args in sends[1]:
                rcopy(*args, {"cols": col - 1}).start()

    def finish():
        @pl.when(col < 15)
        def _():
            for args in sends[0]:
                rcopy(*args, {"cols": col + 1}).wait_send()
            for args in sends[1]:
                rcopy(*args, {"cols": col + 1}).wait_recv()

        @pl.when(col > 0)
        def _():
            for args in sends[1]:
                rcopy(*args, {"cols": col - 1}).wait_send()
            for args in sends[0]:
                rcopy(*args, {"cols": col - 1}).wait_recv()

    return start, finish


def exchange_tokens(v, row, col, loads):
    low = [rcopy(v.coarse.at[p, :, pl.ds(0, 256)], v.got.at[row], v.s_tr.at[n], v.r_tr.at[n], {"rows": p})
           for n, p in enumerate(peer_order("rows", row))]
    for c in low:
        c.start()
    high = scatter_out("cols", v.half_turned, v.half_got, v.s_uc, v.r_uc, col)
    own = pltpu.make_async_copy(v.coarse.at[row, :, pl.ds(0, 256)], v.got.at[row], v.s_l.at[0])
    own.start()
    v.half_got[col] = v.half_turned[col]
    rows_start, rows_finish = halo_rows(v, row)
    rows_start()

    @pl.when(row == 0)
    def _():
        v.field[pl.ds(2, 2), :128] = jnp.zeros((2, 128, 128), B16)
        v.bin_got[pl.ds(0, 16)] = jnp.zeros((16, 128), B16)

    @pl.when(row == 7)
    def _():
        v.field[pl.ds(36, 2), :128] = jnp.zeros((2, 128, 128), B16)
        v.bin_got[pl.ds(48, 16)] = jnp.zeros((16, 128), B16)

    v.field[pl.ds(0, 2), :128] = jnp.zeros((2, 128, 128), B16)
    v.field[pl.ds(38, 2), :128] = jnp.zeros((2, 128, 128), B16)
    v.bin_got[pl.ds(16, 32)] = v.bins16[...]

    own.wait()
    wait_all(high)
    v.half_cross[...] = dot(v.turns[1], v.half_got[...].reshape(256, 256)).astype(B16).reshape(8, 32, 256)
    high = scatter_out("rows", v.half_cross, v.half_tokens, v.s_ur, v.r_ur, row)
    v.half_tokens[row] = v.half_cross[row]
    wait_all(low)
    v.turned[...] = dot(v.turns[0], v.got[...].reshape(256, 256)).astype(B16).reshape(16, 16, 256)
    low = scatter_out("cols", v.turned, v.tokens, v.s_tc, v.r_tc, col)
    v.tokens[col] = v.turned[col]

    loads[0].wait()
    rows_finish()
    rows = dot(v.place[...], v.bin_got[...])
    v.rain[...] = rows
    v.bin_out[0] = jnp.broadcast_to(rows[:, 127:128], (48, 128)).astype(B16)
    v.bin_out[1] = jnp.broadcast_to(rows[:, 0:1], (48, 128)).astype(B16)
    for q in range(5):
        v.edge_out[0, q] = dot(v.pick_hi[...], v.field[8 * q:8 * q + 8, 112:128].reshape(128, 128)).astype(B16)
        v.edge_out[1, q] = dot(v.pick_lo[...], v.field[8 * q:8 * q + 8, 0:16].reshape(128, 128)).astype(B16)
    cols_start, cols_finish = halo_cols(v, col)
    cols_start()

    @pl.when(col == 0)
    def _():
        v.edge_in[0] = jnp.zeros((5, 16, 128), B16)
        v.bin_in[0] = jnp.zeros((48, 128), B16)

    @pl.when(col == 15)
    def _():
        v.edge_in[1] = jnp.zeros((5, 16, 128), B16)
        v.bin_in[1] = jnp.zeros((48, 128), B16)

    wait_all(low)
    wait_all(high)
    return cols_finish


def attend(v):
    v.tok[:, :256] = dot(v.turns[2], v.tokens[...].reshape(256, 256)).astype(B16)
    v.tok[:, 256:] = dot(v.turns[3], v.half_tokens[...].reshape(256, 256)).astype(B16)
    for n in range(3):
        v.qkv[:, n * 512:(n + 1) * 512] = dot(v.tok[...], v.w_qkv[:, n * 512:(n + 1) * 512]).astype(B16)
    for g in range(2):
        for t in range(4):
            rows, at = slice(g * 128, g * 128 + 128), t * 128
            query = v.qkv[rows, at:at + 128]
            keyed = v.qkv[rows, 512 + at:512 + at + 128]
            valued = v.qkv[rows, 1024 + at:1024 + at + 128]
            scores = dot_nt(heads_down(query), keyed) * SCALE
            peak = jnp.max(scores, axis=-1, keepdims=True)
            powers = jnp.exp(scores - peak)
            share = powers / jnp.sum(powers, axis=-1, keepdims=True)
            v.prob[g * 4 + t] = share
            v.mixed[rows, at:at + 128] = dot(side_by_side(share.astype(B16)), heads_down(valued)).astype(B16)
    attended = dot(v.mixed[...], v.w_out[...]).astype(B16)
    v.context[...] = (v.tok[...].astype(F32) + attended.astype(F32)).astype(B16)
    lifted = dot(v.context[...], v.w_up[...]).astype(B16)
    v.raised[...] = dot(v.turns[4], lifted).astype(B16).reshape(16, 16, 128)


def edge_targets(v):
    lane = lax.broadcasted_iota(jnp.int32, (48, 128), 1)
    line = lax.broadcasted_iota(jnp.int32, (48, 128), 0)
    low, high = v.bin_in[0].astype(F32), v.bin_in[1].astype(F32)
    picked = jnp.where((lane & 15) == 0, high, jnp.where((lane & 15) == 15, low, 0.0))
    for b in range(9):
        here = line == 4 * b + (lane >> 4)
        v.edge_bins[b:b + 1] = jnp.sum(jnp.where(here, picked, 0.0), axis=0, keepdims=True)


def fold_copy(v, row, target, source):
    return rcopy(v.dlift.at[target], v.fold_got.at[source], v.s_fr.at[target], v.r_fr.at[source], {"rows": target})


def send_fold(v, row, target):
    @pl.when(row != target)
    def _():
        fold_copy(v, row, target, row).start()


def convolve(v, row, col):
    head_t = dot(v.eye[...], v.w_head_t[...]).astype(B16)
    place = lax.broadcasted_iota(jnp.int32, (144, 1), 0)
    right = jnp.where(col < 15, 130, 128)
    left = jnp.where(col > 0, 142, 144)
    inside = (place < right) | (place >= left)
    level = (lax.broadcasted_iota(jnp.int32, (16, 1), 0) + 1).astype(F32) / 10.0
    quant = lax.broadcasted_iota(jnp.int32, (16, 1), 0) < QUANT
    v.loss_sum[...] = jnp.zeros((16, 128), F32)
    v.head_sum[...] = jnp.zeros((16, 128), F32)
    v.tap_sum[...] = jnp.zeros((144, 128), F32)
    v.active[pl.ds(38, 2)] = jnp.zeros((2, 144, 384), B16)
    v.hidden[pl.ds(38, 2)] = jnp.zeros((2, 144, 128), F32)

    def start(i):
        raised = dot(v.up[...], v.lifted[i])
        rims = {0: (2, 3), 9: (0, 1)}.get(i, range(4))
        for s in rims:
            y = 4 * i + s - 4
            x = v.field[4 * i + s].astype(F32) + raised
            square = x * x
            bend = jnp.tanh(ROOT_2_PI * x * (1.0 + 0.044715 * square))
            half = 0.5 * (1.0 + bend)
            act = x * half
            if i in (0, 9):
                act = jnp.where(inside & (row * 32 + y >= 0) & (row * 32 + y < 256), act, 0.0)
            else:
                act = jnp.concatenate([act[:128], jnp.where(inside[128:], act[128:], 0.0)], axis=0)
            v.hidden[4 * i + s] = x
            v.active[4 * i + s] = shifted(act).astype(B16)
            v.slope[4 * i + s] = half[:128] + (0.5 * ROOT_2_PI) * x[:128] * (1.0 - bend[:128] * bend[:128]) * (
                1.0 + (3 * 0.044715) * square[:128])

    def forward(i):
        windows = [jnp.concatenate([v.active[4 * i + 2 + a], v.active[4 * i + 4 + a]], axis=0) for a in range(4)]
        both = dot(jnp.concatenate(windows, axis=1), v.pair[...])
        for s in range(4):
            at, part = s // 2 * 144, s % 2 * 128
            v.outer[4 * i + s] = (v.hidden[4 * i + 3 + s] + both[at:at + 144, part:part + 128]).astype(B16)

    def turn(i):
        own = v.outer[pl.ds(4 * i, 4), :128].reshape(512, 128)
        edge = v.outer[pl.ds(4 * i, 4), 128:144].reshape(64, 128)
        pixels = jnp.concatenate([own, edge, jnp.zeros((64, 128), B16)], axis=0)
        predicted = dot_nt(head_t, pixels)
        lines = [v.rain[pl.ds(4 * i + s, 1), :] for s in range(4)] + [v.edge_bins[pl.ds(i, 1), :]]
        target = jnp.concatenate(lines, axis=1) * (1.0 / 16.0) - 1.0
        lane = lax.broadcasted_iota(jnp.int32, (1, 640), 1)
        spot = lane - 512
        inner = lane < 512
        y = 4 * i - 1 + jnp.where(inner, lane >> 7, spot >> 4)
        side = (((spot & 15) == 0) & (col < 15)) | (((spot & 15) == 15) & (col > 0))
        seen = (row * 32 + y >= 0) & (row * 32 + y < 256) & (y < 33) & (inner | (side & (spot < 64)))
        mine = inner & (y >= 0) & (y < 32)
        error = target - predicted
        weight = jnp.where(error < 0.0, 1.0 - level, level)
        down = jnp.where(seen & quant, -weight * jnp.clip(error, -1.0, 1.0) * (1.0 / 1024.0), 0.0)
        size = jnp.abs(error)
        loss = weight * jnp.where(size <= 1.0, 0.5 * error * error, size - 0.5)
        loss = jnp.where(mine & quant, loss, 0.0)
        v.loss_sum[...] += loss[:, :128] + loss[:, 128:256] + loss[:, 256:384] + loss[:, 384:512]
        v.head_sum[...] += dot(jnp.where(mine, down, 0.0).astype(B16)[:, :512], own)
        edge = down[:, 512:]
        at = lax.broadcasted_iota(jnp.int32, (1, 128), 1)
        sets = []
        for s in range(4):
            line = down[:, s * 128:(s + 1) * 128]
            before = jnp.where(at == 0, pltpu.roll(edge, 113 - 16 * s, 1), pltpu.roll(line, 1, 1))
            after = jnp.where(at == 127, pltpu.roll(edge, 127 - 16 * s, 1), pltpu.roll(line, 127, 1))
            sets.append(jnp.concatenate([before, line, after], axis=0))
            v.taps[4 * i + s] = sets[s].astype(B16)
            row_y = 4 * i + s - 1
            value = predicted[:, s * 128:(s + 1) * 128]
            if 0 <= row_y < 32:
                for q in range(QUANT):
                    v.quantiles[q, pl.ds(row_y, 1), :] = value[q:q + 1]
        v.taps_turned[pl.ds(4 * i, 4)] = jnp.concatenate(sets, axis=1).T.astype(B16).reshape(4, 128, 48)

    def back(i):
        windows = [v.taps_turned[pl.ds(4 * i + a, 4)].reshape(512, 48) for a in range(3)]
        both = dot(windows[1], v.back_mid[...])
        dactive = both[:, :128] + dot(windows[0], v.back_low[...]) + dot(windows[2], v.back_high[...])
        dhidden = (both[:, 128:] + v.slope[pl.ds(4 * i + 4, 4)].reshape(512, 128) * dactive).reshape(4, 128, 128)
        v.grad_fine[pl.ds(4 * i, 4)] = dhidden * 1024.0
        summed = dhidden[0] + dhidden[1] + dhidden[2] + dhidden[3]
        high = summed.astype(B16)
        low = (summed - high.astype(F32)).astype(B16)
        v.dlift[i] = (dot(v.fold[...], high) + dot(v.fold[...], low)).astype(B16)
        lines = [jnp.concatenate([v.taps[4 * i + a + s] for s in range(4)], axis=1) for a in range(3)]
        seen = v.active[pl.ds(4 * i + 4, 4), :128, 128:256].reshape(512, 128)
        v.tap_sum[...] += dot(jnp.concatenate(lines, axis=0), seen)

    for t in range(10):
        start(t)
    for t in range(9):
        forward(t)
    for t in range(9):
        turn(t)
    for t in range(8):
        back(t)
        if t % 4 == 3:
            for n in range(t - 3, t + 1):
                send_fold(v, row, n)


def back_weights(v):
    head_t = dot(v.eye[...], v.w_head_t[...]).astype(B16)
    for a, name in enumerate(("back_low", "back_mid", "back_high")):
        parts = [dot_nt(head_t, v.w_conv[2 - a, 2 - b]).astype(B16) for b in range(3)]
        getattr(v, name)[:, :128] = jnp.concatenate(parts, axis=0)
    for a in range(4):
        for b in range(2):
            block = v.w_conv[a - b].reshape(384, 128) if 0 <= a - b < 3 else jnp.zeros((384, 128), B16)
            v.pair[a * 384:(a + 1) * 384, b * 128:(b + 1) * 128] = block
    blank = jnp.zeros((16, 128), B16)
    v.back_mid[:, 128:] = jnp.concatenate([blank, head_t, blank], axis=0)


def local_units(v):
    v.a_g[448:466] = v.tap_sum[...].reshape(18, 8, 128).astype(B16)
    spot = lax.broadcasted_iota(jnp.int32, (16, 1), 0)
    total = jnp.sum(v.loss_sum[...], axis=0, keepdims=True)
    tail = jnp.where(spot < QUANT, v.head_sum[...], jnp.where(spot == QUANT, total, 0.0))
    v.a_g[466:468] = tail.reshape(2, 8, 128).astype(B16)
    v.a_g[468:HALF] = jnp.zeros((HALF - 468, 8, 128), B16)
    v.b_g[448:HALF] = jnp.zeros((HALF - 448, 8, 128), B16)


def attend_back(v, mix_grad, g, tiles):
    for s, t in [(s, t) for s in range(2) for t in tiles]:
        rows, at = slice(s * 128, s * 128 + 128), t * 128
        keyed = v.qkv[rows, 512 + at:512 + at + 128]
        valued = v.qkv[rows, 1024 + at:1024 + at + 128]
        mine = mix_grad[rows, at:at + 128]
        dprob = dot_nt(heads_down(mine), valued)
        share = v.prob[s * 4 + t]
        inner = jnp.sum(share * dprob, axis=-1, keepdims=True)
        dscore = (share * (dprob - inner) * SCALE).astype(B16)
        v.dquery[rows, at:at + 128] = dot(side_by_side(dscore), heads_down(keyed)).astype(B16)
        v.dkey[at:at + 128, rows] = dot(v.query_turned[s * 4 + t], dscore).astype(B16)
        v.dvalue[at:at + 128, rows] = dot(heads_across(mine), share.astype(B16)).astype(B16)
    at = tiles[0] * 128
    put(g, 0, dot(v.tok_turned[...], v.dquery[:, at:at + 256]))
    put(g, 128, dot_nt(v.tok_turned[...], v.dkey[at:at + 256]))
    put(g, 256, dot_nt(v.tok_turned[...], v.dvalue[at:at + 256]))


def whole_kernel(names, *refs):
    v = SimpleNamespace(**dict(zip(names, refs)))
    row, col, batch = lax.axis_index("rows"), lax.axis_index("cols"), lax.axis_index("batch")
    core, deep = row % 2, (row // 2) * 2 + batch
    x, y = col // 4, col % 4
    me = SimpleNamespace(
        core=core, deep=deep, other={"rows": row + 1 - 2 * core},
    )
    x_axis = (x, lambda k: {"cols": ((x + k) % 4) * 4 + y})
    y_axis = (y, lambda k: {"cols": x * 4 + (y + k) % 4})

    def in_deep(k):
        p = (deep + k) % 8
        return {"rows": (p // 2) * 2 + core, "batch": p % 2}

    me.in_deep = in_deep

    peers = [{"rows": p} for p in peer_order("rows", row)]
    peers = peers[:2] + [{"rows": (row + 2 * k) % 8, "batch": 1 - batch} for k in (2, 1, 3, 0)] + peers[2:6] + [
        {"cols": p} for p in peer_order("cols", col)] + peers[6:]
    barrier = pltpu.get_barrier_semaphore()
    for peer in peers:
        pl.semaphore_signal(barrier, inc=1, device_id=peer, device_id_type=MESH)
    loads = [pltpu.make_async_copy(v.fine, v.field.at[pl.ds(4, 32), pl.ds(0, 128)], v.s_l.at[1]),
             pltpu.make_async_copy(v.w_qkv_in, v.w_qkv, v.s_l.at[2]),
             pltpu.make_async_copy(v.w_out_in, v.w_out, v.s_l.at[3]),
             pltpu.make_async_copy(v.w_conv_in, v.w_conv, v.s_l.at[4]),
             pltpu.make_async_copy(v.coarse.at[:, :, pl.ds(256, 256)], v.half, v.s_l.at[7]),
             pltpu.make_async_copy(v.turns_in, v.turns, v.s_l.at[8]),
             pltpu.make_async_copy(v.w_up_in, v.w_up, v.s_l.at[9]),
             pltpu.make_async_copy(v.back_in, v.back, v.s_l.at[10])]
    for n in (4, 5, 0, 1, 2, 6, 3, 7):
        loads[n].start()
    v.bins16[...] = v.bins[...].astype(F32).astype(B16)
    loads[4].wait()
    loads[5].wait()
    v.half_turned[...] = dot(v.turns[0], v.half[...].reshape(256, 256)).astype(B16).reshape(16, 16, 256)
    pl.semaphore_wait(barrier, len(peers))
    cols_finish = exchange_tokens(v, row, col, loads)
    loads[1].wait()
    loads[2].wait()
    loads[6].wait()
    loads[7].wait()
    attend(v)

    finish = spread_out("cols", 16, col, v.raised, v.slots, v.s_lc, v.r_lc, v.s_lx, v.r_lx)
    cols_finish()
    for q in range(5):
        edge = dot(v.spread_hi[...], v.edge_in[0, q]) + dot(v.spread_lo[...], v.edge_in[1, q])
        v.field[8 * q:8 * q + 8, 128:144] = edge.astype(B16).reshape(8, 16, 128)
    edge_targets(v)
    for s in range(2):
        for t in range(4):
            v.query_turned[s * 4 + t] = heads_across(v.qkv[s * 128:s * 128 + 128, t * 128:t * 128 + 128])
    finish()
    v.lift_turned[...] = dot(v.back[...], v.slots[...].reshape(288, 128)).astype(B16).reshape(8, 48, 128)
    finish = spread_out("rows", 8, row, v.lift_turned, v.lifted, v.s_lr, v.r_lr, v.s_ly, v.r_ly)
    v.tok_turned[...] = v.tok[...].astype(F32).T.astype(B16)
    loads[3].wait()
    back_weights(v)
    finish()

    convolve(v, row, col)

    results = [pltpu.make_async_copy(v.grad_fine, v.grad_fine_out, v.s_l.at[5]),
               pltpu.make_async_copy(v.quantiles, v.quantiles_out, v.s_l.at[6])]
    v.fold_got[row] = v.dlift[row]
    for c in results:
        c.start()
    local_units(v)
    for p in peer_order("rows", row):
        fold_copy(v, row, p, p).wait()
    v.fold_turned[...] = dot(v.turns[0], v.fold_got[...].reshape(256, 128)).astype(B16).reshape(16, 16, 128)
    sends = scatter_out("cols", v.fold_turned, v.folded, v.s_fc, v.r_fc, col)
    v.folded[col] = v.fold_turned[col]
    wait_all(sends)

    low = reducer(me, (x_axis, y_axis), HALF, v.a_g, v.a_out, v.low_half, v.a_got0, v.a_sum0, v.a_got1, v.a_sum1, v.a_got2, v.a_sum2,
                  v.a_got3, [getattr(v, "a_sem" + str(n)) for n in range(18)])
    high = reducer(me, (y_axis, x_axis), HALF, v.b_g, v.b_out, v.high_half, v.b_got0, v.b_sum0, v.b_got1, v.b_sum1, v.b_got2, v.b_sum2,
                   v.b_got3, [getattr(v, "b_sem" + str(n)) for n in range(18)])
    lift_wide = dot(v.turns[2], v.folded[...].reshape(256, 128))
    lift, lift_turned = lift_wide.astype(B16), lift_wide.T.astype(B16)
    dcontext = dot_nt(lift, v.w_up[...]).astype(B16)
    mix_grad = dot_nt(dcontext, v.w_out[...]).astype(B16)
    put(v.a_g, 384, dot(lift_turned, v.mixed[...]))
    put(v.b_g, 384, dot(lift_turned, v.context[...]))
    attend_back(v, mix_grad, v.a_g, (0, 1))
    low[0]()
    attend_back(v, mix_grad, v.b_g, (2, 3))
    high[0]()
    low[1]()
    high[1]()
    for n in range(2, 9):
        low[n]()
        high[n]()
    wait_all(results)


def unpack_kernel(low, high, fine, quantiles, w_up, w_head_t, eye,
                  grad_qkv, grad_out, grad_up, grad_conv, grad_head, loss, fine_out, quantiles_out,
                  held, wide, square, tall, flat, fine_in, bands_in, sems):
    through = [(fine.at[pl.ds(n * 8, 8)], fine_in.at[pl.ds(n * 8, 8)], fine_out.at[pl.ds(n * 8, 8)]) for n in range(4)]
    through.append((quantiles, bands_in, quantiles_out))
    passing = [pltpu.make_async_copy(src, held, sems.at[12 + n]) for n, (src, held, _) in enumerate(through)]
    reads = [pltpu.make_async_copy((low, high)[h].at[pl.ds(a, b)], held.at[h, pl.ds(a, b)], sems.at[2 * n + h])
             for n, (a, b) in enumerate(((0, 384), (384, HALF - 384))) for h in range(2)]
    for c in passing + reads[2:] + reads[:2]:
        c.start()
    writes = []

    def write(src, dst, n):
        c = pltpu.make_async_copy(src, dst, sems.at[n])
        c.start()
        writes.append(c)

    for m in range(5):
        passing[m].wait()
        write(through[m][1], through[m][2], 17 + m)
    reads[2].wait()
    reads[3].wait()
    for n in range(4):
        mixed = held[0, 384 + n * 16:384 + (n + 1) * 16].astype(F32).reshape(128, 128).T.astype(B16)
        square[n * 128:(n + 1) * 128] = dot_nt(mixed, w_up[...])
        tall[n * 128:(n + 1) * 128] = held[1, 384 + n * 16:384 + (n + 1) * 16].astype(F32).reshape(128, 128).T
    write(square, grad_out, 9)
    write(tall, grad_up, 10)
    head_t = dot(eye[...], w_head_t[...]).astype(B16)
    for a in range(3):
        for b in range(3):
            at = 448 + (2 - a) * 6 + (2 - b) * 2
            seen = held[0, at:at + 2].astype(F32).reshape(16, 128).T.astype(B16)
            flat[(a * 3 + b) * 128:(a * 3 + b + 1) * 128] = dot(seen, head_t)
    write(flat, grad_conv, 11)
    for h in range(2):
        reads[h].wait()
        for n in range(3):
            for m in range(2):
                at = n * 128 + m * 64
                wide[h * 3 + n, :, m * 128:(m + 1) * 128] = held[h, at:at + 64].astype(F32).reshape(512, 128)
            write(wide.at[h * 3 + n], grad_qkv.at[:, pl.ds(n * 512 + h * 256, 256)], 22 + h * 3 + n)
    tail = held[0, 466:468].astype(F32).reshape(16, 128)
    grad_head[...] = tail[:QUANT]
    loss[...] = jnp.sum(tail[QUANT:QUANT + 1], axis=1, keepdims=True) * (1.0 / (1048576.0 * QUANT))
    wait_all(writes)


def body(fine_input, coarse, rain_bins, w_qkv, w_out, w_up, w_conv, w_head):
    mid, group = mid_table(), group_table()
    turns = jnp.stack([mid, mid.T, group, cross_table(), group.T])
    eye = onehot(16, QUANT, [(q, q) for q in range(QUANT)])
    args = [coarse[0], fine_input[0], rain_bins[0], w_qkv, w_out, w_up, w_conv, w_head.T,
            turns, back_table(), pick_table(0), pick_table(14), spread_table(0), spread_table(14),
            bins_table(), up_table(), sum_table(), eye]
    spaces = scratch()
    names = INPUTS + tuple(name for name, _, _ in OUTPUTS) + tuple(name for name, _ in spaces)
    vmem, anywhere = pl.BlockSpec(memory_space=pltpu.VMEM), pl.BlockSpec(memory_space=pl.ANY)

    def kernel(*refs):
        whole_kernel(names, *refs)

    quantiles, grad_fine, low, high = pl.pallas_call(
        kernel,
        out_shape=[jax.ShapeDtypeStruct(shape, dtype) for _, shape, dtype in OUTPUTS],
        in_specs=[pl.BlockSpec(memory_space=pl.ANY) if name in IN_HBM else vmem for name in INPUTS],
        out_specs=[anywhere] * 4,
        scratch_shapes=[space for _, space in spaces],
        compiler_params=pltpu.CompilerParams(vmem_limit_bytes=LIMIT, collective_id=1, has_side_effects=True),
    )(*args)
    shapes = ((512, 1536), (512, 512), (512, 128), (1152, 128), (QUANT, 128), (1, 1), (32, 128, 128), (9, 32, 128))
    grad_qkv, grad_out, grad_up, grad_conv, grad_head, loss, fine, bands = pl.pallas_call(
        unpack_kernel,
        out_shape=[jax.ShapeDtypeStruct(shape, F32) for shape in shapes],
        in_specs=[anywhere] * 4 + [vmem] * 3,
        out_specs=[anywhere] * 4 + [vmem] * 2 + [anywhere] * 2,
        scratch_shapes=[pltpu.VMEM((2, HALF, 8, 128), B16), pltpu.VMEM((6, 512, 256), F32),
                        pltpu.VMEM((512, 512), F32), pltpu.VMEM((512, 128), F32), pltpu.VMEM((1152, 128), F32),
                        pltpu.VMEM((32, 128, 128), F32), pltpu.VMEM((9, 32, 128), F32), DMA((28,))],
        compiler_params=pltpu.CompilerParams(vmem_limit_bytes=LIMIT),
    )(low, high, grad_fine, quantiles, w_up, w_head.T, eye)
    return (bands[None], loss.reshape(()), grad_qkv, grad_out, grad_up, grad_conv.reshape(3, 3, 128, 128),
            grad_head.T, fine[None])


def solution(mesh):
    placed = (
        P("batch", "rows", "cols", None),
        P("batch", "rows", "cols", None),
        P("batch", "rows", "cols"),
        P(),
        P(),
        P(),
        P(),
        P(),
    )
    return jax.shard_map(
        body,
        mesh=mesh,
        in_specs=placed,
        out_specs=(
            P("batch", None, "rows", "cols"),
            P(),
            P(),
            P(),
            P(),
            P(),
            P(),
            P("batch", "rows", "cols", None),
        ),
        check_vma=False,
    )
```

```python
import functools
import jax
import jax.numpy as jnp
import numpy as np
from types import SimpleNamespace
from jax import lax
from jax.experimental import pallas as pl
from jax.experimental.pallas import tpu as pltpu
from jax.sharding import PartitionSpec as P

HEAD_DIM = 32
QUANT = 9
MESH = pl.DeviceIdType.MESH
F32, B16 = jnp.float32, jnp.bfloat16
DMA = pltpu.SemaphoreType.DMA
SCALE = HEAD_DIM ** (-0.5)
ROOT_2_PI = 0.7978845608028654
LIMIT = 58 * 1024 * 1024
HALF, SHARES = 480, 5


def onehot(rows, cols, pairs):
    table = np.zeros((rows, cols), np.float32)
    for row, col in pairs:
        table[row, col] = 1.0
    return jnp.asarray(table, B16)


def mid_table():
    return onehot(256, 256, [(p * 16 + r * 2 + m, r * 32 + p * 2 + m)
                             for p in range(16) for r in range(8) for m in range(2)])


def group_table():
    return onehot(256, 256, [(m * 128 + c * 8 + r, c * 16 + r * 2 + m)
                             for m in range(2) for c in range(16) for r in range(8)])


def cross_table():
    return onehot(256, 256, [(m * 128 + c * 8 + r, r * 32 + c * 2 + m)
                             for m in range(2) for c in range(16) for r in range(8)])


def back_table():
    pairs = []
    for r in range(8):
        for j in range(32):
            pairs.append((r * 48 + j, (1 + j // 2) * 16 + r * 2 + j % 2))
        pairs.append((r * 48 + 32, 17 * 16 + r * 2))
        pairs.append((r * 48 + 35, r * 2 + 1))
    return onehot(384, 288, pairs)


def pick_table(first):
    return onehot(16, 128, [(2 * i + s, 16 * i + first + s) for i in range(8) for s in range(2)])


def spread_table(first):
    return onehot(128, 16, [(16 * i + first + s, 2 * i + s) for i in range(8) for s in range(2)])


def bins_table():
    return onehot(48, 64, [(0, 15)] + [(1 + y, 16 + y) for y in range(32)] + [(33, 48)])


def up_table():
    return onehot(144, 48, [(p, p // 4) for p in range(144)])


def sum_table():
    return onehot(32, 128, [(p // 4, p) for p in range(128)])


def dot(a, b):
    return jnp.dot(a, b, preferred_element_type=F32)


def dot_nt(a, b):
    return lax.dot_general(a, b, (((1,), (1,)), ((), ())), preferred_element_type=F32)


def rcopy(src, dst, send, recv, to):
    return pltpu.make_async_remote_copy(src_ref=src, dst_ref=dst, send_sem=send, recv_sem=recv,
                                        device_id=to, device_id_type=MESH)


def wait_all(copies):
    for c in copies:
        c.wait()


def peer_order(axis, me):
    if axis == "rows":
        steps = [(2, 0), (2, 1), (1, 0), (3, 0), (1, 1), (3, 1), (0, 1)]
        return [((me // 2 + a) % 4) * 2 + (me + b) % 2 for a, b in steps]
    steps = [(a, b) for a in range(4) for b in range(4) if a + b > 0]
    steps.sort(key=lambda step: -min(step[0], 4 - step[0]) - min(step[1], 4 - step[1]))
    return [((me // 4 + a) % 4) * 4 + (me + b) % 4 for a, b in steps]


def scatter_out(axis, src, got, send, recv, me):
    copies = []
    for n, p in enumerate(peer_order(axis, me)):
        c = rcopy(src.at[p], got.at[me], send.at[n], recv.at[n], {axis: p})
        c.start()
        copies.append(c)
    return copies


def spread_out(axis, count, me, src, main, send, recv, send_x, recv_x):
    copies = []
    for n, p in enumerate(peer_order(axis, me)):
        c = rcopy(src.at[p], main.at[1 + me], send.at[n], recv.at[n], {axis: p})
        c.start()
        copies.append(c)
    main[1 + me] = src[me]

    def after(t):
        return rcopy(src.at[t - 1], main.at[0], send_x.at[t], recv_x.at[0], {axis: t})

    def before(t):
        return rcopy(src.at[t + 1], main.at[count + 1], send_x.at[t], recv_x.at[1], {axis: t})

    @pl.when(me == count - 1)
    def _():
        for t in range(1, count - 1):
            after(t).start()
        main[0] = src[count - 2]
        main[count + 1] = jnp.zeros(main.shape[1:], B16)

    @pl.when(me == 0)
    def _():
        for t in range(1, count - 1):
            before(t).start()
        main[count + 1] = src[1]
        main[0] = jnp.zeros(main.shape[1:], B16)

    def finish():
        @pl.when(me == count - 1)
        def _():
            for t in range(1, count - 1):
                after(t).wait_send()

        @pl.when(me == 0)
        def _():
            for t in range(1, count - 1):
                before(t).wait_send()

        @pl.when((me > 0) & (me < count - 1))
        def _():
            after(1).wait_recv()
            before(1).wait_recv()

        wait_all(copies)

    return finish


def head_mask(h):
    lane = lax.broadcasted_iota(jnp.int32, (1, 128), 1)
    return jnp.where((lane >> 5) == h, 1.0, 0.0).astype(B16)


def heads_down(tile):
    return jnp.concatenate([tile * head_mask(h) for h in range(4)], axis=0)


def heads_across(tile):
    turned = tile.astype(F32).T
    line = lax.broadcasted_iota(jnp.int32, (128, 1), 0) >> 5
    return jnp.concatenate([jnp.where(line == h, turned, 0.0) for h in range(4)], axis=1).astype(B16)


def side_by_side(stack):
    return jnp.concatenate([stack[h * 128:(h + 1) * 128] for h in range(4)], axis=1)


def put(g, at, value):
    rows, cols = value.shape
    size = rows // 8
    for n in range(cols // 128):
        g[at + n * size:at + (n + 1) * size] = value[:, n * 128:(n + 1) * 128].reshape(size, 8, 128).astype(B16)


def shifted(line):
    return jnp.concatenate([pltpu.roll(line, 1, 0), line, pltpu.roll(line, 143, 0)], axis=1)


def reducer(me, axes, units, g, out, dest, got0, sum0, got1, sum1, got2, sum2, got3, sems):
    core, deep = me.core, me.deep
    (first, in_first), (second, in_second) = axes
    u0, u1, u2, u3 = units // 2, units // 8, units // 32, units // (32 * SHARES)
    s0, r0, s1, r1, s2, r2, s3, r3, as3, ar3, as2, ar2, as1, ar1, as0, ar0, w0, w1 = sems
    place = core * u0 + first * u1 + second * u2
    held = {}

    def sum_up(terms):
        total = terms[0].astype(F32)
        for term in terms[1:]:
            total = total + term.astype(F32)
        return total

    def near_start():
        held["near"] = []
        for n, k in enumerate((1, 2, 3, 0)):
            p = (first + k) % 4
            c = rcopy(g.at[pl.ds((1 - core) * u0 + p * u1, u1)], got0.at[p], s0.at[n], r0.at[n], me.other)
            c.start()
            held["near"].append(c)

    def first_start():
        held["first"] = []
        for n, k in enumerate((1, 2, 3)):
            p = (first + k) % 4
            held["near"][n].wait_recv()
            sum0[p] = sum_up([g[pl.ds(core * u0 + p * u1, u1)], got0[p]]).astype(B16)
            c = rcopy(sum0.at[p], got1.at[k - 1], s1.at[k - 1], r1.at[k - 1], in_first(k))
            c.start()
            held["first"].append(c)
        held["near"][3].wait_recv()

    def second_start():
        wait_all(held["first"])
        sum1[...] = sum_up([g[pl.ds(core * u0 + first * u1, u1)], got0[first], got1[0], got1[1], got1[2]]).astype(B16)
        held["second"] = []
        for k in (1, 2, 3):
            p = (second + k) % 4
            c = rcopy(sum1.at[pl.ds(p * u2, u2)], got2.at[k - 1], s2.at[k - 1], r2.at[k - 1], in_second(k))
            c.start()
            held["second"].append(c)
        for c in held["near"]:
            c.wait_send()

    def deep_start():
        wait_all(held["second"])
        sum2[...] = sum_up([sum1[pl.ds(second * u2, u2)], got2[0], got2[1], got2[2]]).astype(B16)
        for k in (4, 3, 5, 2, 6, 1, 7):
            pl.when((deep + k) % 8 < SHARES)(functools.partial(deep_send, k))

    def deep_copy(k, share):
        return rcopy(sum2.at[pl.ds(share * u3, u3)], got3.at[k - 1], s3.at[k - 1], r3.at[k - 1], me.in_deep(k))

    def deep_send(k):
        deep_copy(k, (deep + k) % 8).start()

    def deep_sent(k):
        deep_copy(k, 0).wait_send()

    def deep_back(k, share):
        block = out.at[pl.ds(place + share * u3, u3)]
        return rcopy(block, block, as3.at[k - 1], ar3.at[k - 1], me.in_deep(k))

    def deep_here(k):
        deep_back(k, 0).wait_recv()

    def deep_gather():
        for k in range(1, 8):
            pl.when((deep + k) % 8 < SHARES)(functools.partial(deep_sent, k))

        @pl.when(deep < SHARES)
        def _():
            for k in range(1, 8):
                deep_copy(k, 0).wait_recv()
            mine = sum_up([sum2[pl.ds(deep * u3, u3)]] + [got3[k] for k in range(7)])
            out[pl.ds(place + deep * u3, u3)] = mine.astype(B16)
            for k in (4, 3, 5, 2, 6, 1, 7):
                deep_back(k, deep).start()

    def second_gather():
        @pl.when(deep < SHARES)
        def _():
            for k in range(1, 8):
                deep_back(k, 0).wait_send()

        for k in range(1, 8):
            pl.when((deep + 8 - k) % 8 < SHARES)(functools.partial(deep_here, k))
        block = out.at[pl.ds(place, u2)]
        held["second"] = []
        for k in (1, 2, 3):
            c = rcopy(block, block, as2.at[k - 1], ar2.at[k - 1], in_second(k))
            c.start()
            held["second"].append(c)

    def leave(at, sem):
        block = pl.ds(at, u1)
        c = pltpu.make_async_copy(out.at[block], dest.at[block], sem)
        c.start()
        held["leave"].append(c)

    def forward(n, p):
        block = out.at[pl.ds(core * u0 + p * u1, u1)]
        c = rcopy(block, block, as0.at[n], ar0.at[n], me.other)
        c.start()
        held["near"].append(c)
        leave(core * u0 + p * u1, w0.at[n])

    def first_gather():
        wait_all(held["second"])
        block = out.at[pl.ds(core * u0 + first * u1, u1)]
        held["first"], held["near"], held["leave"] = [], [], []
        for k in (1, 2, 3):
            c = rcopy(block, block, as1.at[k - 1], ar1.at[k - 1], in_first(k))
            c.start()
            held["first"].append(c)
        forward(0, first)

    def near_gather():
        for k in (1, 2, 3):
            held["first"][k - 1].wait_recv()
            forward(k, (first + 4 - k) % 4)

    def finish():
        for n, c in enumerate(held["near"]):
            c.wait_recv()
            leave((1 - core) * u0 + (first + 4 - n) % 4 * u1, w1.at[n])
        for c in held["first"] + held["near"]:
            c.wait_send()
        wait_all(held["leave"])

    return [near_start, first_start, second_start, deep_start, deep_gather, second_gather, first_gather,
            near_gather, finish]


def reducer_scratch(tag, units):
    unit = (8, 128)
    u1, u2, u3 = units // 8, units // 32, units // (32 * SHARES)
    shapes = [("g", (units,) + unit), ("out", (units,) + unit), ("got0", (4, u1) + unit), ("sum0", (4, u1) + unit), ("got1", (3, u1) + unit),
              ("sum1", (u1,) + unit), ("got2", (3, u2) + unit), ("sum2", (u2,) + unit), ("got3", (7, u3) + unit)]
    result = [(tag + name, pltpu.VMEM(shape, B16)) for name, shape in shapes]
    for n, count in enumerate((4, 4, 3, 3, 3, 3, 7, 7, 7, 7, 3, 3, 3, 3, 4, 4, 4, 4)):
        result.append((tag + "sem" + str(n), DMA((count,))))
    return result


INPUTS = ("coarse", "fine", "bins", "w_qkv_in", "w_out_in", "w_up_in", "w_conv_in", "w_head_t",
          "turns_in", "back_in", "pick_lo", "pick_hi", "spread_lo", "spread_hi", "place", "up", "fold", "eye")
IN_HBM = ("coarse", "fine", "w_qkv_in", "w_out_in", "w_up_in", "w_conv_in", "turns_in", "back_in")
OUTPUTS = (("quantiles_out", (9, 32, 128), F32), ("grad_fine_out", (32, 128, 128), F32),
           ("low_half", (HALF, 8, 128), B16), ("high_half", (HALF, 8, 128), B16))


def scratch():
    buffers = [
        ("w_qkv", (512, 1536), B16), ("w_out", (512, 512), B16), ("w_conv", (3, 3, 128, 128), B16),
        ("w_up", (512, 128), B16), ("turns", (5, 256, 256), B16), ("back", (384, 288), B16),
        ("got", (8, 32, 256), B16), ("turned", (16, 16, 256), B16), ("tokens", (16, 16, 256), B16),
        ("half", (8, 32, 256), B16), ("half_turned", (16, 16, 256), B16), ("half_got", (16, 16, 256), B16),
        ("half_cross", (8, 32, 256), B16), ("half_tokens", (8, 32, 256), B16),
        ("field", (40, 144, 128), B16), ("bins16", (32, 128), B16), ("bin_got", (64, 128), B16),
        ("edge_out", (2, 5, 16, 128), B16), ("edge_in", (2, 5, 16, 128), B16), ("bin_out", (2, 48, 128), B16),
        ("bin_in", (2, 48, 128), B16), ("rain", (48, 128), F32), ("edge_bins", (16, 128), F32),
        ("tok", (256, 512), B16), ("qkv", (256, 1536), B16), ("prob", (8, 512, 128), F32), ("mixed", (256, 512), B16),
        ("context", (256, 512), B16), ("raised", (16, 16, 128), B16),
        ("slots", (18, 16, 128), B16), ("lift_turned", (8, 48, 128), B16), ("lifted", (10, 48, 128), B16),
        ("query_turned", (8, 128, 512), B16), ("tok_turned", (512, 256), B16),
        ("hidden", (40, 144, 128), F32), ("slope", (40, 128, 128), F32), ("active", (40, 144, 384), B16),
        ("outer", (36, 144, 128), B16), ("taps", (36, 48, 128), B16), ("taps_turned", (36, 128, 48), B16),
        ("back_low", (48, 128), B16), ("back_mid", (48, 256), B16), ("back_high", (48, 128), B16),
        ("tap_sum", (144, 128), F32), ("pair", (1536, 256), B16), ("loss_sum", (16, 128), F32), ("head_sum", (16, 128), F32),
        ("dlift", (8, 32, 128), B16), ("grad_fine", (32, 128, 128), F32), ("quantiles", (9, 32, 128), F32),
        ("fold_got", (8, 32, 128), B16), ("fold_turned", (16, 16, 128), B16), ("folded", (16, 16, 128), B16),
        ("dquery", (256, 512), B16), ("dkey", (512, 256), B16), ("dvalue", (512, 256), B16),
    ]
    sems = [("s_l", 11), ("s_ur", 7), ("r_ur", 7), ("s_uc", 15), ("r_uc", 15), ("s_tr", 7), ("r_tr", 7), ("s_tc", 15), ("r_tc", 15), ("s_h", 4), ("r_h", 4), ("s_e", 4), ("r_e", 4),
            ("s_lc", 15), ("r_lc", 15), ("s_lx", 16), ("r_lx", 2), ("s_lr", 7), ("r_lr", 7), ("s_ly", 8), ("r_ly", 2),
            ("s_fr", 8), ("r_fr", 8), ("s_fc", 15), ("r_fc", 15)]
    return ([(name, pltpu.VMEM(shape, dtype)) for name, shape, dtype in buffers]
            + [(name, DMA((count,))) for name, count in sems]
            + reducer_scratch("a_", HALF) + reducer_scratch("b_", HALF))


def halo_rows(v, row):
    sends = [
        ((v.fine.at[pl.ds(30, 2)], v.field.at[pl.ds(2, 2), pl.ds(0, 128)], v.s_h.at[0], v.r_h.at[0]),
         (v.bins16.at[pl.ds(16, 16)], v.bin_got.at[pl.ds(0, 16)], v.s_h.at[1], v.r_h.at[1])),
        ((v.fine.at[pl.ds(0, 2)], v.field.at[pl.ds(36, 2), pl.ds(0, 128)], v.s_h.at[2], v.r_h.at[2]),
         (v.bins16.at[pl.ds(0, 16)], v.bin_got.at[pl.ds(48, 16)], v.s_h.at[3], v.r_h.at[3])),
    ]

    def start():
        @pl.when(row < 7)
        def _():
            for args in sends[0]:
                rcopy(*args, {"rows": row + 1}).start()

        @pl.when(row > 0)
        def _():
            for args in sends[1]:
                rcopy(*args, {"rows": row - 1}).start()

    def finish():
        @pl.when(row < 7)
        def _():
            for args in sends[0]:
                rcopy(*args, {"rows": row + 1}).wait_send()
            for args in sends[1]:
                rcopy(*args, {"rows": row + 1}).wait_recv()

        @pl.when(row > 0)
        def _():
            for args in sends[1]:
                rcopy(*args, {"rows": row - 1}).wait_send()
            for args in sends[0]:
                rcopy(*args, {"rows": row - 1}).wait_recv()

    return start, finish


def halo_cols(v, col):
    sends = [((v.edge_out.at[n], v.edge_in.at[n], v.s_e.at[2 * n], v.r_e.at[2 * n]),
              (v.bin_out.at[n], v.bin_in.at[n], v.s_e.at[2 * n + 1], v.r_e.at[2 * n + 1])) for n in range(2)]

    def start():
        @pl.when(col < 15)
        def _():
            for args in sends[0]:
                rcopy(*args, {"cols": col + 1}).start()

        @pl.when(col > 0)
        def _():
            for args in sends[1]:
                rcopy(*args, {"cols": col - 1}).start()

    def finish():
        @pl.when(col < 15)
        def _():
            for args in sends[0]:
                rcopy(*args, {"cols": col + 1}).wait_send()
            for args in sends[1]:
                rcopy(*args, {"cols": col + 1}).wait_recv()

        @pl.when(col > 0)
        def _():
            for args in sends[1]:
                rcopy(*args, {"cols": col - 1}).wait_send()
            for args in sends[0]:
                rcopy(*args, {"cols": col - 1}).wait_recv()

    return start, finish


def exchange_tokens(v, row, col, loads):
    low = [rcopy(v.coarse.at[p, :, pl.ds(0, 256)], v.got.at[row], v.s_tr.at[n], v.r_tr.at[n], {"rows": p})
           for n, p in enumerate(peer_order("rows", row))]
    for c in low:
        c.start()
    high = scatter_out("cols", v.half_turned, v.half_got, v.s_uc, v.r_uc, col)
    own = pltpu.make_async_copy(v.coarse.at[row, :, pl.ds(0, 256)], v.got.at[row], v.s_l.at[0])
    own.start()
    v.half_got[col] = v.half_turned[col]
    rows_start, rows_finish = halo_rows(v, row)
    rows_start()

    @pl.when(row == 0)
    def _():
        v.field[pl.ds(2, 2), :128] = jnp.zeros((2, 128, 128), B16)
        v.bin_got[pl.ds(0, 16)] = jnp.zeros((16, 128), B16)

    @pl.when(row == 7)
    def _():
        v.field[pl.ds(36, 2), :128] = jnp.zeros((2, 128, 128), B16)
        v.bin_got[pl.ds(48, 16)] = jnp.zeros((16, 128), B16)

    v.field[pl.ds(0, 2), :128] = jnp.zeros((2, 128, 128), B16)
    v.field[pl.ds(38, 2), :128] = jnp.zeros((2, 128, 128), B16)
    v.bin_got[pl.ds(16, 32)] = v.bins16[...]

    own.wait()
    wait_all(high)
    v.half_cross[...] = dot(v.turns[1], v.half_got[...].reshape(256, 256)).astype(B16).reshape(8, 32, 256)
    high = scatter_out("rows", v.half_cross, v.half_tokens, v.s_ur, v.r_ur, row)
    v.half_tokens[row] = v.half_cross[row]
    wait_all(low)
    v.turned[...] = dot(v.turns[0], v.got[...].reshape(256, 256)).astype(B16).reshape(16, 16, 256)
    low = scatter_out("cols", v.turned, v.tokens, v.s_tc, v.r_tc, col)
    v.tokens[col] = v.turned[col]

    loads[0].wait()
    rows_finish()
    rows = dot(v.place[...], v.bin_got[...])
    v.rain[...] = rows
    v.bin_out[0] = jnp.broadcast_to(rows[:, 127:128], (48, 128)).astype(B16)
    v.bin_out[1] = jnp.broadcast_to(rows[:, 0:1], (48, 128)).astype(B16)
    for q in range(5):
        v.edge_out[0, q] = dot(v.pick_hi[...], v.field[8 * q:8 * q + 8, 112:128].reshape(128, 128)).astype(B16)
        v.edge_out[1, q] = dot(v.pick_lo[...], v.field[8 * q:8 * q + 8, 0:16].reshape(128, 128)).astype(B16)
    cols_start, cols_finish = halo_cols(v, col)
    cols_start()

    @pl.when(col == 0)
    def _():
        v.edge_in[0] = jnp.zeros((5, 16, 128), B16)
        v.bin_in[0] = jnp.zeros((48, 128), B16)

    @pl.when(col == 15)
    def _():
        v.edge_in[1] = jnp.zeros((5, 16, 128), B16)
        v.bin_in[1] = jnp.zeros((48, 128), B16)

    wait_all(low)
    wait_all(high)
    return cols_finish


def attend(v):
    v.tok[:, :256] = dot(v.turns[2], v.tokens[...].reshape(256, 256)).astype(B16)
    v.tok[:, 256:] = dot(v.turns[3], v.half_tokens[...].reshape(256, 256)).astype(B16)
    for n in range(3):
        v.qkv[:, n * 512:(n + 1) * 512] = dot(v.tok[...], v.w_qkv[:, n * 512:(n + 1) * 512]).astype(B16)
    for g in range(2):
        for t in range(4):
            rows, at = slice(g * 128, g * 128 + 128), t * 128
            query = v.qkv[rows, at:at + 128]
            keyed = v.qkv[rows, 512 + at:512 + at + 128]
            valued = v.qkv[rows, 1024 + at:1024 + at + 128]
            scores = dot_nt(heads_down(query), keyed) * SCALE
            peak = jnp.max(scores, axis=-1, keepdims=True)
            powers = jnp.exp(scores - peak)
            share = powers / jnp.sum(powers, axis=-1, keepdims=True)
            v.prob[g * 4 + t] = share
            v.mixed[rows, at:at + 128] = dot(side_by_side(share.astype(B16)), heads_down(valued)).astype(B16)
    attended = dot(v.mixed[...], v.w_out[...]).astype(B16)
    v.context[...] = (v.tok[...].astype(F32) + attended.astype(F32)).astype(B16)
    lifted = dot(v.context[...], v.w_up[...]).astype(B16)
    v.raised[...] = dot(v.turns[4], lifted).astype(B16).reshape(16, 16, 128)


def edge_targets(v):
    lane = lax.broadcasted_iota(jnp.int32, (48, 128), 1)
    line = lax.broadcasted_iota(jnp.int32, (48, 128), 0)
    low, high = v.bin_in[0].astype(F32), v.bin_in[1].astype(F32)
    picked = jnp.where((lane & 15) == 0, high, jnp.where((lane & 15) == 15, low, 0.0))
    for b in range(9):
        here = line == 4 * b + (lane >> 4)
        v.edge_bins[b:b + 1] = jnp.sum(jnp.where(here, picked, 0.0), axis=0, keepdims=True)


def fold_copy(v, row, target, source):
    return rcopy(v.dlift.at[target], v.fold_got.at[source], v.s_fr.at[target], v.r_fr.at[source], {"rows": target})


def send_fold(v, row, target):
    @pl.when(row != target)
    def _():
        fold_copy(v, row, target, row).start()


def convolve(v, row, col):
    head_t = dot(v.eye[...], v.w_head_t[...]).astype(B16)
    place = lax.broadcasted_iota(jnp.int32, (144, 1), 0)
    right = jnp.where(col < 15, 130, 128)
    left = jnp.where(col > 0, 142, 144)
    inside = (place < right) | (place >= left)
    level = (lax.broadcasted_iota(jnp.int32, (16, 1), 0) + 1).astype(F32) / 10.0
    quant = lax.broadcasted_iota(jnp.int32, (16, 1), 0) < QUANT
    v.loss_sum[...] = jnp.zeros((16, 128), F32)
    v.head_sum[...] = jnp.zeros((16, 128), F32)
    v.tap_sum[...] = jnp.zeros((144, 128), F32)
    v.active[pl.ds(38, 2)] = jnp.zeros((2, 144, 384), B16)
    v.hidden[pl.ds(38, 2)] = jnp.zeros((2, 144, 128), F32)

    def start(i):
        raised = dot(v.up[...], v.lifted[i])
        rims = {0: (2, 3), 9: (0, 1)}.get(i, range(4))
        for s in rims:
            y = 4 * i + s - 4
            x = v.field[4 * i + s].astype(F32) + raised
            square = x * x
            bend = jnp.tanh(ROOT_2_PI * x * (1.0 + 0.044715 * square))
            half = 0.5 * (1.0 + bend)
            act = x * half
            if i in (0, 9):
                act = jnp.where(inside & (row * 32 + y >= 0) & (row * 32 + y < 256), act, 0.0)
            else:
                act = jnp.concatenate([act[:128], jnp.where(inside[128:], act[128:], 0.0)], axis=0)
            v.hidden[4 * i + s] = x
            v.active[4 * i + s] = shifted(act).astype(B16)
            v.slope[4 * i + s] = half[:128] + (0.5 * ROOT_2_PI) * x[:128] * (1.0 - bend[:128] * bend[:128]) * (
                1.0 + (3 * 0.044715) * square[:128])

    def forward(i):
        windows = [jnp.concatenate([v.active[4 * i + 2 + a], v.active[4 * i + 4 + a]], axis=0) for a in range(4)]
        both = dot(jnp.concatenate(windows, axis=1), v.pair[...])
        for s in range(4):
            at, part = s // 2 * 144, s % 2 * 128
            v.outer[4 * i + s] = (v.hidden[4 * i + 3 + s] + both[at:at + 144, part:part + 128]).astype(B16)

    def turn(i):
        own = v.outer[pl.ds(4 * i, 4), :128].reshape(512, 128)
        edge = v.outer[pl.ds(4 * i, 4), 128:144].reshape(64, 128)
        pixels = jnp.concatenate([own, edge, jnp.zeros((64, 128), B16)], axis=0)
        predicted = dot_nt(head_t, pixels)
        lines = [v.rain[pl.ds(4 * i + s, 1), :] for s in range(4)] + [v.edge_bins[pl.ds(i, 1), :]]
        target = jnp.concatenate(lines, axis=1) * (1.0 / 16.0) - 1.0
        lane = lax.broadcasted_iota(jnp.int32, (1, 640), 1)
        spot = lane - 512
        inner = lane < 512
        y = 4 * i - 1 + jnp.where(inner, lane >> 7, spot >> 4)
        side = (((spot & 15) == 0) & (col < 15)) | (((spot & 15) == 15) & (col > 0))
        seen = (row * 32 + y >= 0) & (row * 32 + y < 256) & (y < 33) & (inner | (side & (spot < 64)))
        mine = inner & (y >= 0) & (y < 32)
        error = target - predicted
        weight = jnp.where(error < 0.0, 1.0 - level, level)
        down = jnp.where(seen & quant, -weight * jnp.clip(error, -1.0, 1.0) * (1.0 / 1024.0), 0.0)
        size = jnp.abs(error)
        loss = weight * jnp.where(size <= 1.0, 0.5 * error * error, size - 0.5)
        loss = jnp.where(mine & quant, loss, 0.0)
        v.loss_sum[...] += loss[:, :128] + loss[:, 128:256] + loss[:, 256:384] + loss[:, 384:512]
        v.head_sum[...] += dot(jnp.where(mine, down, 0.0).astype(B16)[:, :512], own)
        edge = down[:, 512:]
        at = lax.broadcasted_iota(jnp.int32, (1, 128), 1)
        sets = []
        for s in range(4):
            line = down[:, s * 128:(s + 1) * 128]
            before = jnp.where(at == 0, pltpu.roll(edge, 113 - 16 * s, 1), pltpu.roll(line, 1, 1))
            after = jnp.where(at == 127, pltpu.roll(edge, 127 - 16 * s, 1), pltpu.roll(line, 127, 1))
            sets.append(jnp.concatenate([before, line, after], axis=0))
            v.taps[4 * i + s] = sets[s].astype(B16)
            row_y = 4 * i + s - 1
            value = predicted[:, s * 128:(s + 1) * 128]
            if 0 <= row_y < 32:
                for q in range(QUANT):
                    v.quantiles[q, pl.ds(row_y, 1), :] = value[q:q + 1]
        v.taps_turned[pl.ds(4 * i, 4)] = jnp.concatenate(sets, axis=1).T.astype(B16).reshape(4, 128, 48)

    def back(i):
        windows = [v.taps_turned[pl.ds(4 * i + a, 4)].reshape(512, 48) for a in range(3)]
        both = dot(windows[1], v.back_mid[...])
        dactive = both[:, :128] + dot(windows[0], v.back_low[...]) + dot(windows[2], v.back_high[...])
        dhidden = (both[:, 128:] + v.slope[pl.ds(4 * i + 4, 4)].reshape(512, 128) * dactive).reshape(4, 128, 128)
        v.grad_fine[pl.ds(4 * i, 4)] = dhidden * 1024.0
        summed = dhidden[0] + dhidden[1] + dhidden[2] + dhidden[3]
        high = summed.astype(B16)
        low = (summed - high.astype(F32)).astype(B16)
        v.dlift[i] = (dot(v.fold[...], high) + dot(v.fold[...], low)).astype(B16)
        lines = [jnp.concatenate([v.taps[4 * i + a + s] for s in range(4)], axis=1) for a in range(3)]
        seen = v.active[pl.ds(4 * i + 4, 4), :128, 128:256].reshape(512, 128)
        v.tap_sum[...] += dot(jnp.concatenate(lines, axis=0), seen)

    for t in range(10):
        start(t)
    for t in range(9):
        forward(t)
    for t in range(9):
        turn(t)
    for t in range(8):
        back(t)
        if t % 4 == 3:
            for n in range(t - 3, t + 1):
                send_fold(v, row, n)


def back_weights(v):
    head_t = dot(v.eye[...], v.w_head_t[...]).astype(B16)
    for a, name in enumerate(("back_low", "back_mid", "back_high")):
        parts = [dot_nt(head_t, v.w_conv[2 - a, 2 - b]).astype(B16) for b in range(3)]
        getattr(v, name)[:, :128] = jnp.concatenate(parts, axis=0)
    for a in range(4):
        for b in range(2):
            block = v.w_conv[a - b].reshape(384, 128) if 0 <= a - b < 3 else jnp.zeros((384, 128), B16)
            v.pair[a * 384:(a + 1) * 384, b * 128:(b + 1) * 128] = block
    blank = jnp.zeros((16, 128), B16)
    v.back_mid[:, 128:] = jnp.concatenate([blank, head_t, blank], axis=0)


def local_units(v):
    v.a_g[448:466] = v.tap_sum[...].reshape(18, 8, 128).astype(B16)
    spot = lax.broadcasted_iota(jnp.int32, (16, 1), 0)
    total = jnp.sum(v.loss_sum[...], axis=0, keepdims=True)
    tail = jnp.where(spot < QUANT, v.head_sum[...], jnp.where(spot == QUANT, total, 0.0))
    v.a_g[466:468] = tail.reshape(2, 8, 128).astype(B16)
    v.a_g[468:HALF] = jnp.zeros((HALF - 468, 8, 128), B16)
    v.b_g[448:HALF] = jnp.zeros((HALF - 448, 8, 128), B16)


def attend_back(v, mix_grad, tiles):
    for s, t in [(s, t) for s in range(2) for t in tiles]:
        rows, at = slice(s * 128, s * 128 + 128), t * 128
        keyed = v.qkv[rows, 512 + at:512 + at + 128]
        valued = v.qkv[rows, 1024 + at:1024 + at + 128]
        mine = mix_grad[rows, at:at + 128]
        dprob = dot_nt(heads_down(mine), valued)
        share = v.prob[s * 4 + t]
        inner = jnp.sum(share * dprob, axis=-1, keepdims=True)
        dscore = (share * (dprob - inner) * SCALE).astype(B16)
        v.dquery[rows, at:at + 128] = dot(side_by_side(dscore), heads_down(keyed)).astype(B16)
        v.dkey[at:at + 128, rows] = dot(v.query_turned[s * 4 + t], dscore).astype(B16)
        v.dvalue[at:at + 128, rows] = dot(heads_across(mine), share.astype(B16)).astype(B16)


def projection_units(v, g, tiles):
    at = tiles[0] * 128
    put(g, 0, dot(v.tok_turned[...], v.dquery[:, at:at + 256]))
    put(g, 128, dot_nt(v.tok_turned[...], v.dkey[at:at + 256]))
    put(g, 256, dot_nt(v.tok_turned[...], v.dvalue[at:at + 256]))


def whole_kernel(names, *refs):
    v = SimpleNamespace(**dict(zip(names, refs)))
    row, col, batch = lax.axis_index("rows"), lax.axis_index("cols"), lax.axis_index("batch")
    core, deep = row % 2, (row // 2) * 2 + batch
    x, y = col // 4, col % 4
    me = SimpleNamespace(
        core=core, deep=deep, other={"rows": row + 1 - 2 * core},
    )
    x_axis = (x, lambda k: {"cols": ((x + k) % 4) * 4 + y})
    y_axis = (y, lambda k: {"cols": x * 4 + (y + k) % 4})

    def in_deep(k):
        p = (deep + k) % 8
        return {"rows": (p // 2) * 2 + core, "batch": p % 2}

    me.in_deep = in_deep

    peers = [{"rows": p} for p in peer_order("rows", row)]
    peers = peers[:2] + [{"rows": (row + 2 * k) % 8, "batch": 1 - batch} for k in (2, 1, 3, 0)] + peers[2:6] + [
        {"cols": p} for p in peer_order("cols", col)] + peers[6:]
    barrier = pltpu.get_barrier_semaphore()
    for peer in peers:
        pl.semaphore_signal(barrier, inc=1, device_id=peer, device_id_type=MESH)
    loads = [pltpu.make_async_copy(v.fine, v.field.at[pl.ds(4, 32), pl.ds(0, 128)], v.s_l.at[1]),
             pltpu.make_async_copy(v.w_qkv_in, v.w_qkv, v.s_l.at[2]),
             pltpu.make_async_copy(v.w_out_in, v.w_out, v.s_l.at[3]),
             pltpu.make_async_copy(v.w_conv_in, v.w_conv, v.s_l.at[4]),
             pltpu.make_async_copy(v.coarse.at[:, :, pl.ds(256, 256)], v.half, v.s_l.at[7]),
             pltpu.make_async_copy(v.turns_in, v.turns, v.s_l.at[8]),
             pltpu.make_async_copy(v.w_up_in, v.w_up, v.s_l.at[9]),
             pltpu.make_async_copy(v.back_in, v.back, v.s_l.at[10])]
    for n in (4, 5, 0, 1, 2, 6, 3, 7):
        loads[n].start()
    v.bins16[...] = v.bins[...].astype(F32).astype(B16)
    loads[4].wait()
    loads[5].wait()
    v.half_turned[...] = dot(v.turns[0], v.half[...].reshape(256, 256)).astype(B16).reshape(16, 16, 256)
    pl.semaphore_wait(barrier, len(peers))
    cols_finish = exchange_tokens(v, row, col, loads)
    loads[1].wait()
    loads[2].wait()
    loads[6].wait()
    loads[7].wait()
    attend(v)

    finish = spread_out("cols", 16, col, v.raised, v.slots, v.s_lc, v.r_lc, v.s_lx, v.r_lx)
    cols_finish()
    for q in range(5):
        edge = dot(v.spread_hi[...], v.edge_in[0, q]) + dot(v.spread_lo[...], v.edge_in[1, q])
        v.field[8 * q:8 * q + 8, 128:144] = edge.astype(B16).reshape(8, 16, 128)
    edge_targets(v)
    for s in range(2):
        for t in range(4):
            v.query_turned[s * 4 + t] = heads_across(v.qkv[s * 128:s * 128 + 128, t * 128:t * 128 + 128])
    finish()
    v.lift_turned[...] = dot(v.back[...], v.slots[...].reshape(288, 128)).astype(B16).reshape(8, 48, 128)
    finish = spread_out("rows", 8, row, v.lift_turned, v.lifted, v.s_lr, v.r_lr, v.s_ly, v.r_ly)
    v.tok_turned[...] = v.tok[...].astype(F32).T.astype(B16)
    loads[3].wait()
    back_weights(v)
    finish()

    convolve(v, row, col)

    results = [pltpu.make_async_copy(v.grad_fine, v.grad_fine_out, v.s_l.at[5]),
               pltpu.make_async_copy(v.quantiles, v.quantiles_out, v.s_l.at[6])]
    v.fold_got[row] = v.dlift[row]
    for c in results:
        c.start()
    local_units(v)
    for p in peer_order("rows", row):
        fold_copy(v, row, p, p).wait()
    v.fold_turned[...] = dot(v.turns[0], v.fold_got[...].reshape(256, 128)).astype(B16).reshape(16, 16, 128)
    sends = scatter_out("cols", v.fold_turned, v.folded, v.s_fc, v.r_fc, col)
    v.folded[col] = v.fold_turned[col]
    wait_all(sends)

    low = reducer(me, (x_axis, y_axis), HALF, v.a_g, v.a_out, v.low_half, v.a_got0, v.a_sum0, v.a_got1, v.a_sum1, v.a_got2, v.a_sum2,
                  v.a_got3, [getattr(v, "a_sem" + str(n)) for n in range(18)])
    high = reducer(me, (y_axis, x_axis), HALF, v.b_g, v.b_out, v.high_half, v.b_got0, v.b_sum0, v.b_got1, v.b_sum1, v.b_got2, v.b_sum2,
                   v.b_got3, [getattr(v, "b_sem" + str(n)) for n in range(18)])
    lift_wide = dot(v.turns[2], v.folded[...].reshape(256, 128))
    lift, lift_turned = lift_wide.astype(B16), lift_wide.T.astype(B16)
    dcontext = dot_nt(lift, v.w_up[...]).astype(B16)
    mix_grad = dot_nt(dcontext, v.w_out[...]).astype(B16)
    put(v.a_g, 384, dot(lift_turned, v.mixed[...]))
    put(v.b_g, 384, dot(lift_turned, v.context[...]))
    attend_back(v, mix_grad, (0, 1))
    projection_units(v, v.a_g, (0, 1))
    low[0]()
    attend_back(v, mix_grad, (2, 3))
    low[1]()
    projection_units(v, v.b_g, (2, 3))
    high[0]()
    high[1]()
    for n in range(2, 9):
        low[n]()
        high[n]()
    wait_all(results)


def unpack_kernel(low, high, fine, quantiles, w_up, w_head_t, eye,
                  grad_qkv, grad_out, grad_up, grad_conv, grad_head, loss, fine_out, quantiles_out,
                  held, wide, square, tall, flat, fine_in, bands_in, sems):
    through = [(fine.at[pl.ds(n * 8, 8)], fine_in.at[pl.ds(n * 8, 8)], fine_out.at[pl.ds(n * 8, 8)]) for n in range(4)]
    through.append((quantiles, bands_in, quantiles_out))
    passing = [pltpu.make_async_copy(src, held, sems.at[12 + n]) for n, (src, held, _) in enumerate(through)]
    reads = [pltpu.make_async_copy((low, high)[h].at[pl.ds(a, b)], held.at[h, pl.ds(a, b)], sems.at[2 * n + h])
             for n, (a, b) in enumerate(((0, 384), (384, HALF - 384))) for h in range(2)]
    for c in passing + reads[2:] + reads[:2]:
        c.start()
    writes = []

    def write(src, dst, n):
        c = pltpu.make_async_copy(src, dst, sems.at[n])
        c.start()
        writes.append(c)

    for m in range(5):
        passing[m].wait()
        write(through[m][1], through[m][2], 17 + m)
    reads[2].wait()
    reads[3].wait()
    for n in range(4):
        mixed = held[0, 384 + n * 16:384 + (n + 1) * 16].astype(F32).reshape(128, 128).T.astype(B16)
        square[n * 128:(n + 1) * 128] = dot_nt(mixed, w_up[...])
        tall[n * 128:(n + 1) * 128] = held[1, 384 + n * 16:384 + (n + 1) * 16].astype(F32).reshape(128, 128).T
    write(square, grad_out, 9)
    write(tall, grad_up, 10)
    head_t = dot(eye[...], w_head_t[...]).astype(B16)
    for a in range(3):
        for b in range(3):
            at = 448 + (2 - a) * 6 + (2 - b) * 2
            seen = held[0, at:at + 2].astype(F32).reshape(16, 128).T.astype(B16)
            flat[(a * 3 + b) * 128:(a * 3 + b + 1) * 128] = dot(seen, head_t)
    write(flat, grad_conv, 11)
    for h in range(2):
        reads[h].wait()
        for n in range(3):
            for m in range(2):
                at = n * 128 + m * 64
                wide[h * 3 + n, :, m * 128:(m + 1) * 128] = held[h, at:at + 64].astype(F32).reshape(512, 128)
            write(wide.at[h * 3 + n], grad_qkv.at[:, pl.ds(n * 512 + h * 256, 256)], 22 + h * 3 + n)
    tail = held[0, 466:468].astype(F32).reshape(16, 128)
    grad_head[...] = tail[:QUANT]
    loss[...] = jnp.sum(tail[QUANT:QUANT + 1], axis=1, keepdims=True) * (1.0 / (1048576.0 * QUANT))
    wait_all(writes)


def body(fine_input, coarse, rain_bins, w_qkv, w_out, w_up, w_conv, w_head):
    mid, group = mid_table(), group_table()
    turns = jnp.stack([mid, mid.T, group, cross_table(), group.T])
    eye = onehot(16, QUANT, [(q, q) for q in range(QUANT)])
    args = [coarse[0], fine_input[0], rain_bins[0], w_qkv, w_out, w_up, w_conv, w_head.T,
            turns, back_table(), pick_table(0), pick_table(14), spread_table(0), spread_table(14),
            bins_table(), up_table(), sum_table(), eye]
    spaces = scratch()
    names = INPUTS + tuple(name for name, _, _ in OUTPUTS) + tuple(name for name, _ in spaces)
    vmem, anywhere = pl.BlockSpec(memory_space=pltpu.VMEM), pl.BlockSpec(memory_space=pl.ANY)

    def kernel(*refs):
        whole_kernel(names, *refs)

    quantiles, grad_fine, low, high = pl.pallas_call(
        kernel,
        out_shape=[jax.ShapeDtypeStruct(shape, dtype) for _, shape, dtype in OUTPUTS],
        in_specs=[pl.BlockSpec(memory_space=pl.ANY) if name in IN_HBM else vmem for name in INPUTS],
        out_specs=[anywhere] * 4,
        scratch_shapes=[space for _, space in spaces],
        compiler_params=pltpu.CompilerParams(vmem_limit_bytes=LIMIT, collective_id=1, has_side_effects=True),
    )(*args)
    shapes = ((512, 1536), (512, 512), (512, 128), (1152, 128), (QUANT, 128), (1, 1), (32, 128, 128), (9, 32, 128))
    grad_qkv, grad_out, grad_up, grad_conv, grad_head, loss, fine, bands = pl.pallas_call(
        unpack_kernel,
        out_shape=[jax.ShapeDtypeStruct(shape, F32) for shape in shapes],
        in_specs=[anywhere] * 4 + [vmem] * 3,
        out_specs=[anywhere] * 4 + [vmem] * 2 + [anywhere] * 2,
        scratch_shapes=[pltpu.VMEM((2, HALF, 8, 128), B16), pltpu.VMEM((6, 512, 256), F32),
                        pltpu.VMEM((512, 512), F32), pltpu.VMEM((512, 128), F32), pltpu.VMEM((1152, 128), F32),
                        pltpu.VMEM((32, 128, 128), F32), pltpu.VMEM((9, 32, 128), F32), DMA((28,))],
        compiler_params=pltpu.CompilerParams(vmem_limit_bytes=LIMIT),
    )(low, high, grad_fine, quantiles, w_up, w_head.T, eye)
    return (bands[None], loss.reshape(()), grad_qkv, grad_out, grad_up, grad_conv.reshape(3, 3, 128, 128),
            grad_head.T, fine[None])


def solution(mesh):
    placed = (
        P("batch", "rows", "cols", None),
        P("batch", "rows", "cols", None),
        P("batch", "rows", "cols"),
        P(),
        P(),
        P(),
        P(),
        P(),
    )
    return jax.shard_map(
        body,
        mesh=mesh,
        in_specs=placed,
        out_specs=(
            P("batch", None, "rows", "cols"),
            P(),
            P(),
            P(),
            P(),
            P(),
            P(),
            P("batch", "rows", "cols", None),
        ),
        check_vma=False,
    )
```
